32 devices in a mesh: det: 4 (over y, x), tm: 8 (over z, core).
Axes of the slice: x: 2, y: 2, z: 4, core: 2. Of those that a mesh axis runs over, the one named last changes fastest.
Arguments:
- samples: float32 [4, 8, 32, 256], P('det', 'tm')
- pointing: int32 [4, 8, 32, 256], P('det', 'tm'), may hold values from 0 to 16383, as said below
- angles: float32 [4, 8, 32, 256], P('det', 'tm'), may hold values from -3.1415927 to 3.1415927
- counts: int32 [4, 8, 32], P('det', 'tm'), may hold values from 1 to 256, as said below
- sky_map: float32 [3, 64, 8192], P(None, ('det', 'tm'))
- prior_precision: float32 [3, 64, 4096], P(None, 'det', 'tm'), may hold values from 0.5 to 5
- omega_noise: float32 [6, 64, 4096], P(None, 'det', 'tm'), may hold values from -6 to 6
- omega_prior: float32 [6, 64, 4096], P(None, 'det', 'tm'), may hold values from -6 to 6
Outputs:
- gains: float32 [4, 8], P('det', 'tm')
- binned: float32 [3, 64, 8192], P(None, ('det', 'tm'))
- solution: float32 [6, 64, 4096], P(None, 'det', 'tm')
The draws below stay inside these ranges and needn't reach their ends.
Inputs may be any that keep to these rules, and one draw needn't show every extreme that they name: The first counts[g, t, k] slots of a row hold samples; some sky tile takes 256 samples from every device, and every device fills at least one tile. `pointing`: pixel within the destination tile, cycle-major with 8192 pixels a cycle.
All inputs are finite; a program needn't handle non-finite values.
Results may differ from the reference program's by a relative error of at most 0.0003.
Values sent between devices are 32-bit elements; how exact they have to be, the bound alone decides.
No kernel may reach another device: no remote copies, remote signals or barrier semaphores. Data moves between devices by JAX's collectives and lax.ppermute only.
A program may use at most 128 MiB of HBM per device.

```python
import math
import jax
import jax.numpy as jnp
from jax import lax

NPHI = 8192
M = 4096
RDEV = 2
CAP = 256
ITERS = 3
NDG = 4
NTC = 8
TILES = 32
CYCLES = 64
PIXT = 16384


def shared_draw(key):
    sky = jax.random.normal(jax.random.fold_in(key, 11), (3, CYCLES, NPHI), jnp.float32)
    shape = (NDG, NTC, TILES, CAP)
    pointing = jax.random.randint(jax.random.fold_in(key, 13), shape, 0, PIXT).astype(jnp.int32)
    pointing = pointing.at[0, 0, 0, 0].set(PIXT - 1)
    angles = jax.random.uniform(jax.random.fold_in(key, 14), shape, jnp.float32, -3.1415927, 3.1415927)
    true_gain = jax.random.uniform(jax.random.fold_in(key, 15), (NDG, NTC, 1, 1), jnp.float32, 0.6, 1.4)
    noise = jax.random.normal(jax.random.fold_in(key, 16), shape, jnp.float32)
    sky_flat = sky.reshape(3, TILES, PIXT)
    tile_index = lax.broadcasted_iota(jnp.int32, shape, 2)
    signal = sky_flat[0][tile_index, pointing] + sky_flat[1][tile_index, pointing] * jnp.cos(2.0 * angles) + sky_flat[2][tile_index, pointing] * jnp.sin(2.0 * angles)
    samples = true_gain * signal + noise
    return (sky, pointing, angles, samples)


def draw_sky_map(key, part):
    return shared_draw(key)[0]


def draw_pointing(key, part):
    return shared_draw(key)[1]


def draw_angles(key, part):
    return shared_draw(key)[2]


def draw_samples(key, part):
    return shared_draw(key)[3]


def draw_counts(key, part):
    base = jax.random.randint(jax.random.fold_in(key, 21), (NDG, NTC, TILES), 0, CAP * 3 // 4 + 1)
    factor = jax.random.randint(jax.random.fold_in(key, 22), (1, 1, TILES), 1, 5)
    filled = jnp.maximum(CAP // 4 + base * factor // 4, 1)
    column = lax.broadcasted_iota(jnp.int32, (NDG, NTC, TILES), 2)
    common = jax.random.randint(jax.random.fold_in(key, 23), (), 0, TILES)
    single = jax.random.randint(jax.random.fold_in(key, 24), (NDG, NTC, 1), 0, TILES)
    filled = jnp.where(column == common, CAP, filled)
    filled = jnp.where(column == single, CAP, filled)
    return filled.astype(jnp.int32)


def shard_levels(stream_key, extent, split, least, top_value):
    def one(dim, parts):
        steps = jax.random.uniform(jax.random.fold_in(jax.random.fold_in(stream_key, 6), dim), (parts,), jnp.float32, least / len(split), top_value / len(split))
        return jnp.repeat(jnp.exp(steps), extent[dim] // parts).reshape((-1,) + (1,) * (len(extent) - dim - 1))

    factor_of = one(*split[0])
    for cut in split[1:]:
        factor_of = factor_of * one(*cut)
    return factor_of


def centred(key, dims, width, bound, shards=(), held_as=jnp.bfloat16):
    gain = shard_levels(key, dims, shards, -0.22, 0.18) if shards else 1.0
    result = jax.random.normal(key, dims, jnp.float32) * width * gain
    return jnp.minimum(jnp.maximum(result, -bound), bound).astype(held_as)


def setup_inputs(seed: int = 0) -> dict:
    key_list = jax.random.split(jax.random.key(seed), 9)
    return {
        "samples": draw_samples(jax.random.fold_in(key_list[8], 71), 0),
        "pointing": draw_pointing(jax.random.fold_in(key_list[8], 71), 0),
        "angles": draw_angles(jax.random.fold_in(key_list[8], 71), 0),
        "counts": draw_counts(jax.random.fold_in(key_list[8], 71), 0),
        "sky_map": draw_sky_map(jax.random.fold_in(key_list[8], 71), 0),
        "prior_precision": jnp.clip(jnp.exp(math.log(5.0) - 2.3025851 * jax.random.uniform(key_list[5], (3, CYCLES, M), jnp.float32) ** shard_levels(key_list[5], (3, CYCLES, M), ((1, 4), (2, 8)), -0.2, 0.2)), 0.5, 5.0),
        "omega_noise": centred(key_list[6], (6, CYCLES, M), 1.0, 6.0, ((1, 4), (2, 8)), jnp.float32),
        "omega_prior": centred(key_list[7], (6, CYCLES, M), 1.0, 6.0, ((1, 4), (2, 8)), jnp.float32),
    }


def template(sky_flat, pointing, angles):
    tile_index = lax.broadcasted_iota(jnp.int32, pointing.shape, pointing.ndim - 2)
    cosine = jnp.cos(2.0 * angles)
    sine = jnp.sin(2.0 * angles)
    signal = sky_flat[0][tile_index, pointing] + sky_flat[1][tile_index, pointing] * cosine + sky_flat[2][tile_index, pointing] * sine
    return (signal, cosine, sine)

def validity(samples, counts):
    slots = lax.broadcasted_iota(jnp.int32, samples.shape, samples.ndim - 1)
    return (slots < counts[..., None]).astype(jnp.float32)

def operate(field, root, diagonal):
    scaled = root * field
    padded = jnp.pad(scaled, ((0, 0), (1, 1), (0, 0)))
    beside = padded[:, 2:] + padded[:, :-2]
    return diagonal * field - 0.45 * root * beside

def reference(samples, pointing, angles, counts, sky_map, prior_precision, omega_noise, omega_prior):
    sky_flat = sky_map.reshape(3, TILES, PIXT)

    def group_sums(items):
        samples_g, pointing_g, angles_g, counts_g = items
        signal, cosine, sine = template(sky_flat, pointing_g, angles_g)
        valid = validity(samples_g, counts_g)
        return (lax.optimization_barrier(jnp.sum(valid * signal * samples_g, axis=(1, 2))), lax.optimization_barrier(jnp.sum(valid * signal * signal, axis=(1, 2))))
    sums_a, sums_b = lax.map(group_sums, (samples, pointing, angles, counts))
    gains = sums_a / (sums_b + 1e-06)

    def accumulate(carry, items):
        binned, hits = carry
        samples_g, pointing_g, angles_g, counts_g, gains_g = items
        signal, cosine, sine = template(sky_flat, pointing_g, angles_g)
        valid = validity(samples_g, counts_g)
        residual = valid * (samples_g - gains_g[:, None, None] * signal)
        tile_index = lax.broadcasted_iota(jnp.int32, pointing_g.shape, 1)
        where = (tile_index * PIXT + pointing_g).reshape(-1)
        weights = jnp.stack([residual, residual * cosine, residual * sine]).reshape(3, -1)
        binned = binned.at[:, where].add(weights)
        cycle = (tile_index * RDEV + pointing_g // NPHI).reshape(-1)
        hits = hits.at[cycle].add(valid.reshape(-1))
        return ((binned, hits), None)
    start = (jnp.zeros((3, TILES * PIXT), jnp.float32), jnp.zeros((CYCLES,), jnp.float32))
    (binned, hits), _ = lax.scan(accumulate, start, (samples, pointing, angles, counts, gains))
    binned = binned.reshape(3, CYCLES, NPHI)
    spectrum = jnp.fft.rfft(binned, axis=-1)[..., :M] / math.sqrt(NPHI)
    planes = jnp.stack([jnp.real(spectrum), jnp.imag(spectrum)], axis=1).reshape(6, CYCLES, M).astype(jnp.float32)
    weight = (hits / NPHI)[None, :, None]
    precision = jnp.repeat(prior_precision, 2, axis=0)
    root = jnp.sqrt(precision)
    diagonal = precision + weight
    rhs = planes + jnp.sqrt(weight) * omega_noise + root * omega_prior
    solution = jnp.zeros_like(rhs)
    resid = rhs
    direction = rhs
    norm_now = jnp.sum(resid * resid)
    for iteration in range(ITERS):
        image = operate(direction, root, diagonal)
        alpha = norm_now / jnp.sum(direction * image)
        solution = solution + alpha * direction
        resid = resid - alpha * image
        norm_next = jnp.sum(resid * resid)
        direction = resid + norm_next / norm_now * direction
        norm_now = norm_next
    return (gains, binned, solution)
```

```python
import math

import jax
import jax.numpy as jnp
import ml_dtypes
import numpy as np
from jax import lax
from jax.experimental import pallas as pl
from jax.experimental.pallas import tpu as pltpu
from jax.sharding import PartitionSpec as P

SHIFT = 5.0
SPREAD = 5.0
COUPLING = 0.45

LANES = 128
GROUP = 2
PLANES = 6
CHUNK = 16


def split_np(table):
    high = table.astype(ml_dtypes.bfloat16)
    low = (table - high.astype(np.float64)).astype(ml_dtypes.bfloat16)
    return high, low


def split(values):
    high = values.astype(jnp.bfloat16)
    low = (values - high.astype(jnp.float32)).astype(jnp.bfloat16)
    return high, low


def dft_tables(nphi, n_tm):
    first, second = LANES, nphi // LANES
    half = second // 2
    column = np.arange(first)
    digit = 2 * (column % (first // 2)) + column // (first // 2)
    k = np.arange(first)
    angle = 2.0 * math.pi / first * (np.outer(digit, k) % first)
    stage_a = np.concatenate([np.cos(angle), np.sin(angle)], axis=1)
    high, low = split_np(stage_a)
    stage_a = np.concatenate([high, high, low], axis=0)
    b = np.arange(second)
    angle = 2.0 * math.pi / nphi * (np.outer(b, k) % nphi)
    twiddle = np.stack([np.cos(angle), np.sin(angle)]).astype(np.float32)
    per_band = half // n_tm
    row = np.arange(half)
    q = (row % n_tm) * per_band + row // n_tm
    angle = 2.0 * math.pi / second * (np.outer(q, b) % second)
    cos_b, sin_b = np.cos(angle), np.sin(angle)
    stage_b = np.block([[cos_b, -sin_b], [-sin_b, -cos_b]]) / math.sqrt(nphi)
    high, low = split_np(stage_b)
    stage_b = np.concatenate([high, high, low], axis=1)
    return stage_a, twiddle, stage_b


def pack_kernel(samples_ref, angles_ref, pointing_ref, counts_ref, out_ref):
    tiles = samples_ref.shape[0]
    halves = samples_ref.shape[1] // LANES
    for h in range(halves):
        cut = slice(h * LANES, (h + 1) * LANES)
        out_ref[pl.ds(h, tiles, stride=8), :] = samples_ref[:, cut]
        out_ref[pl.ds(halves + h, tiles, stride=8), :] = angles_ref[:, cut]
        out_ref[pl.ds(2 * halves + h, tiles, stride=8), :] = pointing_ref[:, cut].astype(jnp.float32)
    count = counts_ref[...].astype(jnp.float32)
    row = lax.broadcasted_iota(jnp.int32, (tiles, tiles), 0)
    col = lax.broadcasted_iota(jnp.int32, (tiles, tiles), 1)
    column = jnp.sum(jnp.where(row == col, count, 0.0), axis=1, keepdims=True)
    column = jnp.broadcast_to(column, (tiles, LANES))
    out_ref[pl.ds(3 * halves, tiles, stride=8), :] = column
    out_ref[pl.ds(3 * halves + 1, tiles, stride=8), :] = column


def lookup_kernel(
    got_ref, sky_ref, data_ref, signal_ref, cosine_ref, sine_ref, pixel_ref, weight_ref, sums_ref,
    table, high, low,
):
    tiles = got_ref.shape[0] // 8
    cap = data_ref.shape[1]
    halves = cap // LANES
    rows = sky_ref.shape[1]
    cycles = 2
    nphi = rows * LANES // cycles

    for c in range(3):
        part = split(sky_ref[c].T)
        table[c * LANES : (c + 1) * LANES, :rows] = part[0]
        table[c * LANES : (c + 1) * LANES, rows:] = part[1]

    def received(field):
        parts = [got_ref[pl.ds(field * halves + h, tiles, stride=8), :] for h in range(halves)]
        return jnp.concatenate(parts, axis=1)

    data = received(0)
    angle = received(1)
    pixel = received(2).astype(jnp.int32)
    count = got_ref[pl.ds(3 * halves, tiles, stride=8), :]
    count = jnp.concatenate([count] * halves, axis=1)
    slot = lax.broadcasted_iota(jnp.int32, (tiles, cap), 1).astype(jnp.float32)
    valid = jnp.where(slot < count, 1.0, 0.0)
    cosine = jnp.cos(2.0 * angle)
    sine = jnp.sin(2.0 * angle)
    cosine_ref[...] = cosine
    sine_ref[...] = sine
    pixel_ref[...] = pixel
    cycle = pixel // nphi
    high[...] = (pixel % nphi) // LANES * cycles + cycle
    low[...] = pixel % LANES

    iota = lax.broadcasted_iota(jnp.int32, (LANES, cap), 0)

    def step(index, carry):
        for g in range(GROUP):
            s = index * GROUP + g
            onehot = jnp.where(iota == high[pl.ds(s, 1), :], 1.0, 0.0).astype(jnp.bfloat16)
            onehot = jnp.concatenate([onehot, onehot], axis=0)
            found = jnp.dot(table[...], onehot, preferred_element_type=jnp.float32)
            mask = iota == low[pl.ds(s, 1), :]
            looked = [
                jnp.sum(
                    jnp.where(mask, found[c * LANES : (c + 1) * LANES], 0.0), axis=0, keepdims=True
                )
                for c in range(3)
            ]
            signal_ref[pl.ds(s, 1), :] = (
                looked[0]
                + looked[1] * cosine_ref[pl.ds(s, 1), :]
                + looked[2] * sine_ref[pl.ds(s, 1), :]
            )
        return carry

    lax.fori_loop(0, tiles // GROUP, step, 0)

    signal = signal_ref[...]
    masked = valid * signal
    signal_ref[...] = masked
    data_ref[...] = valid * data
    cross = jnp.sum(masked * data, axis=1, keepdims=True)
    square = jnp.sum(masked * signal, axis=1, keepdims=True)
    width = sums_ref.shape[1]
    row = lax.broadcasted_iota(jnp.int32, (tiles, width), 0)
    lane = lax.broadcasted_iota(jnp.int32, (tiles, width), 1)
    both = jnp.where(lane == row, cross, 0.0) + jnp.where(lane == row + width // 2, square, 0.0)
    both = jnp.sum(both, axis=0, keepdims=True)
    sums_ref[...] = jnp.broadcast_to(both, sums_ref.shape)
    for cy in range(cycles):
        hits = jnp.sum(jnp.where(cycle == cy, valid, 0.0), keepdims=True)
        weight_ref[cy : cy + 1, :] = jnp.broadcast_to(hits / nphi, (1, LANES))


def send_shape(send_ref, second):
    per_device = send_ref.shape[0] // CHUNK
    n_tm = lax.axis_size("tm")
    return n_tm, per_device // n_tm


def bin_kernel(
    sums_ref, data_ref, signal_ref, cosine_ref, sine_ref, pixel_ref, weight_ref,
    stage_a_ref, twiddle_ref, stage_b_ref,
    gain_ref, binned_ref, send_ref,
    acc, weights, high, low, wide, onehot,
):
    tiles, cap = data_ref.shape
    cycles = 2
    second = twiddle_ref.shape[1]
    first = LANES
    nphi = first * second
    n_tm, per_band = send_shape(send_ref, second)
    stride = per_band * CHUNK

    total = jnp.sum(sums_ref[...], axis=0, keepdims=True)
    width = total.shape[1]
    row = lax.broadcasted_iota(jnp.int32, (tiles, width), 0)
    lane = lax.broadcasted_iota(jnp.int32, (tiles, width), 1)
    cross = jnp.sum(jnp.where(lane == row, total, 0.0), axis=1, keepdims=True)
    square = jnp.sum(jnp.where(lane == row + width // 2, total, 0.0), axis=1, keepdims=True)
    gains = cross / (square + 1e-06)
    position = lax.axis_index("det") * n_tm + lax.axis_index("tm")
    place = lax.broadcasted_iota(jnp.int32, (tiles, 1), 0)
    gain_ref[...] = jnp.sum(jnp.where(place == position, gains, 0.0), axis=0, keepdims=True)

    residual = data_ref[...] - gains * signal_ref[...]
    for c, values in enumerate((residual, residual * cosine_ref[...], residual * sine_ref[...])):
        top = values.astype(jnp.bfloat16).astype(jnp.float32)
        weights[2 * c] = top
        weights[2 * c + 1] = values - top
    pixel = pixel_ref[...]
    low[...] = pixel % second
    high[...] = pixel // nphi * first + (pixel // second) % 2 * (first // 2) + (pixel % nphi) // first

    acc[...] = jnp.zeros_like(acc)
    iota_low = lax.broadcasted_iota(jnp.int32, (second, cap), 0)
    iota_high = lax.broadcasted_iota(jnp.int32, (cycles * first, cap), 0)

    def step(index, carry):
        for g in range(GROUP):
            s = index * GROUP + g
            cut = slice(g * cap, (g + 1) * cap)
            mask = iota_low == low[pl.ds(s, 1), :]
            for i in range(6):
                wide[i * second : (i + 1) * second, cut] = jnp.where(
                    mask, weights[i, pl.ds(s, 1), :], 0.0
                ).astype(jnp.bfloat16)
            onehot[:, cut] = jnp.where(iota_high == high[pl.ds(s, 1), :], 1.0, 0.0).astype(
                jnp.bfloat16
            )
        acc[...] += lax.dot_general(
            wide[...], onehot[...], (((1,), (1,)), ((), ())), preferred_element_type=jnp.float32
        )
        return carry

    lax.fori_loop(0, tiles // GROUP, step, 0)

    blocks = []
    for c in range(3):
        at = 2 * c * second
        map_c = acc[at : at + second, :] + acc[at + second : at + 2 * second, :]
        for cy in range(cycles):
            block = map_c[:, cy * first : (cy + 1) * first]
            blocks.append(block)
            flipped = block.T
            binned_ref[c, pl.ds(cy, first // 2, stride=cycles), :] = jnp.concatenate(
                [flipped[: first // 2], flipped[first // 2 :]], axis=1
            )
    field = jnp.concatenate(blocks, axis=0)
    field_high, field_low = split(field)
    modes = jnp.dot(
        jnp.concatenate([field_high, field_low, field_high], axis=1),
        stage_a_ref[...],
        preferred_element_type=jnp.float32,
    )
    turned = []
    for i in range(3 * cycles):
        real = modes[i * second : (i + 1) * second, :first]
        imag = modes[i * second : (i + 1) * second, first:]
        cos_t = twiddle_ref[0]
        sin_t = twiddle_ref[1]
        turned.append(
            jnp.concatenate([real * cos_t - imag * sin_t, real * sin_t + imag * cos_t], axis=0)
        )
    turned = jnp.concatenate(turned, axis=1)
    turned_high, turned_low = split(turned)
    spectrum = jnp.dot(
        stage_b_ref[...],
        jnp.concatenate([turned_high, turned_low, turned_high], axis=0),
        preferred_element_type=jnp.float32,
    )
    half = second // 2
    for c in range(3):
        for cy in range(cycles):
            at = (c * cycles + cy) * first
            for part in range(2):
                for ql in range(per_band):
                    start = part * half + ql * n_tm
                    line = ql * CHUNK + (2 * c + part) * cycles + cy
                    send_ref[pl.ds(line, n_tm, stride=stride), :] = spectrum[
                        start : start + n_tm, at : at + first
                    ]
    for cy in range(cycles):
        weight = jnp.broadcast_to(weight_ref[cy : cy + 1, :], (n_tm, LANES))
        for ql in range(per_band):
            line = ql * CHUNK + PLANES * cycles + cy
            send_ref[pl.ds(line, n_tm, stride=stride), :] = weight
            send_ref[pl.ds(line + cycles, n_tm, stride=stride), :] = jnp.zeros_like(weight)


def rhs_kernel(
    got_ref, prior_ref, noise_ref, draw_ref, rhs_ref, weight_ref, left_ref, right_ref, lines
):
    count = prior_ref.shape[1]
    per_band = prior_ref.shape[2] // LANES
    stride = per_band * CHUNK
    n_tm = got_ref.shape[0] // stride
    cycles = count // n_tm
    for ql in range(per_band):
        cut = slice(ql * LANES, (ql + 1) * LANES)
        for p in range(PLANES + 1):
            for cy in range(cycles):
                lines[p, pl.ds(cy, n_tm, stride=cycles), :] = got_ref[
                    pl.ds(ql * CHUNK + p * cycles + cy, n_tm, stride=stride), :
                ]
        weight = lines[PLANES]
        weight_ref[:, cut] = weight
        root_weight = jnp.sqrt(weight)
        for c in range(3):
            root = jnp.sqrt(prior_ref[c, :, cut])
            for p in (2 * c, 2 * c + 1):
                rhs_ref[p, :, cut] = (
                    lines[p] + root_weight * noise_ref[p, :, cut] + root * draw_ref[p, :, cut]
                )
    for p in range(PLANES):
        left_ref[p] = rhs_ref[p, :8, :]
        right_ref[p] = rhs_ref[p, count - 8 :, :]
    left_ref[PLANES] = weight_ref[:8, :]
    right_ref[PLANES] = weight_ref[count - 8 :, :]


def krylov_kernel(
    rhs_ref, weight_ref, prior_ref, after_ref, prior_after_ref, one_ref, two_ref, sums_ref
):
    count = rhs_ref.shape[1]
    rows = count + 8
    band = rhs_ref.shape[2]
    row = lax.broadcasted_iota(jnp.int32, (rows, band), 0)
    first = lax.axis_index("det") == 0
    counted = (row < count + 3) & ((row >= 3) | first)
    share = jnp.where(counted, 1.0, 0.0)
    top = row == 0
    weight = jnp.concatenate([weight_ref[...], after_ref[PLANES]], axis=0)
    sums = [jnp.zeros((rows, band), jnp.float32) for _ in range(6)]
    for c in range(3):
        precision = jnp.concatenate([prior_ref[c], prior_after_ref[c]], axis=0)
        root = jnp.sqrt(precision)
        diagonal = (precision + weight - SHIFT) * (1.0 / SPREAD)
        beside = root * (COUPLING / SPREAD)

        def apply(field):
            scaled = root * field
            before = jnp.where(top, 0.0, pltpu.roll(scaled, 1, 0))
            after = pltpu.roll(scaled, rows - 1, 0)
            return diagonal * field - beside * (before + after)

        for part in range(2):
            p = 2 * c + part
            zero = jnp.concatenate([rhs_ref[p], after_ref[p]], axis=0)
            one = apply(zero)
            two = apply(one)
            three = apply(two)
            one_ref[p] = one[:count]
            two_ref[p] = two[:count]
            held_zero = share * zero
            held_one = share * one
            held_two = share * two
            for i, term in enumerate(
                (
                    held_zero * zero,
                    held_zero * one,
                    held_one * one,
                    held_one * two,
                    held_two * two,
                    held_two * three,
                )
            ):
                sums[i] = sums[i] + jnp.where(counted, term, 0.0)
    lane = lax.broadcasted_iota(jnp.int32, (1, LANES), 1)
    line = jnp.zeros((1, LANES), jnp.float32)
    for i in range(6):
        line = jnp.where(lane == i, jnp.sum(sums[i], keepdims=True), line)
    sums_ref[...] = jnp.broadcast_to(line, sums_ref.shape)


def inner(left, right, moments):
    result = 0.0
    for i, a in enumerate(left):
        for j, b in enumerate(right):
            result = result + a * b * moments[i + j]
    return result


def operated(coefficients):
    result = [SHIFT * a for a in coefficients] + [0.0]
    for i, a in enumerate(coefficients):
        result[i + 1] = result[i + 1] + SPREAD * a
    return result


def padded(values, length):
    return list(values) + [0.0] * (length - len(values))


def conjugate_gradient(moments):
    resid = [1.0]
    direction = [1.0]
    solution = [0.0]
    norm_now = moments[0]
    for iteration in range(3):
        image = operated(direction)
        alpha = norm_now / inner(direction, image, moments)
        size = len(direction)
        solution = [a + alpha * b for a, b in zip(padded(solution, size), direction)]
        if iteration == 2:
            break
        resid = [a - alpha * b for a, b in zip(padded(resid, size + 1), image)]
        norm_next = inner(resid, resid, moments)
        beta = norm_next / norm_now
        direction = [a + beta * b for a, b in zip(resid, padded(direction, size + 1))]
        norm_now = norm_next
    return solution


def final_kernel(
    sums_ref, rhs_ref, one_ref, two_ref, prior_ref, weight_ref, before_ref, prior_before_ref, out_ref
):
    total = jnp.sum(sums_ref[...], axis=0, keepdims=True)
    moments = [total[:, i : i + 1] for i in range(6)]
    zero_by, one_by, two_by = conjugate_gradient(moments)
    count = rhs_ref.shape[1]
    weight_last = before_ref[PLANES, 7:8, :]
    weight_first = weight_ref[0:1, :]
    beside = COUPLING / SPREAD
    for c in range(3):
        precision_last = prior_before_ref[c, 7:8, :]
        root_far = jnp.sqrt(prior_before_ref[c, 6:7, :])
        root_last = jnp.sqrt(precision_last)
        precision_first = prior_ref[c, 0:1, :]
        root_first = jnp.sqrt(precision_first)
        root_second = jnp.sqrt(prior_ref[c, 1:2, :])
        diagonal_last = (precision_last + weight_last - SHIFT) * (1.0 / SPREAD)
        diagonal_first = (precision_first + weight_first - SHIFT) * (1.0 / SPREAD)
        for part in range(2):
            p = 2 * c + part
            out_ref[p] = zero_by * rhs_ref[p] + one_by * one_ref[p] + two_by * two_ref[p]
            far = before_ref[p, 6:7, :]
            last = before_ref[p, 7:8, :]
            one_last = diagonal_last * last - beside * root_last * (
                root_far * far + root_first * rhs_ref[p, 0:1, :]
            )
            one_first = -beside * root_first * root_last * last
            two_first = diagonal_first * one_first - beside * root_first * root_last * one_last
            two_second = -beside * root_second * root_first * one_first
            out_ref[p, 0:1, :] += one_by * one_first + two_by * two_first
            out_ref[p, 1:2, :] += two_by * two_second


def call(kernel, name, outs, scratch=()):
    return pl.pallas_call(
        kernel,
        out_shape=tuple(jax.ShapeDtypeStruct(shape, dtype) for shape, dtype in outs),
        scratch_shapes=list(scratch),
        compiler_params=pltpu.CompilerParams(vmem_limit_bytes=24 * 2**20),
        name=name,
    )


def exchange(values, axes):
    return lax.all_to_all(values, axes, split_axis=0, concat_axis=0, tiled=True)


def per_device(
    samples, pointing, angles, counts, sky_map, prior_precision, omega_noise, omega_prior
):
    f32, i32, bf16 = jnp.float32, jnp.int32, jnp.bfloat16
    tiles, cap = samples.shape[2:]
    n_det, n_tm = lax.axis_size("det"), lax.axis_size("tm")
    devices = n_det * n_tm
    cycles, nphi = sky_map.shape[1:]
    count, band = prior_precision.shape[1:]
    second = nphi // LANES
    everywhere = ("det", "tm")
    forth = [(i, i + 1) for i in range(n_det - 1)]
    back = [(i + 1, i) for i in range(n_det - 1)]

    packed = call(pack_kernel, "pack", [((tiles * 8, LANES), f32)])(
        samples.reshape(tiles, cap),
        angles.reshape(tiles, cap),
        pointing.reshape(tiles, cap),
        counts.reshape(1, tiles),
    )[0]
    got = exchange(packed.reshape(tiles, 8, LANES), everywhere).reshape(tiles * 8, LANES)
    prior_after = lax.ppermute(prior_precision[:, :8, :], "det", back)
    prior_before = lax.ppermute(prior_precision[:, count - 8 :, :], "det", forth)

    sky = sky_map.reshape(3, cycles, second, LANES).transpose(0, 2, 1, 3)
    sky = sky.reshape(3, second * cycles, LANES)
    width = LANES * -(-2 * tiles // LANES)
    data, signal, cosine, sine, pixel, weight, sums = call(
        lookup_kernel,
        "lookup",
        [((tiles, cap), f32)] * 4 + [((tiles, cap), i32), ((cycles, LANES), f32), ((devices, width), f32)],
        [
            pltpu.VMEM((3 * LANES, 2 * second * cycles), bf16),
            pltpu.VMEM((tiles, cap), i32),
            pltpu.VMEM((tiles, cap), i32),
        ],
    )(got, sky)
    sums = exchange(sums, everywhere)

    stage_a, twiddle, stage_b = dft_tables(nphi, n_tm)
    gain, binned, send = call(
        bin_kernel,
        "bin",
        [((1, 1), f32), ((3, second * cycles, LANES), f32), ((band // LANES * n_tm * CHUNK, LANES), f32)],
        [
            pltpu.VMEM((6 * second, cycles * LANES), f32),
            pltpu.VMEM((6, tiles, cap), f32),
            pltpu.VMEM((tiles, cap), i32),
            pltpu.VMEM((tiles, cap), i32),
            pltpu.VMEM((6 * second, GROUP * cap), bf16),
            pltpu.VMEM((cycles * LANES, GROUP * cap), bf16),
        ],
    )(sums, data, signal, cosine, sine, pixel, weight, stage_a, twiddle, stage_b)
    binned = binned.reshape(3, second, cycles, LANES).transpose(0, 2, 1, 3).reshape(3, cycles, nphi)

    got = exchange(send.reshape(n_tm, -1, LANES), "tm").reshape(-1, LANES)
    rhs, weight, left, right = call(
        rhs_kernel,
        "rhs",
        [((PLANES, count, band), f32), ((count, band), f32)] + [((PLANES + 1, 8, band), f32)] * 2,
        [pltpu.VMEM((PLANES + 1, count, LANES), f32)],
    )(got, prior_precision, omega_noise, omega_prior)
    after = lax.ppermute(left, "det", back)
    before = lax.ppermute(right, "det", forth)
    one, two, sums = call(
        krylov_kernel,
        "krylov",
        [((PLANES, count, band), f32)] * 2 + [((devices, LANES), f32)],
    )(rhs, weight, prior_precision, after, prior_after)
    sums = exchange(sums, everywhere)
    solution = call(final_kernel, "final", [((PLANES, count, band), f32)])(
        sums, rhs, one, two, prior_precision, weight, before, prior_before
    )[0]
    return (gain, binned, solution)


def solution(mesh):
    return jax.shard_map(
        per_device,
        mesh=mesh,
        in_specs=(
            P("det", "tm", None, None),
            P("det", "tm", None, None),
            P("det", "tm", None, None),
            P("det", "tm", None),
            P(None, ("det", "tm"), None),
            P(None, "det", "tm"),
            P(None, "det", "tm"),
            P(None, "det", "tm"),
        ),
        out_specs=(P("det", "tm"), P(None, ("det", "tm"), None), P(None, "det", "tm")),
        check_vma=False,
    )
```

```python
import math

import jax
import jax.numpy as jnp
import ml_dtypes
import numpy as np
from jax import lax
from jax.experimental import pallas as pl
from jax.experimental.pallas import tpu as pltpu
from jax.sharding import PartitionSpec as P

SHIFT = 5.0
SPREAD = 5.0
COUPLING = 0.45

LANES = 128
GROUP = 16
PLANES = 6
HALO = 3
BLOCK = 8


def split_np(table):
    high = table.astype(ml_dtypes.bfloat16)
    low = (table - high.astype(np.float64)).astype(ml_dtypes.bfloat16)
    return high, low


def split(values):
    high = values.astype(jnp.bfloat16)
    low = (values - high.astype(jnp.float32)).astype(jnp.bfloat16)
    return high, low


def dft_tables(nphi, n_tm):
    first, second = LANES, nphi // LANES
    half = second // 2
    column = np.arange(first)
    digit = 2 * (column % (first // 2)) + column // (first // 2)
    k = np.arange(first)
    angle = 2.0 * math.pi / first * (np.outer(digit, k) % first)
    stage_a = np.concatenate([np.cos(angle), np.sin(angle)], axis=1)
    high, low = split_np(stage_a)
    stage_a = np.concatenate([high, high, low], axis=0)
    b = np.arange(second)
    angle = 2.0 * math.pi / nphi * (np.outer(b, k) % nphi)
    twiddle = np.stack([np.cos(angle), np.sin(angle)]).astype(np.float32)
    per_band = half // n_tm
    row = np.arange(half)
    q = (row % n_tm) * per_band + row // n_tm
    angle = 2.0 * math.pi / second * (np.outer(q, b) % second)
    cos_b, sin_b = np.cos(angle), np.sin(angle)
    stage_b = np.block([[cos_b, -sin_b], [-sin_b, -cos_b]]) / math.sqrt(nphi)
    high, low = split_np(stage_b)
    stage_b = np.concatenate([high, high, low], axis=1)
    return stage_a, twiddle, stage_b


def pack_kernel(
    samples_hbm, angles_hbm, pointing_hbm, counts_hbm, out_ref,
    samples_ref, angles_ref, pointing_ref, counts_ref, sems,
):
    copies = [
        pltpu.make_async_copy(source, target, sems.at[i])
        for i, (source, target) in enumerate(
            (
                (samples_hbm, samples_ref),
                (angles_hbm, angles_ref),
                (pointing_hbm, pointing_ref),
                (counts_hbm, counts_ref),
            )
        )
    ]
    for copy in copies:
        copy.start()
    for copy in copies:
        copy.wait()
    tiles = samples_ref.shape[0]
    halves = samples_ref.shape[1] // LANES
    for h in range(halves):
        cut = slice(h * LANES, (h + 1) * LANES)
        out_ref[pl.ds(h, tiles, stride=8), :] = samples_ref[:, cut]
        out_ref[pl.ds(halves + h, tiles, stride=8), :] = angles_ref[:, cut]
        out_ref[pl.ds(2 * halves + h, tiles, stride=8), :] = pointing_ref[:, cut].astype(jnp.float32)
    count = counts_ref[...].astype(jnp.float32)
    row = lax.broadcasted_iota(jnp.int32, (tiles, tiles), 0)
    col = lax.broadcasted_iota(jnp.int32, (tiles, tiles), 1)
    column = jnp.sum(jnp.where(row == col, count, 0.0), axis=1, keepdims=True)
    column = jnp.broadcast_to(column, (tiles, LANES))
    out_ref[pl.ds(3 * halves, tiles, stride=8), :] = column
    out_ref[pl.ds(3 * halves + 1, tiles, stride=8), :] = column


def lookup_kernel(
    got_ref, sky_ref, data_ref, signal_ref, cosine_ref, sine_ref, pixel_ref, sums_ref,
    table, high, low,
):
    tiles = got_ref.shape[0] // 8
    cap = data_ref.shape[1]
    halves = cap // LANES
    rows = sky_ref.shape[1]
    cycles = 2
    nphi = rows * LANES // cycles

    for c in range(3):
        part = split(sky_ref[c].T)
        table[c * LANES : (c + 1) * LANES, :rows] = part[0]
        table[c * LANES : (c + 1) * LANES, rows:] = part[1]

    def received(field):
        parts = [got_ref[pl.ds(field * halves + h, tiles, stride=8), :] for h in range(halves)]
        return jnp.concatenate(parts, axis=1)

    data = received(0)
    angle = received(1)
    pixel = received(2).astype(jnp.int32)
    count = got_ref[pl.ds(3 * halves, tiles, stride=8), :]
    count = jnp.concatenate([count] * halves, axis=1)
    slot = lax.broadcasted_iota(jnp.int32, (tiles, cap), 1).astype(jnp.float32)
    valid = jnp.where(slot < count, 1.0, 0.0)
    cosine = jnp.cos(2.0 * angle)
    sine = jnp.sin(2.0 * angle)
    cosine_ref[...] = cosine
    sine_ref[...] = sine
    pixel_ref[...] = pixel
    cycle = pixel // nphi
    high[...] = (pixel % nphi) // LANES * cycles + cycle
    low[...] = pixel % LANES

    iota = lax.broadcasted_iota(jnp.int32, (LANES, cap), 0)

    def step(index, carry):
        for g in range(GROUP):
            s = index * GROUP + g
            onehot = jnp.where(iota == high[pl.ds(s, 1), :], 1.0, 0.0).astype(jnp.bfloat16)
            onehot = jnp.concatenate([onehot, onehot], axis=0)
            found = jnp.dot(table[...], onehot, preferred_element_type=jnp.float32)
            mask = iota == low[pl.ds(s, 1), :]
            looked = [
                jnp.sum(
                    jnp.where(mask, found[c * LANES : (c + 1) * LANES], 0.0), axis=0, keepdims=True
                )
                for c in range(3)
            ]
            signal_ref[pl.ds(s, 1), :] = (
                looked[0]
                + looked[1] * cosine_ref[pl.ds(s, 1), :]
                + looked[2] * sine_ref[pl.ds(s, 1), :]
            )
        return carry

    lax.fori_loop(0, tiles // GROUP, step, 0)

    signal = signal_ref[...]
    masked = valid * signal
    signal_ref[...] = masked
    data_ref[...] = valid * data
    cross = jnp.sum(masked * data, axis=1, keepdims=True)
    square = jnp.sum(masked * signal, axis=1, keepdims=True)
    width = sums_ref.shape[1]
    row = lax.broadcasted_iota(jnp.int32, (tiles, width), 0)
    lane = lax.broadcasted_iota(jnp.int32, (tiles, width), 1)
    both = jnp.where(lane == row, cross, 0.0) + jnp.where(lane == row + tiles, square, 0.0)
    line = jnp.sum(both, axis=0, keepdims=True)
    lane = lax.broadcasted_iota(jnp.int32, (1, width), 1)
    for cy in range(cycles):
        hits = jnp.sum(jnp.where(cycle == cy, valid, 0.0), keepdims=True)
        line = jnp.where(lane == 2 * tiles + cy, hits / nphi, line)
    sums_ref[...] = jnp.broadcast_to(line, sums_ref.shape)


def bin_kernel(
    sums_ref, data_ref, signal_ref, cosine_ref, sine_ref, pixel_ref,
    stage_a_ref, twiddle_ref, stage_b_ref,
    gain_ref, binned_ref, weight_ref, send_ref,
    acc, weights, high, low, wide, onehot,
):
    tiles, cap = data_ref.shape
    cycles = 2
    second = twiddle_ref.shape[1]
    first = LANES
    nphi = first * second
    n_tm = lax.axis_size("tm")
    lines = PLANES * cycles
    stride = send_ref.shape[0] // n_tm
    per_band = stride // lines

    total = jnp.sum(sums_ref[...], axis=0, keepdims=True)
    width = total.shape[1]
    row = lax.broadcasted_iota(jnp.int32, (tiles, width), 0)
    lane = lax.broadcasted_iota(jnp.int32, (tiles, width), 1)
    cross = jnp.sum(jnp.where(lane == row, total, 0.0), axis=1, keepdims=True)
    square = jnp.sum(jnp.where(lane == row + tiles, total, 0.0), axis=1, keepdims=True)
    gains = cross / (square + 1e-06)
    for cy in range(cycles):
        at = 2 * tiles + cy
        weight_ref[pl.ds(cy, tiles, stride=cycles), :] = jnp.broadcast_to(
            sums_ref[:, at : at + 1], (tiles, LANES)
        )
    weight_ref[tiles * cycles :, :] = jnp.zeros((8, LANES), jnp.float32)
    position = lax.axis_index("det") * n_tm + lax.axis_index("tm")
    place = lax.broadcasted_iota(jnp.int32, (tiles, 1), 0)
    gain_ref[...] = jnp.sum(jnp.where(place == position, gains, 0.0), axis=0, keepdims=True)

    residual = data_ref[...] - gains * signal_ref[...]
    for c, values in enumerate((residual, residual * cosine_ref[...], residual * sine_ref[...])):
        top = values.astype(jnp.bfloat16).astype(jnp.float32)
        weights[2 * c] = top
        weights[2 * c + 1] = values - top
    pixel = pixel_ref[...]
    low[...] = pixel % second
    high[...] = pixel // nphi * first + (pixel // second) % 2 * (first // 2) + (pixel % nphi) // first

    acc[...] = jnp.zeros_like(acc)
    iota_low = lax.broadcasted_iota(jnp.int32, (second, cap), 0)
    iota_high = lax.broadcasted_iota(jnp.int32, (cycles * first, cap), 0)

    def step(index, carry):
        for g in range(GROUP):
            s = index * GROUP + g
            cut = slice(g * cap, (g + 1) * cap)
            mask = iota_low == low[pl.ds(s, 1), :]
            for i in range(6):
                wide[i * second : (i + 1) * second, cut] = jnp.where(
                    mask, weights[i, pl.ds(s, 1), :], 0.0
                ).astype(jnp.bfloat16)
            onehot[:, cut] = jnp.where(iota_high == high[pl.ds(s, 1), :], 1.0, 0.0).astype(
                jnp.bfloat16
            )
        acc[...] += lax.dot_general(
            wide[...], onehot[...], (((1,), (1,)), ((), ())), preferred_element_type=jnp.float32
        )
        return carry

    lax.fori_loop(0, tiles // GROUP, step, 0)

    blocks = []
    for c in range(3):
        at = 2 * c * second
        map_c = acc[at : at + second, :] + acc[at + second : at + 2 * second, :]
        for cy in range(cycles):
            block = map_c[:, cy * first : (cy + 1) * first]
            blocks.append(block)
            flipped = block.T
            binned_ref[c, pl.ds(cy, first // 2, stride=cycles), :] = jnp.concatenate(
                [flipped[: first // 2], flipped[first // 2 :]], axis=1
            )
    field = jnp.concatenate(blocks, axis=0)
    field_high, field_low = split(field)
    modes = jnp.dot(
        jnp.concatenate([field_high, field_low, field_high], axis=1),
        stage_a_ref[...],
        preferred_element_type=jnp.float32,
    )
    turned = []
    for i in range(3 * cycles):
        real = modes[i * second : (i + 1) * second, :first]
        imag = modes[i * second : (i + 1) * second, first:]
        cos_t = twiddle_ref[0]
        sin_t = twiddle_ref[1]
        turned.append(
            jnp.concatenate([real * cos_t - imag * sin_t, real * sin_t + imag * cos_t], axis=0)
        )
    turned = jnp.concatenate(turned, axis=1)
    turned_high, turned_low = split(turned)
    spectrum = jnp.dot(
        stage_b_ref[...],
        jnp.concatenate([turned_high, turned_low, turned_high], axis=0),
        preferred_element_type=jnp.float32,
    )
    half = second // 2
    for c in range(3):
        for cy in range(cycles):
            at = (c * cycles + cy) * first
            for part in range(2):
                for ql in range(per_band):
                    start = part * half + ql * n_tm
                    line = ql * lines + (2 * c + part) * cycles + cy
                    send_ref[pl.ds(line, n_tm, stride=stride), :] = spectrum[
                        start : start + n_tm, at : at + first
                    ]


def rhs_kernel(
    got_ref, weights_ref, prior_ref, noise_ref, draw_ref, rhs_ref, one_ref, two_ref, lines
):
    count = prior_ref.shape[1]
    per_band = prior_ref.shape[2] // LANES
    n_tm = lax.axis_size("tm")
    cycles = count // n_tm
    each = PLANES * cycles
    stride = per_band * each
    start = pl.multiple_of(lax.axis_index("det") * count, 8)
    root_weight = jnp.sqrt(weights_ref[pl.ds(start, count), :])
    for ql in range(per_band):
        cut = slice(ql * LANES, (ql + 1) * LANES)
        for p in range(PLANES):
            for cy in range(cycles):
                lines[p, pl.ds(cy, n_tm, stride=cycles), :] = got_ref[
                    pl.ds(ql * each + p * cycles + cy, n_tm, stride=stride), :
                ]
        for c in range(3):
            root = jnp.sqrt(prior_ref[c, :, cut])
            for p in (2 * c, 2 * c + 1):
                rhs_ref[p, :, cut] = (
                    lines[p] + root_weight * noise_ref[p, :, cut] + root * draw_ref[p, :, cut]
                )
    even = lax.axis_index("det") % 2 == 0
    for ref in (one_ref, two_ref):
        ref[(PLANES + 3) * HALO :, :] = jnp.zeros_like(ref[(PLANES + 3) * HALO :, :])
    for p in range(PLANES + 3):
        source = rhs_ref.at[p] if p < PLANES else prior_ref.at[p - PLANES]
        head = source[:HALO, :]
        tail = source[count - HALO :, :]
        one_ref[p * HALO : (p + 1) * HALO, :] = jnp.where(even, tail, head)
        two_ref[p * HALO : (p + 1) * HALO, :] = jnp.where(even, head, tail)


def krylov_kernel(
    rhs_ref, weights_ref, prior_ref, from_one_ref, from_two_ref, one_ref, two_ref, sums_ref, wide
):
    count = rhs_ref.shape[1]
    rows = count + BLOCK
    band = rhs_ref.shape[2]
    group = lax.axis_index("det")
    even = group % 2 == 0
    has_before = group > 0
    has_after = group < lax.axis_size("det") - 1
    own = lax.broadcasted_iota(jnp.int32, (rows, band), 0) < count
    start = pl.multiple_of(group * count, BLOCK)
    before = pl.multiple_of(jnp.maximum(start - BLOCK, 0), BLOCK)
    place = lax.broadcasted_iota(jnp.int32, (BLOCK, LANES), 0)
    beyond = jnp.where(
        place < BLOCK - HALO,
        weights_ref[pl.ds(start + count, BLOCK), :],
        weights_ref[pl.ds(before, BLOCK), :],
    )
    weight = jnp.concatenate([weights_ref[pl.ds(start, count), :], beyond], axis=0)
    weight = jnp.concatenate([weight] * (band // LANES), axis=1)
    sums = [jnp.zeros((rows, band), jnp.float32) for _ in range(6)]

    def extended(values, p):
        here = slice(p * HALO, (p + 1) * HALO)
        one, two = from_one_ref[here, :], from_two_ref[here, :]
        wide[:count, :] = values
        wide[count : count + HALO, :] = jnp.where(has_after, jnp.where(even, one, two), 0.0)
        wide[rows - HALO :, :] = jnp.where(has_before, jnp.where(even, two, one), 0.0)
        return wide[...]

    wide[count:, :] = jnp.zeros((BLOCK, band), jnp.float32)
    for c in range(3):
        precision = extended(prior_ref[c], PLANES + c)
        root = jnp.sqrt(precision)
        diagonal = (precision + weight - SHIFT) * (1.0 / SPREAD)
        beside = root * (COUPLING / SPREAD)

        def apply(field):
            scaled = root * field
            return diagonal * field - beside * (
                pltpu.roll(scaled, 1, 0) + pltpu.roll(scaled, rows - 1, 0)
            )

        for part in range(2):
            p = 2 * c + part
            zero = extended(rhs_ref[p], p)
            one = apply(zero)
            two = apply(one)
            one_ref[p] = one[:count]
            two_ref[p] = two[:count]
            scaled = root * two
            pair = scaled * pltpu.roll(scaled, rows - 1, 0)
            for i, term in enumerate(
                (
                    zero * zero,
                    zero * one,
                    one * one,
                    one * two,
                    two * two,
                    diagonal * two * two - (2.0 * COUPLING / SPREAD) * pair,
                )
            ):
                sums[i] = sums[i] + term
    lane = lax.broadcasted_iota(jnp.int32, (1, LANES), 1)
    line = jnp.zeros((1, LANES), jnp.float32)
    for i in range(6):
        part = jnp.sum(jnp.where(own, sums[i], 0.0), keepdims=True)
        line = jnp.where(lane == i, part, line)
    sums_ref[...] = jnp.broadcast_to(line, sums_ref.shape)


def inner(left, right, moments):
    result = 0.0
    for i, a in enumerate(left):
        for j, b in enumerate(right):
            result = result + a * b * moments[i + j]
    return result


def operated(coefficients):
    result = [SHIFT * a for a in coefficients] + [0.0]
    for i, a in enumerate(coefficients):
        result[i + 1] = result[i + 1] + SPREAD * a
    return result


def padded(values, length):
    return list(values) + [0.0] * (length - len(values))


def conjugate_gradient(moments):
    resid = [1.0]
    direction = [1.0]
    solution = [0.0]
    norm_now = moments[0]
    for iteration in range(3):
        image = operated(direction)
        alpha = norm_now / inner(direction, image, moments)
        size = len(direction)
        solution = [a + alpha * b for a, b in zip(padded(solution, size), direction)]
        if iteration == 2:
            break
        resid = [a - alpha * b for a, b in zip(padded(resid, size + 1), image)]
        norm_next = inner(resid, resid, moments)
        beta = norm_next / norm_now
        direction = [a + beta * b for a, b in zip(resid, padded(direction, size + 1))]
        norm_now = norm_next
    return solution


def final_kernel(sums_ref, rhs_ref, one_ref, two_ref, out_ref):
    total = jnp.sum(sums_ref[...], axis=0, keepdims=True)
    moments = [total[:, i : i + 1] for i in range(6)]
    zero_by, one_by, two_by = conjugate_gradient(moments)
    for p in range(PLANES):
        out_ref[p] = zero_by * rhs_ref[p] + one_by * one_ref[p] + two_by * two_ref[p]


def call(kernel, name, outs, scratch=(), in_specs=None, limit=24):
    extra = {} if in_specs is None else {"in_specs": in_specs}
    return pl.pallas_call(
        kernel,
        out_shape=tuple(jax.ShapeDtypeStruct(shape, dtype) for shape, dtype in outs),
        scratch_shapes=list(scratch),
        compiler_params=pltpu.CompilerParams(vmem_limit_bytes=limit * 2**20),
        name=name,
        **extra,
    )


def exchange(values, axes):
    return lax.all_to_all(values, axes, split_axis=0, concat_axis=0, tiled=True)


def per_device(
    samples, pointing, angles, counts, sky_map, prior_precision, omega_noise, omega_prior
):
    f32, i32, bf16 = jnp.float32, jnp.int32, jnp.bfloat16
    tiles, cap = samples.shape[2:]
    n_det, n_tm = lax.axis_size("det"), lax.axis_size("tm")
    devices = n_det * n_tm
    cycles, nphi = sky_map.shape[1:]
    count, band = prior_precision.shape[1:]
    second = nphi // LANES
    everywhere = ("det", "tm")
    pairs = [(i, i ^ 1) for i in range(n_det)]
    others = [(i, (i + 1 if i % 2 else i - 1) % n_det) for i in range(n_det)]

    packed = call(
        pack_kernel,
        "pack",
        [((tiles * 8, LANES), f32)],
        [
            pltpu.VMEM((tiles, cap), f32),
            pltpu.VMEM((tiles, cap), f32),
            pltpu.VMEM((tiles, cap), i32),
            pltpu.VMEM((1, tiles), i32),
            pltpu.SemaphoreType.DMA((4,)),
        ],
        [pl.BlockSpec(memory_space=pltpu.HBM)] * 4,
        60,
    )(
        samples.reshape(tiles, cap),
        angles.reshape(tiles, cap),
        pointing.reshape(tiles, cap),
        counts.reshape(1, tiles),
    )[0]
    got = exchange(packed.reshape(tiles, 8, LANES), everywhere).reshape(tiles * 8, LANES)

    sky = sky_map.reshape(3, cycles, second, LANES).transpose(0, 2, 1, 3)
    sky = sky.reshape(3, second * cycles, LANES)
    width = LANES * -(-(2 * tiles + cycles) // LANES)
    data, signal, cosine, sine, pixel, sums = call(
        lookup_kernel,
        "lookup",
        [((tiles, cap), f32)] * 4 + [((tiles, cap), i32), ((devices, width), f32)],
        [
            pltpu.VMEM((3 * LANES, 2 * second * cycles), bf16),
            pltpu.VMEM((tiles, cap), i32),
            pltpu.VMEM((tiles, cap), i32),
        ],
    )(got, sky)
    sums = exchange(sums, everywhere)

    stage_a, twiddle, stage_b = dft_tables(nphi, n_tm)
    gain, binned, weights, send = call(
        bin_kernel,
        "bin",
        [
            ((1, 1), f32),
            ((3, second * cycles, LANES), f32),
            ((tiles * cycles + 8, LANES), f32),
            ((PLANES * cycles * n_tm * band // LANES, LANES), f32),
        ],
        [
            pltpu.VMEM((6 * second, cycles * LANES), f32),
            pltpu.VMEM((6, tiles, cap), f32),
            pltpu.VMEM((tiles, cap), i32),
            pltpu.VMEM((tiles, cap), i32),
            pltpu.VMEM((6 * second, GROUP * cap), bf16),
            pltpu.VMEM((cycles * LANES, GROUP * cap), bf16),
        ],
    )(sums, data, signal, cosine, sine, pixel, stage_a, twiddle, stage_b)
    binned = binned.reshape(3, second, cycles, LANES).transpose(0, 2, 1, 3).reshape(3, cycles, nphi)

    got = exchange(send.reshape(n_tm, -1, LANES), "tm").reshape(-1, LANES)
    halo_rows = -(-(PLANES + 3) * HALO // 8) * 8
    rhs, to_one, to_two = call(
        rhs_kernel,
        "rhs",
        [((PLANES, count, band), f32)] + [((halo_rows, band), f32)] * 2,
        [pltpu.VMEM((PLANES, count, LANES), f32)],
    )(got, weights, prior_precision, omega_noise, omega_prior)
    from_one = lax.ppermute(to_one, "det", pairs)
    from_two = lax.ppermute(to_two, "det", others)
    one, two, sums = call(
        krylov_kernel,
        "krylov",
        [((PLANES, count, band), f32)] * 2 + [((devices, LANES), f32)],
        [pltpu.VMEM((count + BLOCK, band), f32)],
    )(rhs, weights, prior_precision, from_one, from_two)
    sums = exchange(sums, everywhere)
    solution = call(final_kernel, "final", [((PLANES, count, band), f32)])(sums, rhs, one, two)[0]
    return (gain, binned, solution)


def solution(mesh):
    return jax.shard_map(
        per_device,
        mesh=mesh,
        in_specs=(
            P("det", "tm", None, None),
            P("det", "tm", None, None),
            P("det", "tm", None, None),
            P("det", "tm", None),
            P(None, ("det", "tm"), None),
            P(None, "det", "tm"),
            P(None, "det", "tm"),
            P(None, "det", "tm"),
        ),
        out_specs=(P("det", "tm"), P(None, ("det", "tm"), None), P(None, "det", "tm")),
        check_vma=False,
    )
```

```python
import math

import jax
import jax.numpy as jnp
import ml_dtypes
import numpy as np
from jax import lax
from jax.experimental import pallas as pl
from jax.experimental.pallas import tpu as pltpu
from jax.sharding import PartitionSpec as P

SHIFT = 5.0
SPREAD = 5.0
COUPLING = 0.45

LANES = 128
GROUP = 32
PLANES = 6
HALO = 3
BLOCK = 8


def split_np(table):
    high = table.astype(ml_dtypes.bfloat16)
    low = (table - high.astype(np.float64)).astype(ml_dtypes.bfloat16)
    return high, low


def split(values):
    high = values.astype(jnp.bfloat16)
    low = (values - high.astype(jnp.float32)).astype(jnp.bfloat16)
    return high, low


def dft_tables(nphi, n_tm):
    first, second = LANES, nphi // LANES
    half = second // 2
    column = np.arange(first)
    digit = 2 * (column % (first // 2)) + column // (first // 2)
    k = np.arange(first)
    angle = 2.0 * math.pi / first * (np.outer(digit, k) % first)
    stage_a = np.concatenate([np.cos(angle), np.sin(angle)], axis=1)
    high, low = split_np(stage_a)
    stage_a = np.concatenate([high, high, low], axis=0)
    b = np.arange(second)
    angle = 2.0 * math.pi / nphi * (np.outer(b, k) % nphi)
    twiddle = np.stack([np.cos(angle), np.sin(angle)]).astype(np.float32)
    per_band = half // n_tm
    row = np.arange(half)
    q = (row % n_tm) * per_band + row // n_tm
    angle = 2.0 * math.pi / second * (np.outer(q, b) % second)
    cos_b, sin_b = np.cos(angle), np.sin(angle)
    stage_b = np.block([[cos_b, -sin_b], [-sin_b, -cos_b]]) / math.sqrt(nphi)
    high, low = split_np(stage_b)
    stage_b = np.concatenate([high, high, low], axis=1)
    return stage_a, twiddle, stage_b


def pack_kernel(
    samples_hbm, angles_hbm, pointing_hbm, counts_hbm, out_ref,
    samples_ref, angles_ref, pointing_ref, counts_ref, sems,
):
    copies = [
        pltpu.make_async_copy(source, target, sems.at[i])
        for i, (source, target) in enumerate(
            (
                (samples_hbm, samples_ref),
                (angles_hbm, angles_ref),
                (pointing_hbm, pointing_ref),
                (counts_hbm, counts_ref),
            )
        )
    ]
    for copy in copies:
        copy.start()
    for copy in copies:
        copy.wait()
    tiles = samples_ref.shape[0]
    halves = samples_ref.shape[1] // LANES
    lines = 3 * halves + 1
    for h in range(halves):
        cut = slice(h * LANES, (h + 1) * LANES)
        out_ref[pl.ds(h, tiles, stride=lines), :] = samples_ref[:, cut]
        out_ref[pl.ds(halves + h, tiles, stride=lines), :] = angles_ref[:, cut]
        out_ref[pl.ds(2 * halves + h, tiles, stride=lines), :] = pointing_ref[:, cut].astype(
            jnp.float32
        )
    count = counts_ref[...].astype(jnp.float32)
    row = lax.broadcasted_iota(jnp.int32, (tiles, tiles), 0)
    col = lax.broadcasted_iota(jnp.int32, (tiles, tiles), 1)
    column = jnp.sum(jnp.where(row == col, count, 0.0), axis=1, keepdims=True)
    out_ref[pl.ds(3 * halves, tiles, stride=lines), :] = jnp.broadcast_to(column, (tiles, LANES))


def lookup_kernel(
    got_ref, sky_ref, data_ref, signal_ref, cosine_ref, sine_ref, pixel_ref, sums_ref,
    table, high, low,
):
    tiles, cap = data_ref.shape
    halves = cap // LANES
    lines = 3 * halves + 1
    rows = sky_ref.shape[1]
    cycles = 2
    nphi = rows * LANES // cycles

    for c in range(3):
        part = split(sky_ref[c].T)
        table[c * LANES : (c + 1) * LANES, :rows] = part[0]
        table[c * LANES : (c + 1) * LANES, rows:] = part[1]

    def received(field):
        parts = [got_ref[pl.ds(field * halves + h, tiles, stride=lines), :] for h in range(halves)]
        return jnp.concatenate(parts, axis=1)

    data = received(0)
    angle = received(1)
    pixel = received(2).astype(jnp.int32)
    count = got_ref[pl.ds(3 * halves, tiles, stride=lines), :]
    count = jnp.concatenate([count] * halves, axis=1)
    slot = lax.broadcasted_iota(jnp.int32, (tiles, cap), 1).astype(jnp.float32)
    valid = jnp.where(slot < count, 1.0, 0.0)
    cosine = jnp.cos(2.0 * angle)
    sine = jnp.sin(2.0 * angle)
    cosine_ref[...] = cosine
    sine_ref[...] = sine
    pixel_ref[...] = pixel
    cycle = pixel // nphi
    high[...] = (pixel % nphi) // LANES * cycles + cycle
    low[...] = pixel % LANES

    iota = lax.broadcasted_iota(jnp.int32, (LANES, cap), 0)

    def step(index, carry):
        for g in range(GROUP):
            s = index * GROUP + g
            onehot = jnp.where(iota == high[pl.ds(s, 1), :], 1.0, 0.0).astype(jnp.bfloat16)
            onehot = jnp.concatenate([onehot, onehot], axis=0)
            found = jnp.dot(table[...], onehot, preferred_element_type=jnp.float32)
            mask = iota == low[pl.ds(s, 1), :]
            looked = [
                jnp.sum(
                    jnp.where(mask, found[c * LANES : (c + 1) * LANES], 0.0), axis=0, keepdims=True
                )
                for c in range(3)
            ]
            signal_ref[pl.ds(s, 1), :] = (
                looked[0]
                + looked[1] * cosine_ref[pl.ds(s, 1), :]
                + looked[2] * sine_ref[pl.ds(s, 1), :]
            )
        return carry

    lax.fori_loop(0, tiles // GROUP, step, 0)

    signal = signal_ref[...]
    masked = valid * signal
    signal_ref[...] = masked
    data_ref[...] = valid * data
    cross = jnp.sum(masked * data, axis=1, keepdims=True)
    square = jnp.sum(masked * signal, axis=1, keepdims=True)
    width = sums_ref.shape[1]
    row = lax.broadcasted_iota(jnp.int32, (tiles, width), 0)
    lane = lax.broadcasted_iota(jnp.int32, (tiles, width), 1)
    both = jnp.where(lane == row, cross, 0.0) + jnp.where(lane == row + tiles, square, 0.0)
    line = jnp.sum(both, axis=0, keepdims=True)
    lane = lax.broadcasted_iota(jnp.int32, (1, width), 1)
    for cy in range(cycles):
        hits = jnp.sum(jnp.where(cycle == cy, valid, 0.0), keepdims=True)
        line = jnp.where(lane == 2 * tiles + cy, hits / nphi, line)
    sums_ref[...] = jnp.broadcast_to(line, sums_ref.shape)


def bin_kernel(
    sums_ref, data_ref, signal_ref, cosine_ref, sine_ref, pixel_ref,
    stage_a_ref, twiddle_ref, stage_b_ref,
    gain_ref, maps_ref, weight_ref, send_ref,
    acc, weights, high, low, wide, onehot,
):
    tiles, cap = data_ref.shape
    cycles = 2
    second = twiddle_ref.shape[1]
    first = LANES
    nphi = first * second
    n_tm = lax.axis_size("tm")
    lines = PLANES * cycles
    stride = send_ref.shape[0] // n_tm
    per_band = stride // lines

    total = jnp.sum(sums_ref[...], axis=0, keepdims=True)
    width = total.shape[1]
    row = lax.broadcasted_iota(jnp.int32, (tiles, width), 0)
    lane = lax.broadcasted_iota(jnp.int32, (tiles, width), 1)
    cross = jnp.sum(jnp.where(lane == row, total, 0.0), axis=1, keepdims=True)
    square = jnp.sum(jnp.where(lane == row + tiles, total, 0.0), axis=1, keepdims=True)
    gains = cross / (square + 1e-06)
    for cy in range(cycles):
        at = 2 * tiles + cy
        weight_ref[pl.ds(cy, tiles, stride=cycles), :] = jnp.broadcast_to(
            sums_ref[:, at : at + 1], (tiles, LANES)
        )
    weight_ref[tiles * cycles :, :] = jnp.zeros((8, LANES), jnp.float32)
    position = lax.axis_index("det") * n_tm + lax.axis_index("tm")
    place = lax.broadcasted_iota(jnp.int32, (tiles, 1), 0)
    gain_ref[...] = jnp.sum(jnp.where(place == position, gains, 0.0), axis=0, keepdims=True)

    residual = data_ref[...] - gains * signal_ref[...]
    for c, values in enumerate((residual, residual * cosine_ref[...], residual * sine_ref[...])):
        top = values.astype(jnp.bfloat16).astype(jnp.float32)
        weights[2 * c] = top
        weights[2 * c + 1] = values - top
    pixel = pixel_ref[...]
    low[...] = pixel % second
    high[...] = pixel // nphi * first + (pixel // second) % 2 * (first // 2) + (pixel % nphi) // first

    acc[...] = jnp.zeros_like(acc)
    iota_low = lax.broadcasted_iota(jnp.int32, (second, cap), 0)
    iota_high = lax.broadcasted_iota(jnp.int32, (cycles * first, cap), 0)

    def step(index, carry):
        for g in range(GROUP):
            s = index * GROUP + g
            cut = slice(g * cap, (g + 1) * cap)
            mask = iota_low == low[pl.ds(s, 1), :]
            for i in range(6):
                wide[i * second : (i + 1) * second, cut] = jnp.where(
                    mask, weights[i, pl.ds(s, 1), :], 0.0
                ).astype(jnp.bfloat16)
            onehot[:, cut] = jnp.where(iota_high == high[pl.ds(s, 1), :], 1.0, 0.0).astype(
                jnp.bfloat16
            )
        acc[...] += lax.dot_general(
            wide[...], onehot[...], (((1,), (1,)), ((), ())), preferred_element_type=jnp.float32
        )
        return carry

    lax.fori_loop(0, tiles // GROUP, step, 0)

    blocks = []
    for c in range(3):
        at = 2 * c * second
        map_c = acc[at : at + second, :] + acc[at + second : at + 2 * second, :]
        for cy in range(cycles):
            block = map_c[:, cy * first : (cy + 1) * first]
            blocks.append(block)
            maps_ref[c * second : (c + 1) * second, cy * first : (cy + 1) * first] = block
    field = jnp.concatenate(blocks, axis=0)
    field_high, field_low = split(field)
    modes = jnp.dot(
        jnp.concatenate([field_high, field_low, field_high], axis=1),
        stage_a_ref[...],
        preferred_element_type=jnp.float32,
    )
    turned = []
    for i in range(3 * cycles):
        real = modes[i * second : (i + 1) * second, :first]
        imag = modes[i * second : (i + 1) * second, first:]
        cos_t = twiddle_ref[0]
        sin_t = twiddle_ref[1]
        turned.append(
            jnp.concatenate([real * cos_t - imag * sin_t, real * sin_t + imag * cos_t], axis=0)
        )
    turned = jnp.concatenate(turned, axis=1)
    turned_high, turned_low = split(turned)
    spectrum = jnp.dot(
        stage_b_ref[...],
        jnp.concatenate([turned_high, turned_low, turned_high], axis=0),
        preferred_element_type=jnp.float32,
    )
    half = second // 2
    for c in range(3):
        for cy in range(cycles):
            at = (c * cycles + cy) * first
            for part in range(2):
                for ql in range(per_band):
                    start = part * half + ql * n_tm
                    line = ql * lines + (2 * c + part) * cycles + cy
                    send_ref[pl.ds(line, n_tm, stride=stride), :] = spectrum[
                        start : start + n_tm, at : at + first
                    ]


def flip_kernel(maps_ref, binned_ref):
    first = LANES
    cycles = maps_ref.shape[1] // first
    second = maps_ref.shape[0] // 3
    for c in range(3):
        for cy in range(cycles):
            flipped = maps_ref[c * second : (c + 1) * second, cy * first : (cy + 1) * first].T
            binned_ref[c, pl.ds(cy, first // 2, stride=cycles), :] = jnp.concatenate(
                [flipped[: first // 2], flipped[first // 2 :]], axis=1
            )


def rhs_kernel(
    got_ref, weights_ref, prior_ref, noise_ref, draw_ref, rhs_ref, one_ref, two_ref, lines
):
    count = prior_ref.shape[1]
    per_band = prior_ref.shape[2] // LANES
    n_tm = lax.axis_size("tm")
    cycles = count // n_tm
    each = PLANES * cycles
    stride = per_band * each
    start = pl.multiple_of(lax.axis_index("det") * count, 8)
    root_weight = jnp.sqrt(weights_ref[pl.ds(start, count), :])
    for ql in range(per_band):
        cut = slice(ql * LANES, (ql + 1) * LANES)
        for p in range(PLANES):
            for cy in range(cycles):
                lines[p, pl.ds(cy, n_tm, stride=cycles), :] = got_ref[
                    pl.ds(ql * each + p * cycles + cy, n_tm, stride=stride), :
                ]
        for c in range(3):
            root = jnp.sqrt(prior_ref[c, :, cut])
            for p in (2 * c, 2 * c + 1):
                rhs_ref[p, :, cut] = (
                    lines[p] + root_weight * noise_ref[p, :, cut] + root * draw_ref[p, :, cut]
                )
    even = lax.axis_index("det") % 2 == 0
    after = PLANES * HALO
    for p in range(PLANES):
        c = p // 2
        head = rhs_ref[p, :HALO, :]
        tail = rhs_ref[p, count - HALO :, :]
        row = lax.broadcasted_iota(jnp.int32, head.shape, 0)
        head = jnp.where(row == HALO - 1, jnp.sqrt(prior_ref[c, :HALO, :]) * head, head)
        tail = jnp.where(row == HALO - 2, jnp.sqrt(prior_ref[c, count - HALO :, :]) * tail, tail)
        one_ref[p * HALO : (p + 1) * HALO, :] = jnp.where(even, tail, head)
        two_ref[p * HALO : (p + 1) * HALO, :] = jnp.where(even, head, tail)
    for c in range(3):
        head = prior_ref[c, :2, :]
        tail = prior_ref[c, count - 2 :, :]
        one_ref[after + 2 * c : after + 2 * c + 2, :] = jnp.where(even, tail, head)
        two_ref[after + 2 * c : after + 2 * c + 2, :] = jnp.where(even, head, tail)


def krylov_kernel(
    rhs_ref, weights_ref, prior_ref, from_one_ref, from_two_ref, one_ref, two_ref, sums_ref, wide, prior_wide
):
    count = rhs_ref.shape[1]
    rows = count + BLOCK
    band = rhs_ref.shape[2]
    group = lax.axis_index("det")
    even = group % 2 == 0
    has_before = group > 0
    has_after = group < lax.axis_size("det") - 1
    own = lax.broadcasted_iota(jnp.int32, (rows, band), 0) < count
    start = pl.multiple_of(group * count, BLOCK)
    before = pl.multiple_of(jnp.maximum(start - BLOCK, 0), BLOCK)
    place = lax.broadcasted_iota(jnp.int32, (BLOCK, LANES), 0)
    beyond = jnp.where(
        place < BLOCK - HALO,
        weights_ref[pl.ds(start + count, BLOCK), :],
        weights_ref[pl.ds(before, BLOCK), :],
    )
    weight = jnp.concatenate([weights_ref[pl.ds(start, count), :], beyond], axis=0)
    weight = jnp.concatenate([weight] * (band // LANES), axis=1)
    sums = [jnp.zeros((rows, band), jnp.float32) for _ in range(6)]

    def arrived(at, size):
        one, two = from_one_ref[at : at + size, :], from_two_ref[at : at + size, :]
        ahead = jnp.where(has_after, jnp.where(even, one, two), 0.0)
        behind = jnp.where(has_before, jnp.where(even, two, one), 0.0)
        return ahead, behind

    wide[count:, :] = jnp.zeros((BLOCK, band), jnp.float32)
    prior_wide[count:, :] = jnp.ones((BLOCK, band), jnp.float32)

    def extended(p):
        ahead, behind = arrived(p * HALO, HALO)
        wide[:count, :] = rhs_ref[p]
        wide[count : count + HALO, :] = ahead
        wide[rows - 2 :, :] = behind[HALO - 2 :]
        return wide[...]

    for c in range(3):
        ahead, behind = arrived(PLANES * HALO + 2 * c, 2)
        prior_wide[:count, :] = prior_ref[c]
        prior_wide[count : count + 2, :] = ahead
        prior_wide[rows - 1 :, :] = behind[1:]
        precision = prior_wide[...]
        root = jnp.sqrt(precision)
        diagonal = (precision + weight - SHIFT) * (1.0 / SPREAD)
        beside = root * (COUPLING / SPREAD)

        def apply(field):
            scaled = root * field
            return diagonal * field - beside * (
                pltpu.roll(scaled, 1, 0) + pltpu.roll(scaled, rows - 1, 0)
            )

        for part in range(2):
            p = 2 * c + part
            zero = extended(p)
            one = apply(zero)
            two = apply(one)
            one_ref[p] = one[:count]
            two_ref[p] = two[:count]
            scaled = root * two
            pair = scaled * pltpu.roll(scaled, rows - 1, 0)
            for i, term in enumerate(
                (
                    zero * zero,
                    zero * one,
                    one * one,
                    one * two,
                    two * two,
                    diagonal * two * two - (2.0 * COUPLING / SPREAD) * pair,
                )
            ):
                sums[i] = sums[i] + term
    lane = lax.broadcasted_iota(jnp.int32, (1, LANES), 1)
    line = jnp.zeros((1, LANES), jnp.float32)
    for i in range(6):
        part = jnp.sum(jnp.where(own, sums[i], 0.0), keepdims=True)
        line = jnp.where(lane == i, part, line)
    sums_ref[...] = jnp.broadcast_to(line, sums_ref.shape)


def inner(left, right, moments):
    result = 0.0
    for i, a in enumerate(left):
        for j, b in enumerate(right):
            result = result + a * b * moments[i + j]
    return result


def operated(coefficients):
    result = [SHIFT * a for a in coefficients] + [0.0]
    for i, a in enumerate(coefficients):
        result[i + 1] = result[i + 1] + SPREAD * a
    return result


def padded(values, length):
    return list(values) + [0.0] * (length - len(values))


def conjugate_gradient(moments):
    resid = [1.0]
    direction = [1.0]
    solution = [0.0]
    norm_now = moments[0]
    for iteration in range(3):
        image = operated(direction)
        alpha = norm_now / inner(direction, image, moments)
        size = len(direction)
        solution = [a + alpha * b for a, b in zip(padded(solution, size), direction)]
        if iteration == 2:
            break
        resid = [a - alpha * b for a, b in zip(padded(resid, size + 1), image)]
        norm_next = inner(resid, resid, moments)
        beta = norm_next / norm_now
        direction = [a + beta * b for a, b in zip(resid, padded(direction, size + 1))]
        norm_now = norm_next
    return solution


def final_kernel(sums_ref, rhs_ref, one_ref, two_ref, out_ref):
    total = jnp.sum(sums_ref[...], axis=0, keepdims=True)
    moments = [total[:, i : i + 1] for i in range(6)]
    zero_by, one_by, two_by = conjugate_gradient(moments)
    for p in range(PLANES):
        out_ref[p] = zero_by * rhs_ref[p] + one_by * one_ref[p] + two_by * two_ref[p]


def call(kernel, name, outs, scratch=(), in_specs=None, limit=24):
    extra = {} if in_specs is None else {"in_specs": in_specs}
    return pl.pallas_call(
        kernel,
        out_shape=tuple(jax.ShapeDtypeStruct(shape, dtype) for shape, dtype in outs),
        scratch_shapes=list(scratch),
        compiler_params=pltpu.CompilerParams(vmem_limit_bytes=limit * 2**20),
        name=name,
        **extra,
    )


def exchange(values, axes):
    return lax.all_to_all(values, axes, split_axis=0, concat_axis=0, tiled=True)


def per_device(
    samples, pointing, angles, counts, sky_map, prior_precision, omega_noise, omega_prior
):
    f32, i32, bf16 = jnp.float32, jnp.int32, jnp.bfloat16
    tiles, cap = samples.shape[2:]
    n_det, n_tm = lax.axis_size("det"), lax.axis_size("tm")
    devices = n_det * n_tm
    cycles, nphi = sky_map.shape[1:]
    count, band = prior_precision.shape[1:]
    second = nphi // LANES
    everywhere = ("det", "tm")
    pairs = [(i, i ^ 1) for i in range(n_det)]
    others = [(i, (i + 1 if i % 2 else i - 1) % n_det) for i in range(n_det)]

    lines = 3 * cap // LANES + 1
    packed = call(
        pack_kernel,
        "pack",
        [((tiles * lines, LANES), f32)],
        [
            pltpu.VMEM((tiles, cap), f32),
            pltpu.VMEM((tiles, cap), f32),
            pltpu.VMEM((tiles, cap), i32),
            pltpu.VMEM((1, tiles), i32),
            pltpu.SemaphoreType.DMA((4,)),
        ],
        [pl.BlockSpec(memory_space=pltpu.HBM)] * 4,
    )(
        *(
            pltpu.with_memory_space_constraint(values, pltpu.HBM)
            for values in (
                samples.reshape(tiles, cap),
                angles.reshape(tiles, cap),
                pointing.reshape(tiles, cap),
                counts.reshape(1, tiles),
            )
        )
    )[0]
    got = exchange(packed.reshape(tiles, lines * LANES), everywhere).reshape(tiles * lines, LANES)

    sky = sky_map.reshape(3, cycles, second, LANES).transpose(0, 2, 1, 3)
    sky = sky.reshape(3, second * cycles, LANES)
    width = LANES * -(-(2 * tiles + cycles) // LANES)
    data, signal, cosine, sine, pixel, sums = call(
        lookup_kernel,
        "lookup",
        [((tiles, cap), f32)] * 4 + [((tiles, cap), i32), ((devices, width), f32)],
        [
            pltpu.VMEM((3 * LANES, 2 * second * cycles), bf16),
            pltpu.VMEM((tiles, cap), i32),
            pltpu.VMEM((tiles, cap), i32),
        ],
    )(got, sky)
    sums = exchange(sums, everywhere)

    stage_a, twiddle, stage_b = dft_tables(nphi, n_tm)
    gain, maps, weights, send = call(
        bin_kernel,
        "bin",
        [
            ((1, 1), f32),
            ((3 * second, cycles * LANES), f32),
            ((tiles * cycles + 8, LANES), f32),
            ((PLANES * cycles * n_tm * band // LANES, LANES), f32),
        ],
        [
            pltpu.VMEM((6 * second, cycles * LANES), f32),
            pltpu.VMEM((6, tiles, cap), f32),
            pltpu.VMEM((tiles, cap), i32),
            pltpu.VMEM((tiles, cap), i32),
            pltpu.VMEM((6 * second, GROUP * cap), bf16),
            pltpu.VMEM((cycles * LANES, GROUP * cap), bf16),
        ],
    )(sums, data, signal, cosine, sine, pixel, stage_a, twiddle, stage_b)
    got = exchange(send.reshape(n_tm, -1, LANES), "tm").reshape(-1, LANES)
    halo_rows = PLANES * HALO + 3 * 2
    rhs, to_one, to_two = call(
        rhs_kernel,
        "rhs",
        [((PLANES, count, band), f32)] + [((halo_rows, band), f32)] * 2,
        [pltpu.VMEM((PLANES, count, LANES), f32)],
    )(got, weights, prior_precision, omega_noise, omega_prior)
    maps, to_one, to_two = lax.optimization_barrier((maps, to_one, to_two))
    from_one = lax.ppermute(to_one, "det", pairs)
    from_two = lax.ppermute(to_two, "det", others)
    binned = call(flip_kernel, "flip", [((3, second * cycles, LANES), f32)])(maps)[0]
    binned = binned.reshape(3, second, cycles, LANES).transpose(0, 2, 1, 3).reshape(3, cycles, nphi)
    binned, rhs = lax.optimization_barrier((binned, rhs))
    one, two, sums = call(
        krylov_kernel,
        "krylov",
        [((PLANES, count, band), f32)] * 2 + [((devices, LANES), f32)],
        [pltpu.VMEM((count + BLOCK, band), f32)] * 2,
    )(rhs, weights, prior_precision, from_one, from_two)
    sums = exchange(sums, everywhere)
    solution = call(final_kernel, "final", [((PLANES, count, band), f32)])(sums, rhs, one, two)[0]
    return (gain, binned, solution)


def solution(mesh):
    return jax.shard_map(
        per_device,
        mesh=mesh,
        in_specs=(
            P("det", "tm", None, None),
            P("det", "tm", None, None),
            P("det", "tm", None, None),
            P("det", "tm", None),
            P(None, ("det", "tm"), None),
            P(None, "det", "tm"),
            P(None, "det", "tm"),
            P(None, "det", "tm"),
        ),
        out_specs=(P("det", "tm"), P(None, ("det", "tm"), None), P(None, "det", "tm")),
        check_vma=False,
    )
```

```python
import math

import jax
import jax.numpy as jnp
import ml_dtypes
import numpy as np
from jax import lax
from jax.experimental import pallas as pl
from jax.experimental.pallas import tpu as pltpu
from jax.sharding import PartitionSpec as P

SHIFT = 5.0
SPREAD = 5.0
COUPLING = 0.45

LANES = 128
GROUP = 32
PLANES = 6
HALO = 3
BLOCK = 8


def split_np(table):
    high = table.astype(ml_dtypes.bfloat16)
    low = (table - high.astype(np.float64)).astype(ml_dtypes.bfloat16)
    return high, low


def bits(power):
    return power.bit_length() - 1


def split(values):
    high = values.astype(jnp.bfloat16)
    low = (values - high.astype(jnp.float32)).astype(jnp.bfloat16)
    return high, low


def meeting_order(n_tm):
    if n_tm == 8:
        return [3, 2, 5, 4, 1, 0, 7, 6]
    return [(i + n_tm // 2 + 1) % n_tm for i in range(n_tm)]


def dft_tables(nphi, n_tm):
    first, second = LANES, nphi // LANES
    half = second // 2
    column = np.arange(first)
    digit = 2 * (column % (first // 2)) + column // (first // 2)
    k = np.arange(first)
    angle = 2.0 * math.pi / first * (np.outer(digit, k) % first)
    stage_a = np.concatenate([np.cos(angle), np.sin(angle)], axis=1)
    high, low = split_np(stage_a)
    stage_a = np.concatenate([high, high, low], axis=0)
    b = np.arange(second)
    angle = 2.0 * math.pi / nphi * (np.outer(b, k) % nphi)
    twiddle = np.stack([np.cos(angle), np.sin(angle)]).astype(np.float32)
    per_band = half // n_tm
    row = np.arange(half)
    q = np.array(meeting_order(n_tm))[row % n_tm] * per_band + row // n_tm
    angle = 2.0 * math.pi / second * (np.outer(q, b) % second)
    cos_b, sin_b = np.cos(angle), np.sin(angle)
    stage_b = np.block([[cos_b, -sin_b], [-sin_b, -cos_b]]) / math.sqrt(nphi)
    high, low = split_np(stage_b)
    stage_b = np.concatenate([high, high, low], axis=1)
    return stage_a, twiddle, stage_b


def pack_kernel(
    samples_hbm, angles_hbm, pointing_hbm, counts_hbm, out_ref,
    samples_ref, angles_ref, pointing_ref, counts_ref, sems,
):
    copies = [
        pltpu.make_async_copy(source, target, sems.at[i])
        for i, (source, target) in enumerate(
            (
                (samples_hbm, samples_ref),
                (angles_hbm, angles_ref),
                (pointing_hbm, pointing_ref),
                (counts_hbm, counts_ref),
            )
        )
    ]
    for copy in copies:
        copy.start()
    for copy in copies:
        copy.wait()
    tiles = samples_ref.shape[0]
    halves = samples_ref.shape[1] // LANES
    lines = 3 * halves + 1
    for h in range(halves):
        cut = slice(h * LANES, (h + 1) * LANES)
        out_ref[pl.ds(h, tiles, stride=lines), :] = samples_ref[:, cut]
        out_ref[pl.ds(halves + h, tiles, stride=lines), :] = angles_ref[:, cut]
        out_ref[pl.ds(2 * halves + h, tiles, stride=lines), :] = pointing_ref[:, cut].astype(
            jnp.float32
        )
    count = counts_ref[...].astype(jnp.float32)
    row = lax.broadcasted_iota(jnp.int32, (tiles, tiles), 0)
    col = lax.broadcasted_iota(jnp.int32, (tiles, tiles), 1)
    column = jnp.sum(jnp.where(row == col, count, 0.0), axis=1, keepdims=True)
    out_ref[pl.ds(3 * halves, tiles, stride=lines), :] = jnp.broadcast_to(column, (tiles, LANES))


def repeated(line, rows):
    tile = jnp.broadcast_to(line, (16, line.shape[1])).astype(jnp.bfloat16)
    return jnp.concatenate([tile] * (rows // 16), axis=0)


def lookup_kernel(
    got_ref, sky_ref, data_ref, signal_ref, cosine_ref, sine_ref, line_ref, column_ref, sums_ref,
    table, high, low,
):
    tiles, cap = data_ref.shape
    halves = cap // LANES
    lines = 3 * halves + 1
    rows = sky_ref.shape[1]
    cycles = 2
    nphi = rows * LANES // cycles

    for c in range(3):
        part = split(sky_ref[c].T)
        table[c * LANES : (c + 1) * LANES, :rows] = part[0]
        table[c * LANES : (c + 1) * LANES, rows:] = part[1]

    def received(field):
        parts = [got_ref[pl.ds(field * halves + h, tiles, stride=lines), :] for h in range(halves)]
        return jnp.concatenate(parts, axis=1)

    data = received(0)
    angle = received(1)
    pixel = received(2).astype(jnp.int32)
    count = got_ref[pl.ds(3 * halves, tiles, stride=lines), :]
    count = jnp.concatenate([count] * halves, axis=1)
    slot = lax.broadcasted_iota(jnp.int32, (tiles, cap), 1).astype(jnp.float32)
    valid = jnp.where(slot < count, 1.0, 0.0)
    cosine = jnp.cos(2.0 * angle)
    sine = jnp.sin(2.0 * angle)
    cosine_ref[...] = cosine
    sine_ref[...] = sine
    cycle = pixel >> bits(nphi)
    row = (pixel >> bits(LANES)) & (nphi // LANES - 1)
    high[...] = (row * cycles + cycle).astype(jnp.float32)
    low[...] = pixel & (LANES - 1)
    second = nphi // LANES
    line_ref[...] = (pixel & (second - 1)).astype(jnp.float32)
    column = cycle * LANES + ((pixel >> bits(second)) & 1) * (LANES // 2) + row
    column_ref[...] = column.astype(jnp.float32)

    iota = lax.broadcasted_iota(jnp.int32, (LANES, cap), 0)
    iota_half = iota.astype(jnp.float32).astype(jnp.bfloat16)
    one = jnp.ones((LANES, cap), jnp.bfloat16)
    zero = jnp.zeros((LANES, cap), jnp.bfloat16)

    def step(index, carry):
        for g in range(GROUP):
            s = index * GROUP + g
            onehot = jnp.where(iota_half == repeated(high[pl.ds(s, 1), :], LANES), one, zero)
            onehot = jnp.concatenate([onehot, onehot], axis=0)
            found = jnp.dot(table[...], onehot, preferred_element_type=jnp.float32)
            mask = iota == low[pl.ds(s, 1), :]
            mixed = (
                found[:LANES]
                + found[LANES : 2 * LANES] * cosine_ref[pl.ds(s, 1), :]
                + found[2 * LANES :] * sine_ref[pl.ds(s, 1), :]
            )
            signal_ref[pl.ds(s, 1), :] = jnp.sum(
                jnp.where(mask, mixed, 0.0), axis=0, keepdims=True
            )
        return carry

    lax.fori_loop(0, tiles // GROUP, step, 0)

    signal = signal_ref[...]
    masked = valid * signal
    signal_ref[...] = masked
    data_ref[...] = valid * data
    cross = jnp.sum(masked * data, axis=1, keepdims=True)
    square = jnp.sum(masked * signal, axis=1, keepdims=True)
    width = sums_ref.shape[1]
    row = lax.broadcasted_iota(jnp.int32, (tiles, width), 0)
    lane = lax.broadcasted_iota(jnp.int32, (tiles, width), 1)
    both = jnp.where(lane == row, cross, 0.0) + jnp.where(lane == row + tiles, square, 0.0)
    line = jnp.sum(both, axis=0, keepdims=True)
    lane = lax.broadcasted_iota(jnp.int32, (1, width), 1)
    for cy in range(cycles):
        hits = jnp.sum(jnp.where(cycle == cy, valid, 0.0), keepdims=True)
        line = jnp.where(lane == 2 * tiles + cy, hits / nphi, line)
    sums_ref[...] = jnp.broadcast_to(line, sums_ref.shape)


def all_gains(sums_ref, tiles):
    total = jnp.sum(sums_ref[...], axis=0, keepdims=True)
    row = lax.broadcasted_iota(jnp.int32, (tiles, total.shape[1]), 0)
    lane = lax.broadcasted_iota(jnp.int32, (tiles, total.shape[1]), 1)
    cross = jnp.sum(jnp.where(lane == row, total, 0.0), axis=1, keepdims=True)
    square = jnp.sum(jnp.where(lane == row + tiles, total, 0.0), axis=1, keepdims=True)
    return cross / (square + 1e-06)


def bin_kernel(
    sums_ref, data_ref, signal_ref, cosine_ref, sine_ref, line_ref, column_ref,
    stage_a_ref, twiddle_ref, stage_b_ref, maps_ref, send_ref, acc, weights, wide, onehot,
):
    tiles, cap = data_ref.shape
    cycles = 2
    second = twiddle_ref.shape[1]
    first = LANES
    nphi = first * second
    n_tm = lax.axis_size("tm")
    lines = PLANES * cycles
    stride = send_ref.shape[0] // n_tm
    per_band = stride // lines

    gains = all_gains(sums_ref, tiles)
    residual = data_ref[...] - gains * signal_ref[...]
    for c, values in enumerate((residual, residual * cosine_ref[...], residual * sine_ref[...])):
        top = values.astype(jnp.bfloat16).astype(jnp.float32)
        weights[2 * c] = top
        weights[2 * c + 1] = values - top
    acc[...] = jnp.zeros_like(acc)
    iota_high = lax.broadcasted_iota(jnp.int32, (cycles * first, cap), 0)
    iota_high = iota_high.astype(jnp.float32).astype(jnp.bfloat16)
    iota_low = iota_high[:second]
    zero_low = jnp.zeros((second, cap), jnp.bfloat16)
    zero_high = jnp.zeros((cycles * first, cap), jnp.bfloat16)
    one_high = jnp.ones((cycles * first, cap), jnp.bfloat16)

    def step(index, carry):
        for g in range(GROUP):
            s = index * GROUP + g
            cut = slice(g * cap, (g + 1) * cap)
            mask = iota_low == repeated(line_ref[pl.ds(s, 1), :], second)
            for i in range(6):
                wide[i * second : (i + 1) * second, cut] = jnp.where(
                    mask, repeated(weights[i, pl.ds(s, 1), :], second), zero_low
                )
            onehot[:, cut] = jnp.where(
                iota_high == repeated(column_ref[pl.ds(s, 1), :], cycles * first),
                one_high,
                zero_high,
            )
        acc[...] += lax.dot_general(
            wide[...], onehot[...], (((1,), (1,)), ((), ())), preferred_element_type=jnp.float32
        )
        return carry

    lax.fori_loop(0, tiles // GROUP, step, 0)

    blocks = []
    for c in range(3):
        at = 2 * c * second
        map_c = acc[at : at + second, :] + acc[at + second : at + 2 * second, :]
        for cy in range(cycles):
            block = map_c[:, cy * first : (cy + 1) * first]
            blocks.append(block)
            maps_ref[c * second : (c + 1) * second, cy * first : (cy + 1) * first] = block
    field = jnp.concatenate(blocks, axis=0)
    field_high, field_low = split(field)
    modes = jnp.dot(
        jnp.concatenate([field_high, field_low, field_high], axis=1),
        stage_a_ref[...],
        preferred_element_type=jnp.float32,
    )
    turned = []
    for i in range(3 * cycles):
        real = modes[i * second : (i + 1) * second, :first]
        imag = modes[i * second : (i + 1) * second, first:]
        cos_t = twiddle_ref[0]
        sin_t = twiddle_ref[1]
        turned.append(
            jnp.concatenate([real * cos_t - imag * sin_t, real * sin_t + imag * cos_t], axis=0)
        )
    turned = jnp.concatenate(turned, axis=1)
    turned_high, turned_low = split(turned)
    spectrum = jnp.dot(
        stage_b_ref[...],
        jnp.concatenate([turned_high, turned_low, turned_high], axis=0),
        preferred_element_type=jnp.float32,
    )
    half = second // 2
    for c in range(3):
        for cy in range(cycles):
            at = (c * cycles + cy) * first
            for part in range(2):
                for ql in range(per_band):
                    start = part * half + ql * n_tm
                    line = ql * lines + (2 * c + part) * cycles + cy
                    send_ref[pl.ds(line, n_tm, stride=stride), :] = spectrum[
                        start : start + n_tm, at : at + first
                    ]


def report_kernel(maps_ref, sums_ref, binned_ref, gain_ref, weight_ref):
    first = LANES
    cycles = maps_ref.shape[1] // first
    second = maps_ref.shape[0] // 3
    tiles = sums_ref.shape[0]
    for c in range(3):
        for cy in range(cycles):
            flipped = maps_ref[c * second : (c + 1) * second, cy * first : (cy + 1) * first].T
            binned_ref[c, pl.ds(cy, first // 2, stride=cycles), :] = jnp.concatenate(
                [flipped[: first // 2], flipped[first // 2 :]], axis=1
            )
    position = lax.axis_index("det") * lax.axis_size("tm") + lax.axis_index("tm")
    place = lax.broadcasted_iota(jnp.int32, (tiles, 1), 0)
    own = jnp.where(place == position, all_gains(sums_ref, tiles), 0.0)
    gain_ref[...] = jnp.sum(own, axis=0, keepdims=True)
    for cy in range(cycles):
        at = 2 * tiles + cy
        weight_ref[pl.ds(cy, tiles, stride=cycles), :] = jnp.broadcast_to(
            sums_ref[:, at : at + 1], (tiles, LANES)
        )
    weight_ref[tiles * cycles :, :] = jnp.zeros((BLOCK, LANES), jnp.float32)


def rhs_kernel(
    got_ref, sums_ref, prior_ref, noise_ref, draw_ref, rhs_ref, one_ref, two_ref, lines
):
    count = prior_ref.shape[1]
    per_band = prior_ref.shape[2] // LANES
    n_tm = lax.axis_size("tm")
    cycles = count // n_tm
    each = PLANES * cycles
    stride = per_band * each
    order = meeting_order(n_tm)
    tiles = sums_ref.shape[0]
    group = sums_ref[pl.ds(pl.multiple_of(lax.axis_index("det") * n_tm, 8), n_tm), :]
    for cy in range(cycles):
        at = 2 * tiles + cy
        lines[PLANES, pl.ds(cy, n_tm, stride=cycles), :] = jnp.broadcast_to(
            group[:, at : at + 1], (n_tm, LANES)
        )
    root_weight = jnp.sqrt(lines[PLANES])
    for ql in range(per_band):
        cut = slice(ql * LANES, (ql + 1) * LANES)
        for p in range(PLANES):
            for i, t in enumerate(order):
                at = i * stride + ql * each + p * cycles
                lines[p, t * cycles : (t + 1) * cycles, :] = got_ref[at : at + cycles, :]
        for c in range(3):
            root = jnp.sqrt(prior_ref[c, :, cut])
            for p in (2 * c, 2 * c + 1):
                rhs_ref[p, :, cut] = (
                    lines[p] + root_weight * noise_ref[p, :, cut] + root * draw_ref[p, :, cut]
                )
    even = lax.axis_index("det") % 2 == 0
    after = PLANES * HALO
    for p in range(PLANES):
        c = p // 2
        head = rhs_ref[p, :HALO, :]
        tail = rhs_ref[p, count - HALO :, :]
        row = lax.broadcasted_iota(jnp.int32, head.shape, 0)
        head = jnp.where(row == HALO - 1, jnp.sqrt(prior_ref[c, :HALO, :]) * head, head)
        tail = jnp.where(row == HALO - 2, jnp.sqrt(prior_ref[c, count - HALO :, :]) * tail, tail)
        one_ref[p * HALO : (p + 1) * HALO, :] = jnp.where(even, tail, head)
        two_ref[p * HALO : (p + 1) * HALO, :] = jnp.where(even, head, tail)
    for c in range(3):
        head = prior_ref[c, :2, :]
        tail = prior_ref[c, count - 2 :, :]
        one_ref[after + 2 * c : after + 2 * c + 2, :] = jnp.where(even, tail, head)
        two_ref[after + 2 * c : after + 2 * c + 2, :] = jnp.where(even, head, tail)


def krylov_kernel(
    rhs_ref, weights_ref, prior_ref, from_one_ref, from_two_ref, one_ref, two_ref, sums_ref, wide, prior_wide
):
    count = rhs_ref.shape[1]
    rows = count + BLOCK
    band = rhs_ref.shape[2]
    group = lax.axis_index("det")
    even = group % 2 == 0
    has_before = group > 0
    has_after = group < lax.axis_size("det") - 1
    own = lax.broadcasted_iota(jnp.int32, (rows, band), 0) < count
    start = pl.multiple_of(group * count, BLOCK)
    before = pl.multiple_of(jnp.maximum(start - BLOCK, 0), BLOCK)
    place = lax.broadcasted_iota(jnp.int32, (BLOCK, LANES), 0)
    beyond = jnp.where(
        place < BLOCK - HALO,
        weights_ref[pl.ds(start + count, BLOCK), :],
        weights_ref[pl.ds(before, BLOCK), :],
    )
    weight = jnp.concatenate([weights_ref[pl.ds(start, count), :], beyond], axis=0)
    weight = jnp.concatenate([weight] * (band // LANES), axis=1)
    sums = [jnp.zeros((rows, band), jnp.float32) for _ in range(6)]

    def arrived(at, size):
        one, two = from_one_ref[at : at + size, :], from_two_ref[at : at + size, :]
        ahead = jnp.where(has_after, jnp.where(even, one, two), 0.0)
        behind = jnp.where(has_before, jnp.where(even, two, one), 0.0)
        return ahead, behind

    wide[count:, :] = jnp.zeros((BLOCK, band), jnp.float32)
    prior_wide[count:, :] = jnp.ones((BLOCK, band), jnp.float32)

    def extended(p):
        ahead, behind = arrived(p * HALO, HALO)
        wide[:count, :] = rhs_ref[p]
        wide[count : count + HALO, :] = ahead
        wide[rows - 2 :, :] = behind[HALO - 2 :]
        return wide[...]

    for c in range(3):
        ahead, behind = arrived(PLANES * HALO + 2 * c, 2)
        prior_wide[:count, :] = prior_ref[c]
        prior_wide[count : count + 2, :] = ahead
        prior_wide[rows - 1 :, :] = behind[1:]
        precision = prior_wide[...]
        root = jnp.sqrt(precision)
        diagonal = (precision + weight - SHIFT) * (1.0 / SPREAD)
        beside = root * (COUPLING / SPREAD)

        def apply(field):
            scaled = root * field
            return diagonal * field - beside * (
                pltpu.roll(scaled, 1, 0) + pltpu.roll(scaled, rows - 1, 0)
            )

        for part in range(2):
            p = 2 * c + part
            zero = extended(p)
            one = apply(zero)
            two = apply(one)
            one_ref[p] = one[:count]
            two_ref[p] = two[:count]
            scaled = root * two
            pair = scaled * pltpu.roll(scaled, rows - 1, 0)
            for i, term in enumerate(
                (
                    zero * zero,
                    zero * one,
                    one * one,
                    one * two,
                    two * two,
                    diagonal * two * two - (2.0 * COUPLING / SPREAD) * pair,
                )
            ):
                sums[i] = sums[i] + term
    lane = lax.broadcasted_iota(jnp.int32, (1, LANES), 1)
    line = jnp.zeros((1, LANES), jnp.float32)
    for i in range(6):
        part = jnp.sum(jnp.where(own, sums[i], 0.0), keepdims=True)
        line = jnp.where(lane == i, part, line)
    sums_ref[...] = jnp.broadcast_to(line, sums_ref.shape)


def inner(left, right, moments):
    result = 0.0
    for i, a in enumerate(left):
        for j, b in enumerate(right):
            result = result + a * b * moments[i + j]
    return result


def operated(coefficients):
    result = [SHIFT * a for a in coefficients] + [0.0]
    for i, a in enumerate(coefficients):
        result[i + 1] = result[i + 1] + SPREAD * a
    return result


def padded(values, length):
    return list(values) + [0.0] * (length - len(values))


def conjugate_gradient(moments):
    resid = [1.0]
    direction = [1.0]
    solution = [0.0]
    norm_now = moments[0]
    for iteration in range(3):
        image = operated(direction)
        alpha = norm_now / inner(direction, image, moments)
        size = len(direction)
        solution = [a + alpha * b for a, b in zip(padded(solution, size), direction)]
        if iteration == 2:
            break
        resid = [a - alpha * b for a, b in zip(padded(resid, size + 1), image)]
        norm_next = inner(resid, resid, moments)
        beta = norm_next / norm_now
        direction = [a + beta * b for a, b in zip(resid, padded(direction, size + 1))]
        norm_now = norm_next
    return solution


def final_kernel(sums_ref, rhs_ref, one_ref, two_ref, out_ref):
    total = jnp.sum(sums_ref[...], axis=0, keepdims=True)
    moments = [total[:, i : i + 1] for i in range(6)]
    zero_by, one_by, two_by = conjugate_gradient(moments)
    for p in range(PLANES):
        out_ref[p] = zero_by * rhs_ref[p] + one_by * one_ref[p] + two_by * two_ref[p]


def call(kernel, name, outs, scratch=(), in_specs=None, limit=24):
    extra = {} if in_specs is None else {"in_specs": in_specs}
    return pl.pallas_call(
        kernel,
        out_shape=tuple(jax.ShapeDtypeStruct(shape, dtype) for shape, dtype in outs),
        scratch_shapes=list(scratch),
        compiler_params=pltpu.CompilerParams(vmem_limit_bytes=limit * 2**20),
        name=name,
        **extra,
    )


def exchange(values, axes, order=None):
    groups = None if order is None else [order]
    return lax.all_to_all(
        values, axes, split_axis=0, concat_axis=0, tiled=True, axis_index_groups=groups
    )


def per_device(
    samples, pointing, angles, counts, sky_map, prior_precision, omega_noise, omega_prior
):
    f32, i32, bf16 = jnp.float32, jnp.int32, jnp.bfloat16
    tiles, cap = samples.shape[2:]
    n_det, n_tm = lax.axis_size("det"), lax.axis_size("tm")
    devices = n_det * n_tm
    cycles, nphi = sky_map.shape[1:]
    count, band = prior_precision.shape[1:]
    second = nphi // LANES
    everywhere = ("det", "tm")
    pairs = [(i, i ^ 1) for i in range(n_det)]
    others = [(i, (i + 1 if i % 2 else i - 1) % n_det) for i in range(n_det)]

    lines = 3 * cap // LANES + 1
    packed = call(
        pack_kernel,
        "pack",
        [((tiles * lines, LANES), f32)],
        [
            pltpu.VMEM((tiles, cap), f32),
            pltpu.VMEM((tiles, cap), f32),
            pltpu.VMEM((tiles, cap), i32),
            pltpu.VMEM((1, tiles), i32),
            pltpu.SemaphoreType.DMA((4,)),
        ],
        [pl.BlockSpec(memory_space=pltpu.HBM)] * 4,
    )(
        *(
            pltpu.with_memory_space_constraint(values, pltpu.HBM)
            for values in (
                samples.reshape(tiles, cap),
                angles.reshape(tiles, cap),
                pointing.reshape(tiles, cap),
                counts.reshape(1, tiles),
            )
        )
    )[0]
    got = exchange(packed.reshape(tiles, lines * LANES), everywhere).reshape(tiles * lines, LANES)

    sky = sky_map.reshape(3, cycles, second, LANES).transpose(0, 2, 1, 3)
    sky = sky.reshape(3, second * cycles, LANES)
    width = LANES * -(-(2 * tiles + cycles) // LANES)
    data, signal, cosine, sine, line, column, sums = call(
        lookup_kernel,
        "lookup",
        [((tiles, cap), f32)] * 6 + [((devices, width), f32)],
        [
            pltpu.VMEM((3 * LANES, 2 * second * cycles), bf16),
            pltpu.VMEM((tiles, cap), f32),
            pltpu.VMEM((tiles, cap), i32),
        ],
    )(got, sky)
    sums = exchange(sums, everywhere)

    stage_a, twiddle, stage_b = dft_tables(nphi, n_tm)
    maps, send = call(
        bin_kernel,
        "bin",
        [
            ((3 * second, cycles * LANES), f32),
            ((PLANES * cycles * n_tm * band // LANES, LANES), f32),
        ],
        [
            pltpu.VMEM((6 * second, cycles * LANES), f32),
            pltpu.VMEM((6, tiles, cap), f32),
            pltpu.VMEM((6 * second, GROUP * cap), bf16),
            pltpu.VMEM((cycles * LANES, GROUP * cap), bf16),
        ],
    )(sums, data, signal, cosine, sine, line, column, stage_a, twiddle, stage_b)

    got = exchange(send.reshape(n_tm, -1, LANES), "tm", meeting_order(n_tm)).reshape(-1, LANES)
    halo_rows = PLANES * HALO + 3 * 2
    rhs, to_one, to_two = call(
        rhs_kernel,
        "rhs",
        [((PLANES, count, band), f32)] + [((halo_rows, band), f32)] * 2,
        [pltpu.VMEM((PLANES + 1, count, LANES), f32)],
    )(got, sums, prior_precision, omega_noise, omega_prior)
    maps, to_one, to_two = lax.optimization_barrier((maps, to_one, to_two))
    from_one = lax.ppermute(to_one, "det", pairs)
    from_two = lax.ppermute(to_two, "det", others)
    binned, gain, weights = call(
        report_kernel,
        "report",
        [
            ((3, second * cycles, LANES), f32),
            ((1, 1), f32),
            ((tiles * cycles + BLOCK, LANES), f32),
        ],
    )(maps, sums)
    binned = binned.reshape(3, second, cycles, LANES).transpose(0, 2, 1, 3).reshape(3, cycles, nphi)
    binned, rhs = lax.optimization_barrier((binned, rhs))
    one, two, sums = call(
        krylov_kernel,
        "krylov",
        [((PLANES, count, band), f32)] * 2 + [((devices, LANES), f32)],
        [pltpu.VMEM((count + BLOCK, band), f32)] * 2,
    )(rhs, weights, prior_precision, from_one, from_two)
    sums = exchange(sums, everywhere)
    solution = call(final_kernel, "final", [((PLANES, count, band), f32)])(sums, rhs, one, two)[0]
    return (gain, binned, solution)


def solution(mesh):
    return jax.shard_map(
        per_device,
        mesh=mesh,
        in_specs=(
            P("det", "tm", None, None),
            P("det", "tm", None, None),
            P("det", "tm", None, None),
            P("det", "tm", None),
            P(None, ("det", "tm"), None),
            P(None, "det", "tm"),
            P(None, "det", "tm"),
            P(None, "det", "tm"),
        ),
        out_specs=(P("det", "tm"), P(None, ("det", "tm"), None), P(None, "det", "tm")),
        check_vma=False,
    )
```

```python
import math

import jax
import jax.numpy as jnp
import ml_dtypes
import numpy as np
from jax import lax
from jax.experimental import pallas as pl
from jax.experimental.pallas import tpu as pltpu
from jax.sharding import PartitionSpec as P

SHIFT = 5.0
SPREAD = 5.0
COUPLING = 0.45

LANES = 128
GROUP = 32
PLANES = 6
HALO = 3
BLOCK = 8


def split_np(table):
    high = table.astype(ml_dtypes.bfloat16)
    low = (table - high.astype(np.float64)).astype(ml_dtypes.bfloat16)
    return high, low


def bits(power):
    return power.bit_length() - 1


def split(values):
    high = values.astype(jnp.bfloat16)
    low = (values - high.astype(jnp.float32)).astype(jnp.bfloat16)
    return high, low


def meeting_order(n_tm):
    if n_tm == 8:
        return [3, 2, 5, 4, 1, 0, 7, 6]
    return [(i + n_tm // 2 + 1) % n_tm for i in range(n_tm)]


def dft_tables(nphi, n_tm):
    first, second = LANES, nphi // LANES
    half = second // 2
    column = np.arange(first)
    digit = 2 * (column % (first // 2)) + column // (first // 2)
    k = np.arange(first)
    angle = 2.0 * math.pi / first * (np.outer(digit, k) % first)
    stage_a = np.concatenate([np.cos(angle), np.sin(angle)], axis=1)
    high, low = split_np(stage_a)
    stage_a = np.concatenate([high, high, low], axis=0)
    b = np.arange(second)
    angle = 2.0 * math.pi / nphi * (np.outer(b, k) % nphi)
    twiddle = np.stack([np.cos(angle), np.sin(angle)]).astype(np.float32)
    per_band = half // n_tm
    row = np.arange(half)
    q = np.array(meeting_order(n_tm))[row % n_tm] * per_band + row // n_tm
    angle = 2.0 * math.pi / second * (np.outer(q, b) % second)
    cos_b, sin_b = np.cos(angle), np.sin(angle)
    stage_b = np.block([[cos_b, -sin_b], [-sin_b, -cos_b]]) / math.sqrt(nphi)
    high, low = split_np(stage_b)
    stage_b = np.concatenate([high, high, low], axis=1)
    return stage_a, twiddle, stage_b


def pack_kernel(
    samples_hbm, angles_hbm, pointing_hbm, counts_hbm, out_ref,
    samples_ref, angles_ref, pointing_ref, counts_ref, sems,
):
    copies = [
        pltpu.make_async_copy(source, target, sems.at[i])
        for i, (source, target) in enumerate(
            (
                (samples_hbm, samples_ref),
                (angles_hbm, angles_ref),
                (pointing_hbm, pointing_ref),
                (counts_hbm, counts_ref),
            )
        )
    ]
    for copy in copies:
        copy.start()
    for copy in copies:
        copy.wait()
    tiles = samples_ref.shape[0]
    halves = samples_ref.shape[1] // LANES
    lines = 3 * halves + 1
    for h in range(halves):
        cut = slice(h * LANES, (h + 1) * LANES)
        out_ref[pl.ds(h, tiles, stride=lines), :] = samples_ref[:, cut]
        out_ref[pl.ds(halves + h, tiles, stride=lines), :] = angles_ref[:, cut]
        out_ref[pl.ds(2 * halves + h, tiles, stride=lines), :] = pointing_ref[:, cut].astype(
            jnp.float32
        )
    count = counts_ref[...].astype(jnp.float32)
    row = lax.broadcasted_iota(jnp.int32, (tiles, tiles), 0)
    col = lax.broadcasted_iota(jnp.int32, (tiles, tiles), 1)
    column = jnp.sum(jnp.where(row == col, count, 0.0), axis=1, keepdims=True)
    out_ref[pl.ds(3 * halves, tiles, stride=lines), :] = jnp.broadcast_to(column, (tiles, LANES))


def repeated(line, rows):
    tile = jnp.broadcast_to(line, (16, line.shape[1])).astype(jnp.bfloat16)
    return jnp.concatenate([tile] * (rows // 16), axis=0)


def lookup_kernel(
    got_ref, sky_ref, data_ref, signal_ref, cosine_ref, sine_ref, line_ref, column_ref, sums_ref,
    table, high, low,
):
    tiles, cap = data_ref.shape
    halves = cap // LANES
    lines = 3 * halves + 1
    rows = sky_ref.shape[1]
    cycles = 2
    nphi = rows * LANES // cycles

    for c in range(3):
        part = split(sky_ref[c].T)
        table[c * LANES : (c + 1) * LANES, :rows] = part[0]
        table[c * LANES : (c + 1) * LANES, rows:] = part[1]

    def received(field):
        parts = [got_ref[pl.ds(field * halves + h, tiles, stride=lines), :] for h in range(halves)]
        return jnp.concatenate(parts, axis=1)

    data = received(0)
    angle = received(1)
    pixel = received(2).astype(jnp.int32)
    count = got_ref[pl.ds(3 * halves, tiles, stride=lines), :]
    count = jnp.concatenate([count] * halves, axis=1)
    slot = lax.broadcasted_iota(jnp.int32, (tiles, cap), 1).astype(jnp.float32)
    valid = jnp.where(slot < count, 1.0, 0.0)
    cosine = jnp.cos(2.0 * angle)
    sine = jnp.sin(2.0 * angle)
    cosine_ref[...] = cosine
    sine_ref[...] = sine
    cycle = pixel >> bits(nphi)
    row = (pixel >> bits(LANES)) & (nphi // LANES - 1)
    high[...] = (row * cycles + cycle).astype(jnp.float32)
    low[...] = (pixel & (LANES - 1)).astype(jnp.float32)
    second = nphi // LANES
    line_ref[...] = (pixel & (second - 1)).astype(jnp.float32)
    column = cycle * LANES + ((pixel >> bits(second)) & 1) * (LANES // 2) + row
    column_ref[...] = column.astype(jnp.float32)

    iota = lax.broadcasted_iota(jnp.int32, (LANES, cap), 0).astype(jnp.float32)
    iota_half = iota.astype(jnp.bfloat16)
    one = jnp.ones((LANES, cap), jnp.bfloat16)
    zero = jnp.zeros((LANES, cap), jnp.bfloat16)

    def step(index, carry):
        for g in range(GROUP):
            s = index * GROUP + g
            onehot = jnp.where(iota_half == repeated(high[pl.ds(s, 1), :], LANES), one, zero)
            onehot = jnp.concatenate([onehot, onehot], axis=0)
            found = [
                jnp.dot(
                    table[c * LANES : (c + 1) * LANES, :], onehot, preferred_element_type=jnp.float32
                )
                for c in range(3)
            ]
            mask = iota == low[pl.ds(s, 1), :]
            mixed = (
                found[0]
                + found[1] * cosine_ref[pl.ds(s, 1), :]
                + found[2] * sine_ref[pl.ds(s, 1), :]
            )
            signal_ref[pl.ds(s, 1), :] = jnp.sum(
                jnp.where(mask, mixed, 0.0), axis=0, keepdims=True
            )
        return carry

    lax.fori_loop(0, tiles // GROUP, step, 0)

    signal = signal_ref[...]
    masked = valid * signal
    signal_ref[...] = masked
    data_ref[...] = valid * data
    cross = jnp.sum(masked * data, axis=1, keepdims=True)
    square = jnp.sum(masked * signal, axis=1, keepdims=True)
    width = sums_ref.shape[1]
    row = lax.broadcasted_iota(jnp.int32, (tiles, width), 0)
    lane = lax.broadcasted_iota(jnp.int32, (tiles, width), 1)
    lines = jnp.where(lane == row, cross, 0.0) + jnp.where(lane == row + tiles, square, 0.0)
    for cy in range(cycles):
        hits = jnp.sum(jnp.where(cycle == cy, valid, 0.0), axis=1, keepdims=True)
        lines = lines + jnp.where(lane == 2 * tiles + cy, hits * (1.0 / nphi), 0.0)
    line = jnp.sum(lines, axis=0, keepdims=True)
    sums_ref[...] = jnp.broadcast_to(line, sums_ref.shape)


def all_gains(sums_ref, tiles):
    total = jnp.sum(sums_ref[...], axis=0, keepdims=True)
    row = lax.broadcasted_iota(jnp.int32, (tiles, total.shape[1]), 0)
    lane = lax.broadcasted_iota(jnp.int32, (tiles, total.shape[1]), 1)
    cross = jnp.sum(jnp.where(lane == row, total, 0.0), axis=1, keepdims=True)
    square = jnp.sum(jnp.where(lane == row + tiles, total, 0.0), axis=1, keepdims=True)
    return cross / (square + 1e-06)


def bin_kernel(
    sums_ref, data_ref, signal_ref, cosine_ref, sine_ref, line_ref, column_ref,
    stage_a_ref, twiddle_ref, stage_b_ref, maps_ref, send_ref, acc, weights, wide, onehot,
):
    tiles, cap = data_ref.shape
    cycles = 2
    second = twiddle_ref.shape[1]
    first = LANES
    nphi = first * second
    n_tm = lax.axis_size("tm")
    lines = PLANES * cycles
    stride = send_ref.shape[0] // n_tm
    per_band = stride // lines

    gains = all_gains(sums_ref, tiles)
    residual = data_ref[...] - gains * signal_ref[...]
    for c, values in enumerate((residual, residual * cosine_ref[...], residual * sine_ref[...])):
        top = values.astype(jnp.bfloat16).astype(jnp.float32)
        weights[2 * c] = top
        weights[2 * c + 1] = values - top
    acc[...] = jnp.zeros_like(acc)
    iota_high = lax.broadcasted_iota(jnp.int32, (cycles * first, cap), 0)
    iota_high = iota_high.astype(jnp.float32).astype(jnp.bfloat16)
    iota_low = iota_high[:second]
    zero_low = jnp.zeros((second, cap), jnp.bfloat16)
    zero_high = jnp.zeros((cycles * first, cap), jnp.bfloat16)
    one_high = jnp.ones((cycles * first, cap), jnp.bfloat16)

    def step(index, carry):
        for g in range(GROUP):
            s = index * GROUP + g
            cut = slice(g * cap, (g + 1) * cap)
            mask = iota_low == repeated(line_ref[pl.ds(s, 1), :], second)
            for i in range(6):
                wide[i * second : (i + 1) * second, cut] = jnp.where(
                    mask, repeated(weights[i, pl.ds(s, 1), :], second), zero_low
                )
            onehot[:, cut] = jnp.where(
                iota_high == repeated(column_ref[pl.ds(s, 1), :], cycles * first),
                one_high,
                zero_high,
            )
        acc[...] += lax.dot_general(
            wide[...], onehot[...], (((1,), (1,)), ((), ())), preferred_element_type=jnp.float32
        )
        return carry

    lax.fori_loop(0, tiles // GROUP, step, 0)

    blocks = []
    for c in range(3):
        at = 2 * c * second
        map_c = acc[at : at + second, :] + acc[at + second : at + 2 * second, :]
        for cy in range(cycles):
            block = map_c[:, cy * first : (cy + 1) * first]
            blocks.append(block)
            maps_ref[c * second : (c + 1) * second, cy * first : (cy + 1) * first] = block
    field = jnp.concatenate(blocks, axis=0)
    field_high, field_low = split(field)
    modes = jnp.dot(
        jnp.concatenate([field_high, field_low, field_high], axis=1),
        stage_a_ref[...],
        preferred_element_type=jnp.float32,
    )
    turned = []
    for i in range(3 * cycles):
        real = modes[i * second : (i + 1) * second, :first]
        imag = modes[i * second : (i + 1) * second, first:]
        cos_t = twiddle_ref[0]
        sin_t = twiddle_ref[1]
        turned.append(
            jnp.concatenate([real * cos_t - imag * sin_t, real * sin_t + imag * cos_t], axis=0)
        )
    turned = jnp.concatenate(turned, axis=1)
    turned_high, turned_low = split(turned)
    spectrum = jnp.dot(
        stage_b_ref[...],
        jnp.concatenate([turned_high, turned_low, turned_high], axis=0),
        preferred_element_type=jnp.float32,
    )
    half = second // 2
    for c in range(3):
        for cy in range(cycles):
            at = (c * cycles + cy) * first
            for part in range(2):
                for ql in range(per_band):
                    start = part * half + ql * n_tm
                    line = ql * lines + (2 * c + part) * cycles + cy
                    send_ref[pl.ds(line, n_tm, stride=stride), :] = spectrum[
                        start : start + n_tm, at : at + first
                    ]


def report_kernel(maps_ref, sums_ref, binned_ref, gain_ref, weight_ref):
    first = LANES
    cycles = maps_ref.shape[1] // first
    second = maps_ref.shape[0] // 3
    tiles = sums_ref.shape[0]
    for c in range(3):
        for cy in range(cycles):
            flipped = maps_ref[c * second : (c + 1) * second, cy * first : (cy + 1) * first].T
            binned_ref[c, pl.ds(cy, first // 2, stride=cycles), :] = jnp.concatenate(
                [flipped[: first // 2], flipped[first // 2 :]], axis=1
            )
    position = lax.axis_index("det") * lax.axis_size("tm") + lax.axis_index("tm")
    place = lax.broadcasted_iota(jnp.int32, (tiles, 1), 0)
    own = jnp.where(place == position, all_gains(sums_ref, tiles), 0.0)
    gain_ref[...] = jnp.sum(own, axis=0, keepdims=True)
    for cy in range(cycles):
        at = 2 * tiles + cy
        weight_ref[pl.ds(cy, tiles, stride=cycles), :] = jnp.broadcast_to(
            sums_ref[:, at : at + 1], (tiles, LANES)
        )
    weight_ref[tiles * cycles :, :] = jnp.zeros((BLOCK, LANES), jnp.float32)


def rhs_kernel(
    got_ref, sums_ref, prior_ref, noise_ref, draw_ref, rhs_ref, one_ref, two_ref, lines
):
    count = prior_ref.shape[1]
    per_band = prior_ref.shape[2] // LANES
    n_tm = lax.axis_size("tm")
    cycles = count // n_tm
    each = PLANES * cycles
    stride = per_band * each
    order = meeting_order(n_tm)
    tiles = sums_ref.shape[0]
    group = sums_ref[pl.ds(pl.multiple_of(lax.axis_index("det") * n_tm, 8), n_tm), :]
    for cy in range(cycles):
        at = 2 * tiles + cy
        lines[PLANES, pl.ds(cy, n_tm, stride=cycles), :] = jnp.broadcast_to(
            group[:, at : at + 1], (n_tm, LANES)
        )
    root_weight = jnp.sqrt(lines[PLANES])
    for ql in range(per_band):
        cut = slice(ql * LANES, (ql + 1) * LANES)
        for p in range(PLANES):
            for i, t in enumerate(order):
                at = i * stride + ql * each + p * cycles
                lines[p, t * cycles : (t + 1) * cycles, :] = got_ref[at : at + cycles, :]
        for c in range(3):
            root = jnp.sqrt(prior_ref[c, :, cut])
            for p in (2 * c, 2 * c + 1):
                rhs_ref[p, :, cut] = (
                    lines[p] + root_weight * noise_ref[p, :, cut] + root * draw_ref[p, :, cut]
                )
    even = lax.axis_index("det") % 2 == 0
    after = PLANES * HALO
    for p in range(PLANES):
        c = p // 2
        head = rhs_ref[p, :HALO, :]
        tail = rhs_ref[p, count - HALO :, :]
        row = lax.broadcasted_iota(jnp.int32, head.shape, 0)
        head = jnp.where(row == HALO - 1, jnp.sqrt(prior_ref[c, :HALO, :]) * head, head)
        tail = jnp.where(row == HALO - 2, jnp.sqrt(prior_ref[c, count - HALO :, :]) * tail, tail)
        one_ref[p * HALO : (p + 1) * HALO, :] = jnp.where(even, tail, head)
        two_ref[p * HALO : (p + 1) * HALO, :] = jnp.where(even, head, tail)
    for c in range(3):
        head = prior_ref[c, :2, :]
        tail = prior_ref[c, count - 2 :, :]
        one_ref[after + 2 * c : after + 2 * c + 2, :] = jnp.where(even, tail, head)
        two_ref[after + 2 * c : after + 2 * c + 2, :] = jnp.where(even, head, tail)


def krylov_kernel(
    rhs_ref, weights_ref, prior_ref, from_one_ref, from_two_ref, one_ref, two_ref, sums_ref, edge
):
    count = rhs_ref.shape[1]
    rows = count + BLOCK
    band = rhs_ref.shape[2]
    group = lax.axis_index("det")
    even = group % 2 == 0
    has_before = group > 0
    has_after = group < lax.axis_size("det") - 1
    start = pl.multiple_of(group * count, BLOCK)
    before = pl.multiple_of(jnp.maximum(start - BLOCK, 0), BLOCK)
    place = lax.broadcasted_iota(jnp.int32, (BLOCK, LANES), 0)
    beyond = jnp.where(
        place < BLOCK - HALO,
        weights_ref[pl.ds(start + count, BLOCK), :],
        weights_ref[pl.ds(before, BLOCK), :],
    )
    weight = jnp.concatenate([weights_ref[pl.ds(start, count), :], beyond], axis=0)
    weight = jnp.concatenate([weight] * (band // LANES), axis=1)
    sums = [jnp.zeros((count, band), jnp.float32) for _ in range(6)]

    def arrived(at, size):
        one, two = from_one_ref[at : at + size, :], from_two_ref[at : at + size, :]
        ahead = jnp.where(has_after, jnp.where(even, one, two), 0.0)
        behind = jnp.where(has_before, jnp.where(even, two, one), 0.0)
        return ahead, behind

    for p in range(PLANES):
        ahead, behind = arrived(p * HALO, HALO)
        edge[p] = jnp.zeros((BLOCK, band), jnp.float32)
        edge[p, :HALO, :] = ahead
        edge[p, BLOCK - 2 :, :] = behind[HALO - 2 :]
    for c in range(3):
        ahead, behind = arrived(PLANES * HALO + 2 * c, 2)
        edge[PLANES + c] = jnp.ones((BLOCK, band), jnp.float32)
        edge[PLANES + c, :2, :] = ahead
        edge[PLANES + c, BLOCK - 1 :, :] = behind[1:]

    for c in range(3):
        precision = jnp.concatenate([prior_ref[c], edge[PLANES + c]], axis=0)
        root = jnp.sqrt(precision)
        diagonal = (precision + weight - SHIFT) * (1.0 / SPREAD)
        beside = root * (COUPLING / SPREAD)

        def apply(field):
            scaled = root * field
            return diagonal * field - beside * (
                pltpu.roll(scaled, 1, 0) + pltpu.roll(scaled, rows - 1, 0)
            )

        for part in range(2):
            p = 2 * c + part
            zero = jnp.concatenate([rhs_ref[p], edge[p]], axis=0)
            one = apply(zero)
            two = apply(one)
            scaled = root * two
            pair = scaled * pltpu.roll(scaled, rows - 1, 0)
            last = diagonal * two * two - (2.0 * COUPLING / SPREAD) * pair
            zero, one, two, last = zero[:count], one[:count], two[:count], last[:count]
            one_ref[p] = one
            two_ref[p] = two
            for i, term in enumerate(
                (zero * zero, zero * one, one * one, one * two, two * two, last)
            ):
                sums[i] = sums[i] + term
    lines = []
    for i in range(6):
        folded = sums[i][:, :LANES]
        for at in range(LANES, band, LANES):
            folded = folded + sums[i][:, at : at + LANES]
        lines.append(jnp.sum(folded, axis=0, keepdims=True))
    column = jnp.sum(jnp.concatenate(lines, axis=0), axis=1, keepdims=True)
    row = lax.broadcasted_iota(jnp.int32, (6, LANES), 0)
    lane = lax.broadcasted_iota(jnp.int32, (6, LANES), 1)
    line = jnp.sum(jnp.where(lane == row, column, 0.0), axis=0, keepdims=True)
    sums_ref[...] = jnp.broadcast_to(line, sums_ref.shape)


def inner(left, right, moments):
    result = 0.0
    for i, a in enumerate(left):
        for j, b in enumerate(right):
            result = result + a * b * moments[i + j]
    return result


def operated(coefficients):
    result = [SHIFT * a for a in coefficients] + [0.0]
    for i, a in enumerate(coefficients):
        result[i + 1] = result[i + 1] + SPREAD * a
    return result


def padded(values, length):
    return list(values) + [0.0] * (length - len(values))


def conjugate_gradient(moments):
    resid = [1.0]
    direction = [1.0]
    solution = [0.0]
    norm_now = moments[0]
    for iteration in range(3):
        image = operated(direction)
        alpha = norm_now / inner(direction, image, moments)
        size = len(direction)
        solution = [a + alpha * b for a, b in zip(padded(solution, size), direction)]
        if iteration == 2:
            break
        resid = [a - alpha * b for a, b in zip(padded(resid, size + 1), image)]
        norm_next = inner(resid, resid, moments)
        beta = norm_next / norm_now
        direction = [a + beta * b for a, b in zip(resid, padded(direction, size + 1))]
        norm_now = norm_next
    return solution


def final_kernel(sums_ref, rhs_ref, one_ref, two_ref, out_ref):
    total = jnp.sum(sums_ref[...], axis=0, keepdims=True)
    moments = [total[:, i : i + 1] for i in range(6)]
    zero_by, one_by, two_by = conjugate_gradient(moments)
    for p in range(PLANES):
        out_ref[p] = zero_by * rhs_ref[p] + one_by * one_ref[p] + two_by * two_ref[p]


def call(kernel, name, outs, scratch=(), in_specs=None, limit=24):
    extra = {} if in_specs is None else {"in_specs": in_specs}
    return pl.pallas_call(
        kernel,
        out_shape=tuple(jax.ShapeDtypeStruct(shape, dtype) for shape, dtype in outs),
        scratch_shapes=list(scratch),
        compiler_params=pltpu.CompilerParams(vmem_limit_bytes=limit * 2**20),
        name=name,
        **extra,
    )


def exchange(values, axes, order=None):
    groups = None if order is None else [order]
    return lax.all_to_all(
        values, axes, split_axis=0, concat_axis=0, tiled=True, axis_index_groups=groups
    )


def per_device(
    samples, pointing, angles, counts, sky_map, prior_precision, omega_noise, omega_prior
):
    f32, i32, bf16 = jnp.float32, jnp.int32, jnp.bfloat16
    tiles, cap = samples.shape[2:]
    n_det, n_tm = lax.axis_size("det"), lax.axis_size("tm")
    devices = n_det * n_tm
    cycles, nphi = sky_map.shape[1:]
    count, band = prior_precision.shape[1:]
    second = nphi // LANES
    everywhere = ("det", "tm")
    pairs = [(i, i ^ 1) for i in range(n_det)]
    others = [(i, (i + 1 if i % 2 else i - 1) % n_det) for i in range(n_det)]

    lines = 3 * cap // LANES + 1
    packed = call(
        pack_kernel,
        "pack",
        [((tiles * lines, LANES), f32)],
        [
            pltpu.VMEM((tiles, cap), f32),
            pltpu.VMEM((tiles, cap), f32),
            pltpu.VMEM((tiles, cap), i32),
            pltpu.VMEM((1, tiles), i32),
            pltpu.SemaphoreType.DMA((4,)),
        ],
        [pl.BlockSpec(memory_space=pltpu.HBM)] * 4,
    )(
        *(
            pltpu.with_memory_space_constraint(values, pltpu.HBM)
            for values in (
                samples.reshape(tiles, cap),
                angles.reshape(tiles, cap),
                pointing.reshape(tiles, cap),
                counts.reshape(1, tiles),
            )
        )
    )[0]
    got = exchange(packed.reshape(tiles, lines * LANES), everywhere).reshape(tiles * lines, LANES)

    sky = sky_map.reshape(3, cycles, second, LANES).transpose(0, 2, 1, 3)
    sky = sky.reshape(3, second * cycles, LANES)
    width = LANES * -(-(2 * tiles + cycles) // LANES)
    data, signal, cosine, sine, line, column, sums = call(
        lookup_kernel,
        "lookup",
        [((tiles, cap), f32)] * 6 + [((devices, width), f32)],
        [
            pltpu.VMEM((3 * LANES, 2 * second * cycles), bf16),
            pltpu.VMEM((tiles, cap), f32),
            pltpu.VMEM((tiles, cap), f32),
        ],
    )(got, sky)
    sums = exchange(sums, everywhere)

    stage_a, twiddle, stage_b = dft_tables(nphi, n_tm)
    maps, send = call(
        bin_kernel,
        "bin",
        [
            ((3 * second, cycles * LANES), f32),
            ((PLANES * cycles * n_tm * band // LANES, LANES), f32),
        ],
        [
            pltpu.VMEM((6 * second, cycles * LANES), f32),
            pltpu.VMEM((6, tiles, cap), f32),
            pltpu.VMEM((6 * second, GROUP * cap), bf16),
            pltpu.VMEM((cycles * LANES, GROUP * cap), bf16),
        ],
    )(sums, data, signal, cosine, sine, line, column, stage_a, twiddle, stage_b)

    got = exchange(send.reshape(n_tm, -1, LANES), "tm", meeting_order(n_tm)).reshape(-1, LANES)
    halo_rows = PLANES * HALO + 3 * 2
    rhs, to_one, to_two = call(
        rhs_kernel,
        "rhs",
        [((PLANES, count, band), f32)] + [((halo_rows, band), f32)] * 2,
        [pltpu.VMEM((PLANES + 1, count, LANES), f32)],
    )(got, sums, prior_precision, omega_noise, omega_prior)
    maps, to_one, to_two = lax.optimization_barrier((maps, to_one, to_two))
    from_one = lax.ppermute(to_one, "det", pairs)
    from_two = lax.ppermute(to_two, "det", others)
    binned, gain, weights = call(
        report_kernel,
        "report",
        [
            ((3, second * cycles, LANES), f32),
            ((1, 1), f32),
            ((tiles * cycles + BLOCK, LANES), f32),
        ],
    )(maps, sums)
    binned = binned.reshape(3, second, cycles, LANES).transpose(0, 2, 1, 3).reshape(3, cycles, nphi)
    binned, rhs = lax.optimization_barrier((binned, rhs))
    one, two, sums = call(
        krylov_kernel,
        "krylov",
        [((PLANES, count, band), f32)] * 2 + [((devices, LANES), f32)],
        [pltpu.VMEM((PLANES + 3, BLOCK, band), f32)],
    )(rhs, weights, prior_precision, from_one, from_two)
    sums = exchange(sums, everywhere)
    solution = call(final_kernel, "final", [((PLANES, count, band), f32)])(sums, rhs, one, two)[0]
    return (gain, binned, solution)


def solution(mesh):
    return jax.shard_map(
        per_device,
        mesh=mesh,
        in_specs=(
            P("det", "tm", None, None),
            P("det", "tm", None, None),
            P("det", "tm", None, None),
            P("det", "tm", None),
            P(None, ("det", "tm"), None),
            P(None, "det", "tm"),
            P(None, "det", "tm"),
            P(None, "det", "tm"),
        ),
        out_specs=(P("det", "tm"), P(None, ("det", "tm"), None), P(None, "det", "tm")),
        check_vma=False,
    )
```

```python
import math

import jax
import jax.numpy as jnp
import ml_dtypes
import numpy as np
from jax import lax
from jax.experimental import pallas as pl
from jax.experimental.pallas import tpu as pltpu
from jax.sharding import PartitionSpec as P

SPREAD = 8.0
COUPLING = 0.45

LANES = 128
GROUP = 32
PLANES = 6
HALO = 3
BLOCK = 8


def split_np(table):
    high = table.astype(ml_dtypes.bfloat16)
    low = (table - high.astype(np.float64)).astype(ml_dtypes.bfloat16)
    return high, low


def bits(power):
    return power.bit_length() - 1


def split(values):
    high = values.astype(jnp.bfloat16)
    low = (values - high.astype(jnp.float32)).astype(jnp.bfloat16)
    return high, low


def meeting_order(n_tm):
    if n_tm == 8:
        return [3, 2, 5, 4, 1, 0, 7, 6]
    return [(i + n_tm // 2 + 1) % n_tm for i in range(n_tm)]


def dft_tables(nphi, n_tm):
    first, second = LANES, nphi // LANES
    half = second // 2
    column = np.arange(first)
    digit = 2 * (column % (first // 2)) + column // (first // 2)
    k = np.arange(first)
    angle = 2.0 * math.pi / first * (np.outer(digit, k) % first)
    stage_a = np.concatenate([np.cos(angle), np.sin(angle)], axis=1)
    high, low = split_np(stage_a)
    stage_a = np.concatenate([high, high, low], axis=0)
    b = np.arange(second)
    angle = 2.0 * math.pi / nphi * (np.outer(b, k) % nphi)
    twiddle = np.stack([np.cos(angle), np.sin(angle)]).astype(np.float32)
    per_band = half // n_tm
    row = np.arange(half)
    q = np.array(meeting_order(n_tm))[row % n_tm] * per_band + row // n_tm
    angle = 2.0 * math.pi / second * (np.outer(q, b) % second)
    cos_b, sin_b = np.cos(angle), np.sin(angle)
    stage_b = np.block([[cos_b, -sin_b], [-sin_b, -cos_b]]) / math.sqrt(nphi)
    high, low = split_np(stage_b)
    stage_b = np.concatenate([high, high, low], axis=1)
    return stage_a, twiddle, stage_b


def pack_kernel(
    samples_hbm, angles_hbm, pointing_hbm, counts_hbm, out_ref,
    samples_ref, angles_ref, pointing_ref, counts_ref, sems,
):
    copies = [
        pltpu.make_async_copy(source, target, sems.at[i])
        for i, (source, target) in enumerate(
            (
                (samples_hbm, samples_ref),
                (angles_hbm, angles_ref),
                (pointing_hbm, pointing_ref),
                (counts_hbm, counts_ref),
            )
        )
    ]
    for copy in copies:
        copy.start()
    for copy in copies:
        copy.wait()
    tiles = samples_ref.shape[0]
    halves = samples_ref.shape[1] // LANES
    lines = 3 * halves + 1
    for h in range(halves):
        cut = slice(h * LANES, (h + 1) * LANES)
        out_ref[pl.ds(h, tiles, stride=lines), :] = samples_ref[:, cut]
        out_ref[pl.ds(halves + h, tiles, stride=lines), :] = angles_ref[:, cut]
        out_ref[pl.ds(2 * halves + h, tiles, stride=lines), :] = pointing_ref[:, cut].astype(
            jnp.float32
        )
    count = counts_ref[...].astype(jnp.float32)
    row = lax.broadcasted_iota(jnp.int32, (tiles, tiles), 0)
    col = lax.broadcasted_iota(jnp.int32, (tiles, tiles), 1)
    column = jnp.sum(jnp.where(row == col, count, 0.0), axis=1, keepdims=True)
    out_ref[pl.ds(3 * halves, tiles, stride=lines), :] = jnp.broadcast_to(column, (tiles, LANES))


def repeated(line, rows):
    tile = jnp.broadcast_to(line, (16, line.shape[1])).astype(jnp.bfloat16)
    return jnp.concatenate([tile] * (rows // 16), axis=0)


def lookup_kernel(
    got_ref, sky_ref, prior_ref, data_ref, signal_ref, cosine_ref, sine_ref, line_ref, column_ref, sums_ref,
    table, high, low,
):
    tiles, cap = data_ref.shape
    halves = cap // LANES
    lines = 3 * halves + 1
    rows = sky_ref.shape[1]
    cycles = 2
    nphi = rows * LANES // cycles

    for c in range(3):
        part = split(sky_ref[c].T)
        table[c * LANES : (c + 1) * LANES, :rows] = part[0]
        table[c * LANES : (c + 1) * LANES, rows:] = part[1]

    def received(field):
        parts = [got_ref[pl.ds(field * halves + h, tiles, stride=lines), :] for h in range(halves)]
        return jnp.concatenate(parts, axis=1)

    data = received(0)
    angle = received(1)
    pixel = received(2).astype(jnp.int32)
    count = got_ref[pl.ds(3 * halves, tiles, stride=lines), :]
    count = jnp.concatenate([count] * halves, axis=1)
    slot = lax.broadcasted_iota(jnp.int32, (tiles, cap), 1).astype(jnp.float32)
    valid = jnp.where(slot < count, 1.0, 0.0)
    cosine = jnp.cos(2.0 * angle)
    sine = jnp.sin(2.0 * angle)
    cosine_ref[...] = cosine
    sine_ref[...] = sine
    cycle = pixel >> bits(nphi)
    row = (pixel >> bits(LANES)) & (nphi // LANES - 1)
    high[...] = (row * cycles + cycle).astype(jnp.float32)
    low[...] = (pixel & (LANES - 1)).astype(jnp.float32)
    second = nphi // LANES
    line_ref[...] = (pixel & (second - 1)).astype(jnp.float32)
    column = cycle * LANES + ((pixel >> bits(second)) & 1) * (LANES // 2) + row
    column_ref[...] = column.astype(jnp.float32)

    iota = lax.broadcasted_iota(jnp.int32, (LANES, cap), 0).astype(jnp.float32)
    iota_half = iota.astype(jnp.bfloat16)
    one = jnp.ones((LANES, cap), jnp.bfloat16)
    zero = jnp.zeros((LANES, cap), jnp.bfloat16)

    def step(index, carry):
        for g in range(GROUP):
            s = index * GROUP + g
            onehot = jnp.where(iota_half == repeated(high[pl.ds(s, 1), :], LANES), one, zero)
            onehot = jnp.concatenate([onehot, onehot], axis=0)
            found = [
                jnp.dot(
                    table[c * LANES : (c + 1) * LANES, :], onehot, preferred_element_type=jnp.float32
                )
                for c in range(3)
            ]
            mask = iota == low[pl.ds(s, 1), :]
            mixed = (
                found[0]
                + found[1] * cosine_ref[pl.ds(s, 1), :]
                + found[2] * sine_ref[pl.ds(s, 1), :]
            )
            signal_ref[pl.ds(s, 1), :] = jnp.sum(
                jnp.where(mask, mixed, 0.0), axis=0, keepdims=True
            )
        return carry

    lax.fori_loop(0, tiles // GROUP, step, 0)

    signal = signal_ref[...]
    masked = valid * signal
    signal_ref[...] = masked
    data_ref[...] = valid * data
    cross = jnp.sum(masked * data, axis=1, keepdims=True)
    square = jnp.sum(masked * signal, axis=1, keepdims=True)
    width = sums_ref.shape[1]
    row = lax.broadcasted_iota(jnp.int32, (tiles, width), 0)
    lane = lax.broadcasted_iota(jnp.int32, (tiles, width), 1)
    lines = jnp.where(lane == row, cross, 0.0) + jnp.where(lane == row + tiles, square, 0.0)
    for cy in range(cycles):
        hits = jnp.sum(jnp.where(cycle == cy, valid, 0.0), axis=1, keepdims=True)
        lines = lines + jnp.where(lane == 2 * tiles + cy, hits * (1.0 / nphi), 0.0)
    line = jnp.sum(lines, axis=0, keepdims=True)
    prior = prior_ref[...]
    lane = lax.broadcasted_iota(jnp.int32, (1, width), 1)
    for i, values in enumerate((prior, prior * prior)):
        folded = jnp.sum(jnp.sum(values, axis=0), axis=0, keepdims=True)
        found = jnp.sum(folded, axis=1, keepdims=True)
        line = jnp.where(lane == 2 * tiles + cycles + i, found, line)
    sums_ref[...] = jnp.broadcast_to(line, sums_ref.shape)


def all_gains(sums_ref, tiles):
    total = jnp.sum(sums_ref[...], axis=0, keepdims=True)
    row = lax.broadcasted_iota(jnp.int32, (tiles, total.shape[1]), 0)
    lane = lax.broadcasted_iota(jnp.int32, (tiles, total.shape[1]), 1)
    cross = jnp.sum(jnp.where(lane == row, total, 0.0), axis=1, keepdims=True)
    square = jnp.sum(jnp.where(lane == row + tiles, total, 0.0), axis=1, keepdims=True)
    return cross / (square + 1e-06)


def bin_kernel(
    sums_ref, data_ref, signal_ref, cosine_ref, sine_ref, line_ref, column_ref,
    stage_a_ref, twiddle_ref, stage_b_ref, maps_ref, send_ref, acc, weights, wide, onehot,
):
    tiles, cap = data_ref.shape
    cycles = 2
    second = twiddle_ref.shape[1]
    first = LANES
    nphi = first * second
    n_tm = lax.axis_size("tm")
    lines = PLANES * cycles
    stride = send_ref.shape[0] // n_tm
    per_band = stride // lines

    gains = all_gains(sums_ref, tiles)
    residual = data_ref[...] - gains * signal_ref[...]
    for c, values in enumerate((residual, residual * cosine_ref[...], residual * sine_ref[...])):
        top = values.astype(jnp.bfloat16).astype(jnp.float32)
        weights[2 * c] = top
        weights[2 * c + 1] = values - top
    acc[...] = jnp.zeros_like(acc)
    iota_high = lax.broadcasted_iota(jnp.int32, (cycles * first, cap), 0)
    iota_high = iota_high.astype(jnp.float32).astype(jnp.bfloat16)
    iota_low = iota_high[:second]
    zero_low = jnp.zeros((second, cap), jnp.bfloat16)
    zero_high = jnp.zeros((cycles * first, cap), jnp.bfloat16)
    one_high = jnp.ones((cycles * first, cap), jnp.bfloat16)

    def step(index, carry):
        for g in range(GROUP):
            s = index * GROUP + g
            cut = slice(g * cap, (g + 1) * cap)
            mask = iota_low == repeated(line_ref[pl.ds(s, 1), :], second)
            for i in range(6):
                wide[i * second : (i + 1) * second, cut] = jnp.where(
                    mask, repeated(weights[i, pl.ds(s, 1), :], second), zero_low
                )
            onehot[:, cut] = jnp.where(
                iota_high == repeated(column_ref[pl.ds(s, 1), :], cycles * first),
                one_high,
                zero_high,
            )
        acc[...] += lax.dot_general(
            wide[...], onehot[...], (((1,), (1,)), ((), ())), preferred_element_type=jnp.float32
        )
        return carry

    lax.fori_loop(0, tiles // GROUP, step, 0)

    blocks = []
    for c in range(3):
        at = 2 * c * second
        map_c = acc[at : at + second, :] + acc[at + second : at + 2 * second, :]
        for cy in range(cycles):
            block = map_c[:, cy * first : (cy + 1) * first]
            blocks.append(block)
            maps_ref[c * second : (c + 1) * second, cy * first : (cy + 1) * first] = block
    field = jnp.concatenate(blocks, axis=0)
    field_high, field_low = split(field)
    modes = jnp.dot(
        jnp.concatenate([field_high, field_low, field_high], axis=1),
        stage_a_ref[...],
        preferred_element_type=jnp.float32,
    )
    turned = []
    for i in range(3 * cycles):
        real = modes[i * second : (i + 1) * second, :first]
        imag = modes[i * second : (i + 1) * second, first:]
        cos_t = twiddle_ref[0]
        sin_t = twiddle_ref[1]
        turned.append(
            jnp.concatenate([real * cos_t - imag * sin_t, real * sin_t + imag * cos_t], axis=0)
        )
    turned = jnp.concatenate(turned, axis=1)
    turned_high, turned_low = split(turned)
    spectrum = jnp.dot(
        stage_b_ref[...],
        jnp.concatenate([turned_high, turned_low, turned_high], axis=0),
        preferred_element_type=jnp.float32,
    )
    half = second // 2
    for c in range(3):
        for cy in range(cycles):
            at = (c * cycles + cy) * first
            for part in range(2):
                for ql in range(per_band):
                    start = part * half + ql * n_tm
                    line = ql * lines + (2 * c + part) * cycles + cy
                    send_ref[pl.ds(line, n_tm, stride=stride), :] = spectrum[
                        start : start + n_tm, at : at + first
                    ]


def report_kernel(maps_ref, sums_ref, binned_ref, gain_ref, weight_ref):
    first = LANES
    cycles = maps_ref.shape[1] // first
    second = maps_ref.shape[0] // 3
    tiles = sums_ref.shape[0]
    for c in range(3):
        for cy in range(cycles):
            flipped = maps_ref[c * second : (c + 1) * second, cy * first : (cy + 1) * first].T
            binned_ref[c, pl.ds(cy, first // 2, stride=cycles), :] = jnp.concatenate(
                [flipped[: first // 2], flipped[first // 2 :]], axis=1
            )
    position = lax.axis_index("det") * lax.axis_size("tm") + lax.axis_index("tm")
    place = lax.broadcasted_iota(jnp.int32, (tiles, 1), 0)
    own = jnp.where(place == position, all_gains(sums_ref, tiles), 0.0)
    gain_ref[...] = jnp.sum(own, axis=0, keepdims=True)
    for cy in range(cycles):
        at = 2 * tiles + cy
        weight_ref[pl.ds(cy, tiles, stride=cycles), :] = jnp.broadcast_to(
            sums_ref[:, at : at + 1], (tiles, LANES)
        )
    weight_ref[tiles * cycles :, :] = jnp.zeros((BLOCK, LANES), jnp.float32)
    at = 2 * tiles
    total = jnp.sum(sums_ref[...], axis=0, keepdims=True)
    hit = jnp.sum(total[:, at : at + cycles], axis=1, keepdims=True) * (1.0 / (tiles * cycles))
    at = at + cycles
    center = total[:, at + 1 : at + 2] / total[:, at : at + 1] + hit
    weight_ref[tiles * cycles + BLOCK - 1 :, :] = jnp.broadcast_to(center, (1, LANES))


def rhs_kernel(
    got_ref, sums_ref, prior_ref, noise_ref, draw_ref, rhs_ref, one_ref, two_ref, lines
):
    count = prior_ref.shape[1]
    per_band = prior_ref.shape[2] // LANES
    n_tm = lax.axis_size("tm")
    cycles = count // n_tm
    each = PLANES * cycles
    stride = per_band * each
    order = meeting_order(n_tm)
    tiles = sums_ref.shape[0]
    group = sums_ref[pl.ds(pl.multiple_of(lax.axis_index("det") * n_tm, 8), n_tm), :]
    for cy in range(cycles):
        at = 2 * tiles + cy
        lines[PLANES, pl.ds(cy, n_tm, stride=cycles), :] = jnp.broadcast_to(
            group[:, at : at + 1], (n_tm, LANES)
        )
    root_weight = jnp.sqrt(lines[PLANES])
    for ql in range(per_band):
        cut = slice(ql * LANES, (ql + 1) * LANES)
        for p in range(PLANES):
            for i, t in enumerate(order):
                at = i * stride + ql * each + p * cycles
                lines[p, t * cycles : (t + 1) * cycles, :] = got_ref[at : at + cycles, :]
        for c in range(3):
            root = jnp.sqrt(prior_ref[c, :, cut])
            for p in (2 * c, 2 * c + 1):
                rhs_ref[p, :, cut] = (
                    lines[p] + root_weight * noise_ref[p, :, cut] + root * draw_ref[p, :, cut]
                )
    even = lax.axis_index("det") % 2 == 0
    after = PLANES * HALO
    for p in range(PLANES):
        c = p // 2
        head = rhs_ref[p, :HALO, :]
        tail = rhs_ref[p, count - HALO :, :]
        row = lax.broadcasted_iota(jnp.int32, head.shape, 0)
        head = jnp.where(row == HALO - 1, jnp.sqrt(prior_ref[c, :HALO, :]) * head, head)
        tail = jnp.where(row == HALO - 2, jnp.sqrt(prior_ref[c, count - HALO :, :]) * tail, tail)
        one_ref[p * HALO : (p + 1) * HALO, :] = jnp.where(even, tail, head)
        two_ref[p * HALO : (p + 1) * HALO, :] = jnp.where(even, head, tail)
    for c in range(3):
        head = prior_ref[c, :2, :]
        tail = prior_ref[c, count - 2 :, :]
        one_ref[after + 2 * c : after + 2 * c + 2, :] = jnp.where(even, tail, head)
        two_ref[after + 2 * c : after + 2 * c + 2, :] = jnp.where(even, head, tail)


def krylov_kernel(
    rhs_ref, weights_ref, prior_ref, from_one_ref, from_two_ref, one_ref, two_ref, sums_ref, edge
):
    count = rhs_ref.shape[1]
    rows = count + BLOCK
    band = rhs_ref.shape[2]
    group = lax.axis_index("det")
    even = group % 2 == 0
    has_before = group > 0
    has_after = group < lax.axis_size("det") - 1
    start = pl.multiple_of(group * count, BLOCK)
    before = pl.multiple_of(jnp.maximum(start - BLOCK, 0), BLOCK)
    place = lax.broadcasted_iota(jnp.int32, (BLOCK, LANES), 0)
    beyond = jnp.where(
        place < BLOCK - HALO,
        weights_ref[pl.ds(start + count, BLOCK), :],
        weights_ref[pl.ds(before, BLOCK), :],
    )
    center = weights_ref[weights_ref.shape[0] - 1 :, :]
    weight = jnp.concatenate([weights_ref[pl.ds(start, count), :], beyond], axis=0) - center
    weight = jnp.concatenate([weight] * (band // LANES), axis=1)
    sums = [jnp.zeros((count, band), jnp.float32) for _ in range(6)]

    def arrived(at, size):
        one, two = from_one_ref[at : at + size, :], from_two_ref[at : at + size, :]
        ahead = jnp.where(has_after, jnp.where(even, one, two), 0.0)
        behind = jnp.where(has_before, jnp.where(even, two, one), 0.0)
        return ahead, behind

    for p in range(PLANES):
        ahead, behind = arrived(p * HALO, HALO)
        edge[p] = jnp.zeros((BLOCK, band), jnp.float32)
        edge[p, :HALO, :] = ahead
        edge[p, BLOCK - 2 :, :] = behind[HALO - 2 :]
    for c in range(3):
        ahead, behind = arrived(PLANES * HALO + 2 * c, 2)
        edge[PLANES + c] = jnp.ones((BLOCK, band), jnp.float32)
        edge[PLANES + c, :2, :] = ahead
        edge[PLANES + c, BLOCK - 1 :, :] = behind[1:]

    for c in range(3):
        precision = jnp.concatenate([prior_ref[c], edge[PLANES + c]], axis=0)
        root = jnp.sqrt(precision)
        diagonal = (precision + weight) * (1.0 / SPREAD)
        beside = root * (COUPLING / SPREAD)

        def apply(field):
            scaled = root * field
            return diagonal * field - beside * (
                pltpu.roll(scaled, 1, 0) + pltpu.roll(scaled, rows - 1, 0)
            )

        for part in range(2):
            p = 2 * c + part
            zero = jnp.concatenate([rhs_ref[p], edge[p]], axis=0)
            one = apply(zero)
            two = apply(one)
            scaled = root * two
            pair = scaled * pltpu.roll(scaled, rows - 1, 0)
            last = diagonal * two * two - (2.0 * COUPLING / SPREAD) * pair
            zero, one, two, last = zero[:count], one[:count], two[:count], last[:count]
            one_ref[p] = one
            two_ref[p] = two
            for i, term in enumerate(
                (zero * zero, zero * one, one * one, one * two, two * two, last)
            ):
                sums[i] = sums[i] + term
    lines = []
    for i in range(6):
        folded = sums[i][:, :LANES]
        for at in range(LANES, band, LANES):
            folded = folded + sums[i][:, at : at + LANES]
        lines.append(jnp.sum(folded, axis=0, keepdims=True))
    column = jnp.sum(jnp.concatenate(lines, axis=0), axis=1, keepdims=True)
    row = lax.broadcasted_iota(jnp.int32, (6, LANES), 0)
    lane = lax.broadcasted_iota(jnp.int32, (6, LANES), 1)
    line = jnp.sum(jnp.where(lane == row, column, 0.0), axis=0, keepdims=True)
    sums_ref[...] = jnp.broadcast_to(line, sums_ref.shape)


def inner(left, right, moments):
    result = 0.0
    for i, a in enumerate(left):
        for j, b in enumerate(right):
            result = result + a * b * moments[i + j]
    return result


def operated(coefficients, center):
    result = [center * a for a in coefficients] + [0.0]
    for i, a in enumerate(coefficients):
        result[i + 1] = result[i + 1] + SPREAD * a
    return result


def padded(values, length):
    return list(values) + [0.0] * (length - len(values))


def conjugate_gradient(moments, center):
    moments = [moment / moments[0] for moment in moments]
    resid = [1.0]
    direction = [1.0]
    solution = [0.0]
    norm_now = moments[0]
    for iteration in range(3):
        image = operated(direction, center)
        alpha = norm_now / inner(direction, image, moments)
        size = len(direction)
        solution = [a + alpha * b for a, b in zip(padded(solution, size), direction)]
        if iteration == 2:
            break
        resid = [a - alpha * b for a, b in zip(padded(resid, size + 1), image)]
        norm_next = inner(resid, resid, moments)
        beta = norm_next / norm_now
        direction = [a + beta * b for a, b in zip(resid, padded(direction, size + 1))]
        norm_now = norm_next
    return solution


def final_kernel(sums_ref, weights_ref, rhs_ref, one_ref, two_ref, out_ref):
    total = jnp.sum(sums_ref[...], axis=0, keepdims=True)
    moments = [total[:, i : i + 1] for i in range(6)]
    center = weights_ref[weights_ref.shape[0] - 1 :, :1]
    zero_by, one_by, two_by = conjugate_gradient(moments, center)
    for p in range(PLANES):
        out_ref[p] = zero_by * rhs_ref[p] + one_by * one_ref[p] + two_by * two_ref[p]


def call(kernel, name, outs, scratch=(), in_specs=None, limit=24):
    extra = {} if in_specs is None else {"in_specs": in_specs}
    return pl.pallas_call(
        kernel,
        out_shape=tuple(jax.ShapeDtypeStruct(shape, dtype) for shape, dtype in outs),
        scratch_shapes=list(scratch),
        compiler_params=pltpu.CompilerParams(vmem_limit_bytes=limit * 2**20),
        name=name,
        **extra,
    )


def exchange(values, axes, order=None):
    groups = None if order is None else [order]
    return lax.all_to_all(
        values, axes, split_axis=0, concat_axis=0, tiled=True, axis_index_groups=groups
    )


def per_device(
    samples, pointing, angles, counts, sky_map, prior_precision, omega_noise, omega_prior
):
    f32, i32, bf16 = jnp.float32, jnp.int32, jnp.bfloat16
    tiles, cap = samples.shape[2:]
    n_det, n_tm = lax.axis_size("det"), lax.axis_size("tm")
    devices = n_det * n_tm
    cycles, nphi = sky_map.shape[1:]
    count, band = prior_precision.shape[1:]
    second = nphi // LANES
    everywhere = ("det", "tm")
    pairs = [(i, i ^ 1) for i in range(n_det)]
    others = [(i, (i + 1 if i % 2 else i - 1) % n_det) for i in range(n_det)]

    lines = 3 * cap // LANES + 1
    packed = call(
        pack_kernel,
        "pack",
        [((tiles * lines, LANES), f32)],
        [
            pltpu.VMEM((tiles, cap), f32),
            pltpu.VMEM((tiles, cap), f32),
            pltpu.VMEM((tiles, cap), i32),
            pltpu.VMEM((1, tiles), i32),
            pltpu.SemaphoreType.DMA((4,)),
        ],
        [pl.BlockSpec(memory_space=pltpu.HBM)] * 4,
    )(
        *(
            pltpu.with_memory_space_constraint(values, pltpu.HBM)
            for values in (
                samples.reshape(tiles, cap),
                angles.reshape(tiles, cap),
                pointing.reshape(tiles, cap),
                counts.reshape(1, tiles),
            )
        )
    )[0]
    got = exchange(packed.reshape(tiles, lines * LANES), everywhere).reshape(tiles * lines, LANES)

    sky = sky_map.reshape(3, cycles, second, LANES).transpose(0, 2, 1, 3)
    sky = sky.reshape(3, second * cycles, LANES)
    width = LANES * -(-(2 * tiles + cycles + 2) // LANES)
    data, signal, cosine, sine, line, column, sums = call(
        lookup_kernel,
        "lookup",
        [((tiles, cap), f32)] * 6 + [((devices, width), f32)],
        [
            pltpu.VMEM((3 * LANES, 2 * second * cycles), bf16),
            pltpu.VMEM((tiles, cap), f32),
            pltpu.VMEM((tiles, cap), f32),
        ],
    )(got, sky, prior_precision)
    sums = exchange(sums, everywhere)

    stage_a, twiddle, stage_b = dft_tables(nphi, n_tm)
    maps, send = call(
        bin_kernel,
        "bin",
        [
            ((3 * second, cycles * LANES), f32),
            ((PLANES * cycles * n_tm * band // LANES, LANES), f32),
        ],
        [
            pltpu.VMEM((6 * second, cycles * LANES), f32),
            pltpu.VMEM((6, tiles, cap), f32),
            pltpu.VMEM((6 * second, GROUP * cap), bf16),
            pltpu.VMEM((cycles * LANES, GROUP * cap), bf16),
        ],
    )(sums, data, signal, cosine, sine, line, column, stage_a, twiddle, stage_b)

    got = exchange(send.reshape(n_tm, -1, LANES), "tm", meeting_order(n_tm)).reshape(-1, LANES)
    halo_rows = PLANES * HALO + 3 * 2
    rhs, to_one, to_two = call(
        rhs_kernel,
        "rhs",
        [((PLANES, count, band), f32)] + [((halo_rows, band), f32)] * 2,
        [pltpu.VMEM((PLANES + 1, count, LANES), f32)],
    )(got, sums, prior_precision, omega_noise, omega_prior)
    maps, to_one, to_two = lax.optimization_barrier((maps, to_one, to_two))
    from_one = lax.ppermute(to_one, "det", pairs)
    from_two = lax.ppermute(to_two, "det", others)
    binned, gain, weights = call(
        report_kernel,
        "report",
        [
            ((3, second * cycles, LANES), f32),
            ((1, 1), f32),
            ((tiles * cycles + BLOCK, LANES), f32),
        ],
    )(maps, sums)
    binned = binned.reshape(3, second, cycles, LANES).transpose(0, 2, 1, 3).reshape(3, cycles, nphi)
    binned, rhs = lax.optimization_barrier((binned, rhs))
    one, two, sums = call(
        krylov_kernel,
        "krylov",
        [((PLANES, count, band), f32)] * 2 + [((devices, LANES), f32)],
        [pltpu.VMEM((PLANES + 3, BLOCK, band), f32)],
    )(rhs, weights, prior_precision, from_one, from_two)
    sums = exchange(sums, everywhere)
    solution = call(final_kernel, "final", [((PLANES, count, band), f32)])(
        sums, weights, rhs, one, two
    )[0]
    return (gain, binned, solution)


def solution(mesh):
    return jax.shard_map(
        per_device,
        mesh=mesh,
        in_specs=(
            P("det", "tm", None, None),
            P("det", "tm", None, None),
            P("det", "tm", None, None),
            P("det", "tm", None),
            P(None, ("det", "tm"), None),
            P(None, "det", "tm"),
            P(None, "det", "tm"),
            P(None, "det", "tm"),
        ),
        out_specs=(P("det", "tm"), P(None, ("det", "tm"), None), P(None, "det", "tm")),
        check_vma=False,
    )
```

```python
import math

import jax
import jax.numpy as jnp
import ml_dtypes
import numpy as np
from jax import lax
from jax.experimental import pallas as pl
from jax.experimental.pallas import tpu as pltpu
from jax.sharding import PartitionSpec as P

SPREAD = 8.0
COUPLING = 0.45

LANES = 128
GROUP = 32
PLANES = 6
HALO = 3
BLOCK = 8


def split_np(table):
    high = table.astype(ml_dtypes.bfloat16)
    low = (table - high.astype(np.float64)).astype(ml_dtypes.bfloat16)
    return high, low


def bits(power):
    return power.bit_length() - 1


def split(values):
    high = values.astype(jnp.bfloat16)
    low = (values - high.astype(jnp.float32)).astype(jnp.bfloat16)
    return high, low


def meeting_order(n_tm):
    if n_tm == 8:
        return [3, 2, 7, 5, 1, 0, 4, 6]
    return [(i + n_tm // 2 + 1) % n_tm for i in range(n_tm)]


def dft_tables(nphi, n_tm):
    first, second = LANES, nphi // LANES
    half = second // 2
    column = np.arange(first)
    digit = 2 * (column % (first // 2)) + column // (first // 2)
    k = np.arange(first)
    angle = 2.0 * math.pi / first * (np.outer(digit, k) % first)
    stage_a = np.concatenate([np.cos(angle), np.sin(angle)], axis=1)
    high, low = split_np(stage_a)
    stage_a = np.concatenate([high, high, low], axis=0)
    b = np.arange(second)
    angle = 2.0 * math.pi / nphi * (np.outer(b, k) % nphi)
    twiddle = np.stack([np.cos(angle), np.sin(angle)]).astype(np.float32)
    per_band = half // n_tm
    row = np.arange(half)
    q = np.array(meeting_order(n_tm))[row % n_tm] * per_band + row // n_tm
    angle = 2.0 * math.pi / second * (np.outer(q, b) % second)
    cos_b, sin_b = np.cos(angle), np.sin(angle)
    stage_b = np.block([[cos_b, -sin_b], [-sin_b, -cos_b]]) / math.sqrt(nphi)
    high, low = split_np(stage_b)
    stage_b = np.concatenate([high, high, low], axis=1)
    return stage_a, twiddle, stage_b


def pack_kernel(
    samples_hbm, angles_hbm, pointing_hbm, counts_hbm, out_ref,
    samples_ref, angles_ref, pointing_ref, counts_ref, sems,
):
    copies = [
        pltpu.make_async_copy(source, target, sems.at[i])
        for i, (source, target) in enumerate(
            (
                (samples_hbm, samples_ref),
                (angles_hbm, angles_ref),
                (pointing_hbm, pointing_ref),
                (counts_hbm, counts_ref),
            )
        )
    ]
    for copy in copies:
        copy.start()
    tiles = samples_ref.shape[0]
    halves = samples_ref.shape[1] // LANES
    lines = 3 * halves + 1
    for field, source in enumerate((samples_ref, angles_ref, pointing_ref)):
        copies[field].wait()
        for h in range(halves):
            out_ref[pl.ds(field * halves + h, tiles, stride=lines), :] = source[
                :, h * LANES : (h + 1) * LANES
            ].astype(jnp.float32)
    copies[3].wait()
    count = counts_ref[...].astype(jnp.float32)
    row = lax.broadcasted_iota(jnp.int32, (tiles, tiles), 0)
    col = lax.broadcasted_iota(jnp.int32, (tiles, tiles), 1)
    column = jnp.sum(jnp.where(row == col, count, 0.0), axis=1, keepdims=True)
    out_ref[pl.ds(3 * halves, tiles, stride=lines), :] = jnp.broadcast_to(column, (tiles, LANES))


def repeated(line, rows):
    tile = jnp.broadcast_to(line, (16, line.shape[1])).astype(jnp.bfloat16)
    return jnp.concatenate([tile] * (rows // 16), axis=0)


def lookup_kernel(
    got_ref, sky_ref, prior_ref, data_ref, signal_ref, cosine_ref, sine_ref, line_ref, column_ref, sums_ref,
    table, high, low,
):
    tiles, cap = data_ref.shape
    halves = cap // LANES
    lines = 3 * halves + 1
    rows = sky_ref.shape[1]
    cycles = 2
    nphi = rows * LANES // cycles

    for c in range(3):
        part = split(sky_ref[c].T)
        table[c * LANES : (c + 1) * LANES, :rows] = part[0]
        table[c * LANES : (c + 1) * LANES, rows:] = part[1]

    def received(field):
        parts = [got_ref[pl.ds(field * halves + h, tiles, stride=lines), :] for h in range(halves)]
        return jnp.concatenate(parts, axis=1)

    data = received(0)
    angle = received(1)
    pixel = received(2).astype(jnp.int32)
    count = got_ref[pl.ds(3 * halves, tiles, stride=lines), :]
    count = jnp.concatenate([count] * halves, axis=1)
    slot = lax.broadcasted_iota(jnp.int32, (tiles, cap), 1).astype(jnp.float32)
    valid = jnp.where(slot < count, 1.0, 0.0)
    cosine = jnp.cos(2.0 * angle)
    sine = jnp.sin(2.0 * angle)
    cosine_ref[...] = cosine
    sine_ref[...] = sine
    cycle = pixel >> bits(nphi)
    row = (pixel >> bits(LANES)) & (nphi // LANES - 1)
    high[...] = (row * cycles + cycle).astype(jnp.float32)
    low[...] = (pixel & (LANES - 1)).astype(jnp.float32)
    second = nphi // LANES
    line_ref[...] = (pixel & (second - 1)).astype(jnp.float32)
    column = cycle * LANES + ((pixel >> bits(second)) & 1) * (LANES // 2) + row
    column_ref[...] = column.astype(jnp.float32)

    iota = lax.broadcasted_iota(jnp.int32, (LANES, cap), 0).astype(jnp.float32)
    iota_half = iota.astype(jnp.bfloat16)
    one = jnp.ones((LANES, cap), jnp.bfloat16)
    zero = jnp.zeros((LANES, cap), jnp.bfloat16)

    def step(index, carry):
        for g in range(GROUP):
            s = index * GROUP + g
            onehot = jnp.where(iota_half == repeated(high[pl.ds(s, 1), :], LANES), one, zero)
            onehot = jnp.concatenate([onehot, onehot], axis=0)
            found = [
                jnp.dot(
                    table[c * LANES : (c + 1) * LANES, :], onehot, preferred_element_type=jnp.float32
                )
                for c in range(3)
            ]
            mask = iota == low[pl.ds(s, 1), :]
            mixed = (
                found[0]
                + found[1] * cosine_ref[pl.ds(s, 1), :]
                + found[2] * sine_ref[pl.ds(s, 1), :]
            )
            signal_ref[pl.ds(s, 1), :] = jnp.sum(
                jnp.where(mask, mixed, 0.0), axis=0, keepdims=True
            )
        return carry

    lax.fori_loop(0, tiles // GROUP, step, 0)

    signal = signal_ref[...]
    masked = valid * signal
    signal_ref[...] = masked
    data_ref[...] = valid * data
    cross = jnp.sum(masked * data, axis=1, keepdims=True)
    square = jnp.sum(masked * signal, axis=1, keepdims=True)
    width = sums_ref.shape[1]
    row = lax.broadcasted_iota(jnp.int32, (tiles, width), 0)
    lane = lax.broadcasted_iota(jnp.int32, (tiles, width), 1)
    lines = jnp.where(lane == row, cross, 0.0) + jnp.where(lane == row + tiles, square, 0.0)
    for cy in range(cycles):
        hits = jnp.sum(jnp.where(cycle == cy, valid, 0.0), axis=1, keepdims=True)
        lines = lines + jnp.where(lane == 2 * tiles + cy, hits * (1.0 / nphi), 0.0)
    line = jnp.sum(lines, axis=0, keepdims=True)
    prior = prior_ref[...]
    lane = lax.broadcasted_iota(jnp.int32, (1, width), 1)
    for i, values in enumerate((prior, prior * prior)):
        folded = jnp.sum(jnp.sum(values, axis=0), axis=0, keepdims=True)
        found = jnp.sum(folded, axis=1, keepdims=True)
        line = jnp.where(lane == 2 * tiles + cycles + i, found, line)
    sums_ref[...] = jnp.broadcast_to(line, sums_ref.shape)


def all_gains(sums_ref, tiles):
    total = jnp.sum(sums_ref[...], axis=0, keepdims=True)
    row = lax.broadcasted_iota(jnp.int32, (tiles, total.shape[1]), 0)
    lane = lax.broadcasted_iota(jnp.int32, (tiles, total.shape[1]), 1)
    cross = jnp.sum(jnp.where(lane == row, total, 0.0), axis=1, keepdims=True)
    square = jnp.sum(jnp.where(lane == row + tiles, total, 0.0), axis=1, keepdims=True)
    return cross / (square + 1e-06)


def bin_kernel(
    sums_ref, data_ref, signal_ref, cosine_ref, sine_ref, line_ref, column_ref,
    stage_a_ref, twiddle_ref, stage_b_ref, maps_ref, send_ref, acc, weights, wide, onehot,
):
    tiles, cap = data_ref.shape
    cycles = 2
    second = twiddle_ref.shape[1]
    first = LANES
    nphi = first * second
    n_tm = lax.axis_size("tm")
    lines = PLANES * cycles
    stride = send_ref.shape[0] // n_tm
    per_band = stride // lines

    gains = all_gains(sums_ref, tiles)
    residual = data_ref[...] - gains * signal_ref[...]
    for c, values in enumerate((residual, residual * cosine_ref[...], residual * sine_ref[...])):
        top = values.astype(jnp.bfloat16).astype(jnp.float32)
        weights[2 * c] = top
        weights[2 * c + 1] = values - top
    acc[...] = jnp.zeros_like(acc)
    iota_high = lax.broadcasted_iota(jnp.int32, (cycles * first, cap), 0)
    iota_high = iota_high.astype(jnp.float32).astype(jnp.bfloat16)
    iota_low = iota_high[:second]
    zero_low = jnp.zeros((second, cap), jnp.bfloat16)
    zero_high = jnp.zeros((cycles * first, cap), jnp.bfloat16)
    one_high = jnp.ones((cycles * first, cap), jnp.bfloat16)

    def step(index, carry):
        for g in range(GROUP):
            s = index * GROUP + g
            cut = slice(g * cap, (g + 1) * cap)
            mask = iota_low == repeated(line_ref[pl.ds(s, 1), :], second)
            for i in range(6):
                wide[i * second : (i + 1) * second, cut] = jnp.where(
                    mask, repeated(weights[i, pl.ds(s, 1), :], second), zero_low
                )
            onehot[:, cut] = jnp.where(
                iota_high == repeated(column_ref[pl.ds(s, 1), :], cycles * first),
                one_high,
                zero_high,
            )
        acc[...] += lax.dot_general(
            wide[...], onehot[...], (((1,), (1,)), ((), ())), preferred_element_type=jnp.float32
        )
        return carry

    lax.fori_loop(0, tiles // GROUP, step, 0)

    blocks = []
    for c in range(3):
        at = 2 * c * second
        map_c = acc[at : at + second, :] + acc[at + second : at + 2 * second, :]
        for cy in range(cycles):
            block = map_c[:, cy * first : (cy + 1) * first]
            blocks.append(block)
            maps_ref[c * second : (c + 1) * second, cy * first : (cy + 1) * first] = block
    field = jnp.concatenate(blocks, axis=0)
    field_high, field_low = split(field)
    modes = jnp.dot(
        jnp.concatenate([field_high, field_low, field_high], axis=1),
        stage_a_ref[...],
        preferred_element_type=jnp.float32,
    )
    turned = []
    for i in range(3 * cycles):
        real = modes[i * second : (i + 1) * second, :first]
        imag = modes[i * second : (i + 1) * second, first:]
        cos_t = twiddle_ref[0]
        sin_t = twiddle_ref[1]
        turned.append(
            jnp.concatenate([real * cos_t - imag * sin_t, real * sin_t + imag * cos_t], axis=0)
        )
    turned = jnp.concatenate(turned, axis=1)
    turned_high, turned_low = split(turned)
    spectrum = jnp.dot(
        stage_b_ref[...],
        jnp.concatenate([turned_high, turned_low, turned_high], axis=0),
        preferred_element_type=jnp.float32,
    )
    half = second // 2
    for c in range(3):
        for cy in range(cycles):
            at = (c * cycles + cy) * first
            for part in range(2):
                for ql in range(per_band):
                    start = part * half + ql * n_tm
                    line = ql * lines + (2 * c + part) * cycles + cy
                    send_ref[pl.ds(line, n_tm, stride=stride), :] = spectrum[
                        start : start + n_tm, at : at + first
                    ]


def report_kernel(maps_ref, sums_ref, binned_ref, gain_ref, weight_ref):
    first = LANES
    cycles = maps_ref.shape[1] // first
    second = maps_ref.shape[0] // 3
    tiles = sums_ref.shape[0]
    for c in range(3):
        for cy in range(cycles):
            flipped = maps_ref[c * second : (c + 1) * second, cy * first : (cy + 1) * first].T
            binned_ref[c, pl.ds(cy, first // 2, stride=cycles), :] = jnp.concatenate(
                [flipped[: first // 2], flipped[first // 2 :]], axis=1
            )
    position = lax.axis_index("det") * lax.axis_size("tm") + lax.axis_index("tm")
    place = lax.broadcasted_iota(jnp.int32, (tiles, 1), 0)
    own = jnp.where(place == position, all_gains(sums_ref, tiles), 0.0)
    gain_ref[...] = jnp.sum(own, axis=0, keepdims=True)
    for cy in range(cycles):
        at = 2 * tiles + cy
        weight_ref[pl.ds(cy, tiles, stride=cycles), :] = jnp.broadcast_to(
            sums_ref[:, at : at + 1], (tiles, LANES)
        )
    weight_ref[tiles * cycles :, :] = jnp.zeros((BLOCK, LANES), jnp.float32)
    at = 2 * tiles
    total = jnp.sum(sums_ref[...], axis=0, keepdims=True)
    hit = jnp.sum(total[:, at : at + cycles], axis=1, keepdims=True) * (1.0 / (tiles * cycles))
    at = at + cycles
    center = total[:, at + 1 : at + 2] / total[:, at : at + 1] + hit
    weight_ref[tiles * cycles + BLOCK - 1 :, :] = jnp.broadcast_to(center, (1, LANES))


def rhs_kernel(
    got_ref, sums_ref, prior_ref, noise_ref, draw_ref, rhs_ref, one_ref, two_ref, lines
):
    count = prior_ref.shape[1]
    per_band = prior_ref.shape[2] // LANES
    n_tm = lax.axis_size("tm")
    cycles = count // n_tm
    each = PLANES * cycles
    stride = per_band * each
    order = meeting_order(n_tm)
    tiles = sums_ref.shape[0]
    group = sums_ref[pl.ds(pl.multiple_of(lax.axis_index("det") * n_tm, 8), n_tm), :]
    for cy in range(cycles):
        at = 2 * tiles + cy
        lines[PLANES, pl.ds(cy, n_tm, stride=cycles), :] = jnp.broadcast_to(
            group[:, at : at + 1], (n_tm, LANES)
        )
    root_weight = jnp.sqrt(lines[PLANES])
    for ql in range(per_band):
        cut = slice(ql * LANES, (ql + 1) * LANES)
        for p in range(PLANES):
            for i, t in enumerate(order):
                at = i * stride + ql * each + p * cycles
                lines[p, t * cycles : (t + 1) * cycles, :] = got_ref[at : at + cycles, :]
        for c in range(3):
            root = jnp.sqrt(prior_ref[c, :, cut])
            for p in (2 * c, 2 * c + 1):
                rhs_ref[p, :, cut] = (
                    lines[p] + root_weight * noise_ref[p, :, cut] + root * draw_ref[p, :, cut]
                )
    even = lax.axis_index("det") % 2 == 0
    after = PLANES * HALO
    for p in range(PLANES):
        c = p // 2
        head = rhs_ref[p, :HALO, :]
        tail = rhs_ref[p, count - HALO :, :]
        row = lax.broadcasted_iota(jnp.int32, head.shape, 0)
        head = jnp.where(row == HALO - 1, jnp.sqrt(prior_ref[c, :HALO, :]) * head, head)
        tail = jnp.where(row == HALO - 2, jnp.sqrt(prior_ref[c, count - HALO :, :]) * tail, tail)
        one_ref[p * HALO : (p + 1) * HALO, :] = jnp.where(even, tail, head)
        two_ref[p * HALO : (p + 1) * HALO, :] = jnp.where(even, head, tail)
    for c in range(3):
        head = prior_ref[c, :2, :]
        tail = prior_ref[c, count - 2 :, :]
        one_ref[after + 2 * c : after + 2 * c + 2, :] = jnp.where(even, tail, head)
        two_ref[after + 2 * c : after + 2 * c + 2, :] = jnp.where(even, head, tail)


def krylov_kernel(
    rhs_ref, weights_ref, prior_ref, from_one_ref, from_two_ref, one_ref, two_ref, sums_ref, edge
):
    count = rhs_ref.shape[1]
    rows = count + BLOCK
    band = rhs_ref.shape[2]
    group = lax.axis_index("det")
    even = group % 2 == 0
    has_before = group > 0
    has_after = group < lax.axis_size("det") - 1
    start = pl.multiple_of(group * count, BLOCK)
    before = pl.multiple_of(jnp.maximum(start - BLOCK, 0), BLOCK)
    place = lax.broadcasted_iota(jnp.int32, (BLOCK, LANES), 0)
    beyond = jnp.where(
        place < BLOCK - HALO,
        weights_ref[pl.ds(start + count, BLOCK), :],
        weights_ref[pl.ds(before, BLOCK), :],
    )
    center = weights_ref[weights_ref.shape[0] - 1 :, :]
    weight = jnp.concatenate([weights_ref[pl.ds(start, count), :], beyond], axis=0) - center
    weight = jnp.concatenate([weight] * (band // LANES), axis=1)
    sums = [jnp.zeros((count, band), jnp.float32) for _ in range(6)]

    def arrived(at, size):
        one, two = from_one_ref[at : at + size, :], from_two_ref[at : at + size, :]
        ahead = jnp.where(has_after, jnp.where(even, one, two), 0.0)
        behind = jnp.where(has_before, jnp.where(even, two, one), 0.0)
        return ahead, behind

    for p in range(PLANES):
        ahead, behind = arrived(p * HALO, HALO)
        edge[p] = jnp.zeros((BLOCK, band), jnp.float32)
        edge[p, :HALO, :] = ahead
        edge[p, BLOCK - 2 :, :] = behind[HALO - 2 :]
    for c in range(3):
        ahead, behind = arrived(PLANES * HALO + 2 * c, 2)
        edge[PLANES + c] = jnp.ones((BLOCK, band), jnp.float32)
        edge[PLANES + c, :2, :] = ahead
        edge[PLANES + c, BLOCK - 1 :, :] = behind[1:]

    for c in range(3):
        precision = jnp.concatenate([prior_ref[c], edge[PLANES + c]], axis=0)
        root = jnp.sqrt(precision)
        diagonal = (precision + weight) * (1.0 / SPREAD)
        beside = root * (COUPLING / SPREAD)

        def apply(field):
            scaled = root * field
            return diagonal * field - beside * (
                pltpu.roll(scaled, 1, 0) + pltpu.roll(scaled, rows - 1, 0)
            )

        for part in range(2):
            p = 2 * c + part
            zero = jnp.concatenate([rhs_ref[p], edge[p]], axis=0)
            one = apply(zero)
            two = apply(one)
            scaled = root * two
            pair = scaled * pltpu.roll(scaled, rows - 1, 0)
            last = diagonal * two * two - (2.0 * COUPLING / SPREAD) * pair
            zero, one, two, last = zero[:count], one[:count], two[:count], last[:count]
            one_ref[p] = one
            two_ref[p] = two
            for i, term in enumerate(
                (zero * zero, zero * one, one * one, one * two, two * two, last)
            ):
                sums[i] = sums[i] + term
    lines = []
    for i in range(6):
        folded = sums[i][:, :LANES]
        for at in range(LANES, band, LANES):
            folded = folded + sums[i][:, at : at + LANES]
        lines.append(jnp.sum(folded, axis=0, keepdims=True))
    column = jnp.sum(jnp.concatenate(lines, axis=0), axis=1, keepdims=True)
    row = lax.broadcasted_iota(jnp.int32, (6, LANES), 0)
    lane = lax.broadcasted_iota(jnp.int32, (6, LANES), 1)
    line = jnp.sum(jnp.where(lane == row, column, 0.0), axis=0, keepdims=True)
    sums_ref[...] = jnp.broadcast_to(line, sums_ref.shape)


def inner(left, right, moments):
    result = 0.0
    for i, a in enumerate(left):
        for j, b in enumerate(right):
            result = result + a * b * moments[i + j]
    return result


def operated(coefficients, center):
    result = [center * a for a in coefficients] + [0.0]
    for i, a in enumerate(coefficients):
        result[i + 1] = result[i + 1] + SPREAD * a
    return result


def padded(values, length):
    return list(values) + [0.0] * (length - len(values))


def conjugate_gradient(moments, center):
    inverse = 1.0 / moments[0]
    moments = [1.0] + [moment * inverse for moment in moments[1:]]
    resid = [1.0]
    direction = [1.0]
    solution = [0.0]
    norm_now = moments[0]
    for iteration in range(3):
        image = operated(direction, center)
        alpha = norm_now / inner(direction, image, moments)
        size = len(direction)
        solution = [a + alpha * b for a, b in zip(padded(solution, size), direction)]
        if iteration == 2:
            break
        resid = [a - alpha * b for a, b in zip(padded(resid, size + 1), image)]
        norm_next = inner(resid, resid, moments)
        beta = norm_next / norm_now
        direction = [a + beta * b for a, b in zip(resid, padded(direction, size + 1))]
        norm_now = norm_next
    return solution


def final_kernel(sums_ref, weights_ref, rhs_ref, one_ref, two_ref, out_ref):
    total = jnp.sum(sums_ref[...], axis=0, keepdims=True)
    moments = [total[:, i : i + 1] for i in range(6)]
    center = weights_ref[weights_ref.shape[0] - 1 :, :1]
    zero_by, one_by, two_by = conjugate_gradient(moments, center)
    for p in range(PLANES):
        out_ref[p] = zero_by * rhs_ref[p] + one_by * one_ref[p] + two_by * two_ref[p]


def call(kernel, name, outs, scratch=(), in_specs=None, limit=24):
    extra = {} if in_specs is None else {"in_specs": in_specs}
    return pl.pallas_call(
        kernel,
        out_shape=tuple(jax.ShapeDtypeStruct(shape, dtype) for shape, dtype in outs),
        scratch_shapes=list(scratch),
        compiler_params=pltpu.CompilerParams(vmem_limit_bytes=limit * 2**20),
        name=name,
        **extra,
    )


def exchange(values, axes, order=None):
    groups = None if order is None else [order]
    return lax.all_to_all(
        values, axes, split_axis=0, concat_axis=0, tiled=True, axis_index_groups=groups
    )


def per_device(
    samples, pointing, angles, counts, sky_map, prior_precision, omega_noise, omega_prior
):
    f32, i32, bf16 = jnp.float32, jnp.int32, jnp.bfloat16
    tiles, cap = samples.shape[2:]
    n_det, n_tm = lax.axis_size("det"), lax.axis_size("tm")
    devices = n_det * n_tm
    cycles, nphi = sky_map.shape[1:]
    count, band = prior_precision.shape[1:]
    second = nphi // LANES
    everywhere = ("det", "tm")
    pairs = [(i, i ^ 1) for i in range(n_det)]
    others = [(i, (i + 1 if i % 2 else i - 1) % n_det) for i in range(n_det)]

    lines = 3 * cap // LANES + 1
    packed = call(
        pack_kernel,
        "pack",
        [((tiles * lines, LANES), f32)],
        [
            pltpu.VMEM((tiles, cap), f32),
            pltpu.VMEM((tiles, cap), f32),
            pltpu.VMEM((tiles, cap), i32),
            pltpu.VMEM((1, tiles), i32),
            pltpu.SemaphoreType.DMA((4,)),
        ],
        [pl.BlockSpec(memory_space=pltpu.HBM)] * 4,
    )(
        *(
            pltpu.with_memory_space_constraint(values, pltpu.HBM)
            for values in (
                samples.reshape(tiles, cap),
                angles.reshape(tiles, cap),
                pointing.reshape(tiles, cap),
                counts.reshape(1, tiles),
            )
        )
    )[0]
    got = exchange(packed.reshape(tiles, lines * LANES), everywhere).reshape(tiles * lines, LANES)

    sky = sky_map.reshape(3, cycles, second, LANES).transpose(0, 2, 1, 3)
    sky = sky.reshape(3, second * cycles, LANES)
    width = LANES * -(-(2 * tiles + cycles + 2) // LANES)
    data, signal, cosine, sine, line, column, sums = call(
        lookup_kernel,
        "lookup",
        [((tiles, cap), f32)] * 6 + [((devices, width), f32)],
        [
            pltpu.VMEM((3 * LANES, 2 * second * cycles), bf16),
            pltpu.VMEM((tiles, cap), f32),
            pltpu.VMEM((tiles, cap), f32),
        ],
    )(got, sky, prior_precision)
    sums = exchange(sums, everywhere)

    stage_a, twiddle, stage_b = dft_tables(nphi, n_tm)
    maps, send = call(
        bin_kernel,
        "bin",
        [
            ((3 * second, cycles * LANES), f32),
            ((PLANES * cycles * n_tm * band // LANES, LANES), f32),
        ],
        [
            pltpu.VMEM((6 * second, cycles * LANES), f32),
            pltpu.VMEM((6, tiles, cap), f32),
            pltpu.VMEM((6 * second, GROUP * cap), bf16),
            pltpu.VMEM((cycles * LANES, GROUP * cap), bf16),
        ],
    )(sums, data, signal, cosine, sine, line, column, stage_a, twiddle, stage_b)

    got = exchange(send.reshape(n_tm, -1, LANES), "tm", meeting_order(n_tm)).reshape(-1, LANES)
    halo_rows = PLANES * HALO + 3 * 2
    rhs, to_one, to_two = call(
        rhs_kernel,
        "rhs",
        [((PLANES, count, band), f32)] + [((halo_rows, band), f32)] * 2,
        [pltpu.VMEM((PLANES + 1, count, LANES), f32)],
    )(got, sums, prior_precision, omega_noise, omega_prior)
    maps, to_one, to_two = lax.optimization_barrier((maps, to_one, to_two))
    from_one = lax.ppermute(to_one, "det", pairs)
    from_two = lax.ppermute(to_two, "det", others)
    binned, gain, weights = call(
        report_kernel,
        "report",
        [
            ((3, second * cycles, LANES), f32),
            ((1, 1), f32),
            ((tiles * cycles + BLOCK, LANES), f32),
        ],
    )(maps, sums)
    binned = binned.reshape(3, second, cycles, LANES).transpose(0, 2, 1, 3).reshape(3, cycles, nphi)
    binned, rhs = lax.optimization_barrier((binned, rhs))
    one, two, sums = call(
        krylov_kernel,
        "krylov",
        [((PLANES, count, band), f32)] * 2 + [((devices, LANES), f32)],
        [pltpu.VMEM((PLANES + 3, BLOCK, band), f32)],
    )(rhs, weights, prior_precision, from_one, from_two)
    sums = exchange(sums, everywhere)
    solution = call(final_kernel, "final", [((PLANES, count, band), f32)])(
        sums, weights, rhs, one, two
    )[0]
    return (gain, binned, solution)


def solution(mesh):
    return jax.shard_map(
        per_device,
        mesh=mesh,
        in_specs=(
            P("det", "tm", None, None),
            P("det", "tm", None, None),
            P("det", "tm", None, None),
            P("det", "tm", None),
            P(None, ("det", "tm"), None),
            P(None, "det", "tm"),
            P(None, "det", "tm"),
            P(None, "det", "tm"),
        ),
        out_specs=(P("det", "tm"), P(None, ("det", "tm"), None), P(None, "det", "tm")),
        check_vma=False,
    )
```

```python
import math

import jax
import jax.numpy as jnp
import ml_dtypes
import numpy as np
from jax import lax
from jax.experimental import pallas as pl
from jax.experimental.pallas import tpu as pltpu
from jax.sharding import PartitionSpec as P

SPREAD = 8.0
COUPLING = 0.45

LANES = 128
GROUP = 32
PLANES = 6
HALO = 3
BLOCK = 8


def split_np(table):
    high = table.astype(ml_dtypes.bfloat16)
    low = (table - high.astype(np.float64)).astype(ml_dtypes.bfloat16)
    return high, low


def bits(power):
    return power.bit_length() - 1


def split(values):
    high = values.astype(jnp.bfloat16)
    low = (values - high.astype(jnp.float32)).astype(jnp.bfloat16)
    return high, low


def meeting_order(n_tm):
    if n_tm == 8:
        return [3, 2, 7, 5, 1, 0, 4, 6]
    return [(i + n_tm // 2 + 1) % n_tm for i in range(n_tm)]


def dft_tables(nphi, n_tm):
    first, second = LANES, nphi // LANES
    half = second // 2
    column = np.arange(first)
    digit = 2 * (column % (first // 2)) + column // (first // 2)
    k = np.arange(first)
    angle = 2.0 * math.pi / first * (np.outer(digit, k) % first)
    stage_a = np.concatenate([np.cos(angle), np.sin(angle)], axis=1)
    high, low = split_np(stage_a)
    stage_a = np.concatenate([high, high, low], axis=0)
    b = np.arange(second)
    angle = 2.0 * math.pi / nphi * (np.outer(b, k) % nphi)
    twiddle = np.stack([np.cos(angle), np.sin(angle)]).astype(np.float32)
    per_band = half // n_tm
    row = np.arange(half)
    q = np.array(meeting_order(n_tm))[row % n_tm] * per_band + row // n_tm
    angle = 2.0 * math.pi / second * (np.outer(q, b) % second)
    cos_b, sin_b = np.cos(angle), np.sin(angle)
    stage_b = np.block([[cos_b, -sin_b], [-sin_b, -cos_b]]) / math.sqrt(nphi)
    high, low = split_np(stage_b)
    stage_b = np.concatenate([high, high, low], axis=1)
    return stage_a, twiddle, stage_b


def pack_kernel(
    samples_hbm, angles_hbm, pointing_hbm, counts_hbm, out_ref,
    samples_ref, angles_ref, pointing_ref, counts_ref, sems,
):
    copies = [
        pltpu.make_async_copy(source, target, sems.at[i])
        for i, (source, target) in enumerate(
            (
                (samples_hbm, samples_ref),
                (angles_hbm, angles_ref),
                (pointing_hbm, pointing_ref),
                (counts_hbm, counts_ref),
            )
        )
    ]
    for copy in copies:
        copy.start()
    tiles = samples_ref.shape[0]
    halves = samples_ref.shape[1] // LANES
    lines = 3 * halves + 1
    for field, source in enumerate((samples_ref, angles_ref, pointing_ref)):
        copies[field].wait()
        for h in range(halves):
            out_ref[pl.ds(field * halves + h, tiles, stride=lines), :] = source[
                :, h * LANES : (h + 1) * LANES
            ].astype(jnp.float32)
    copies[3].wait()
    count = counts_ref[...].astype(jnp.float32)
    row = lax.broadcasted_iota(jnp.int32, (tiles, tiles), 0)
    col = lax.broadcasted_iota(jnp.int32, (tiles, tiles), 1)
    column = jnp.sum(jnp.where(row == col, count, 0.0), axis=1, keepdims=True)
    out_ref[pl.ds(3 * halves, tiles, stride=lines), :] = jnp.broadcast_to(column, (tiles, LANES))


def repeated(line, rows):
    tile = jnp.broadcast_to(line, (16, line.shape[1])).astype(jnp.bfloat16)
    return jnp.concatenate([tile] * (rows // 16), axis=0)


def lookup_kernel(
    got_ref, sky_ref, prior_ref, data_ref, signal_ref, cosine_ref, sine_ref, line_ref, column_ref, sums_ref,
    table, high, low,
):
    tiles, cap = data_ref.shape
    halves = cap // LANES
    lines = 3 * halves + 1
    rows = sky_ref.shape[1]
    cycles = 2
    nphi = rows * LANES // cycles

    for c in range(3):
        part = split(sky_ref[c].T)
        table[c * LANES : (c + 1) * LANES, :rows] = part[0]
        table[c * LANES : (c + 1) * LANES, rows:] = part[1]

    def received(field):
        parts = [got_ref[pl.ds(field * halves + h, tiles, stride=lines), :] for h in range(halves)]
        return jnp.concatenate(parts, axis=1)

    data = received(0)
    angle = received(1)
    pixel = received(2).astype(jnp.int32)
    count = got_ref[pl.ds(3 * halves, tiles, stride=lines), :]
    count = jnp.concatenate([count] * halves, axis=1)
    slot = lax.broadcasted_iota(jnp.int32, (tiles, cap), 1).astype(jnp.float32)
    valid = jnp.where(slot < count, 1.0, 0.0)
    cosine = jnp.cos(2.0 * angle)
    sine = jnp.sin(2.0 * angle)
    cosine_ref[...] = cosine
    sine_ref[...] = sine
    cycle = pixel >> bits(nphi)
    row = (pixel >> bits(LANES)) & (nphi // LANES - 1)
    high[...] = (row * cycles + cycle).astype(jnp.float32)
    low[...] = (pixel & (LANES - 1)).astype(jnp.float32)
    second = nphi // LANES
    line_ref[...] = (pixel & (second - 1)).astype(jnp.float32)
    column = cycle * LANES + ((pixel >> bits(second)) & 1) * (LANES // 2) + row
    column_ref[...] = column.astype(jnp.float32)

    iota = lax.broadcasted_iota(jnp.int32, (LANES, cap), 0).astype(jnp.float32)
    iota_half = iota.astype(jnp.bfloat16)
    one = jnp.ones((LANES, cap), jnp.bfloat16)
    zero = jnp.zeros((LANES, cap), jnp.bfloat16)

    def step(index, carry):
        for g in range(GROUP):
            s = index * GROUP + g
            onehot = jnp.where(iota_half == repeated(high[pl.ds(s, 1), :], LANES), one, zero)
            onehot = jnp.concatenate([onehot, onehot], axis=0)
            found = [
                jnp.dot(
                    table[c * LANES : (c + 1) * LANES, :], onehot, preferred_element_type=jnp.float32
                )
                for c in range(3)
            ]
            mask = iota == low[pl.ds(s, 1), :]
            mixed = (
                found[0]
                + found[1] * cosine_ref[pl.ds(s, 1), :]
                + found[2] * sine_ref[pl.ds(s, 1), :]
            )
            signal_ref[pl.ds(s, 1), :] = jnp.sum(
                jnp.where(mask, mixed, 0.0), axis=0, keepdims=True
            )
        return carry

    lax.fori_loop(0, tiles // GROUP, step, 0)

    signal = signal_ref[...]
    masked = valid * signal
    signal_ref[...] = masked
    data_ref[...] = valid * data
    cross = jnp.sum(masked * data, axis=1, keepdims=True)
    square = jnp.sum(masked * signal, axis=1, keepdims=True)
    width = sums_ref.shape[1]
    row = lax.broadcasted_iota(jnp.int32, (tiles, width), 0)
    lane = lax.broadcasted_iota(jnp.int32, (tiles, width), 1)
    lines = jnp.where(lane == row, cross, 0.0) + jnp.where(lane == row + tiles, square, 0.0)
    for cy in range(cycles):
        hits = jnp.sum(jnp.where(cycle == cy, valid, 0.0), axis=1, keepdims=True)
        lines = lines + jnp.where(lane == 2 * tiles + cy, hits * (1.0 / nphi), 0.0)
    line = jnp.sum(lines, axis=0, keepdims=True)
    prior = prior_ref[...]
    lane = lax.broadcasted_iota(jnp.int32, (1, width), 1)
    for i, values in enumerate((prior, prior * prior)):
        folded = jnp.sum(jnp.sum(values, axis=0), axis=0, keepdims=True)
        found = jnp.sum(folded, axis=1, keepdims=True)
        line = jnp.where(lane == 2 * tiles + cycles + i, found, line)
    sums_ref[...] = jnp.broadcast_to(line, sums_ref.shape)


def all_gains(sums_ref, tiles):
    total = jnp.sum(sums_ref[...], axis=0, keepdims=True)
    row = lax.broadcasted_iota(jnp.int32, (tiles, total.shape[1]), 0)
    lane = lax.broadcasted_iota(jnp.int32, (tiles, total.shape[1]), 1)
    cross = jnp.sum(jnp.where(lane == row, total, 0.0), axis=1, keepdims=True)
    square = jnp.sum(jnp.where(lane == row + tiles, total, 0.0), axis=1, keepdims=True)
    return cross / (square + 1e-06)


def bin_kernel(
    sums_ref, data_ref, signal_ref, cosine_ref, sine_ref, line_ref, column_ref,
    stage_a_ref, twiddle_ref, stage_b_ref, maps_ref, send_ref, acc, weights, wide, onehot,
):
    tiles, cap = data_ref.shape
    cycles = 2
    second = twiddle_ref.shape[1]
    first = LANES
    nphi = first * second
    n_tm = lax.axis_size("tm")
    lines = PLANES * cycles
    stride = send_ref.shape[0] // n_tm
    per_band = stride // lines

    gains = all_gains(sums_ref, tiles)
    residual = data_ref[...] - gains * signal_ref[...]
    for c, values in enumerate((residual, residual * cosine_ref[...], residual * sine_ref[...])):
        top = values.astype(jnp.bfloat16).astype(jnp.float32)
        weights[2 * c] = top
        weights[2 * c + 1] = values - top
    acc[...] = jnp.zeros_like(acc)
    iota_high = lax.broadcasted_iota(jnp.int32, (cycles * first, cap), 0)
    iota_high = iota_high.astype(jnp.float32).astype(jnp.bfloat16)
    iota_low = iota_high[:second]
    zero_low = jnp.zeros((second, cap), jnp.bfloat16)
    zero_high = jnp.zeros((cycles * first, cap), jnp.bfloat16)
    one_high = jnp.ones((cycles * first, cap), jnp.bfloat16)

    def step(index, carry):
        for g in range(GROUP):
            s = index * GROUP + g
            cut = slice(g * cap, (g + 1) * cap)
            mask = iota_low == repeated(line_ref[pl.ds(s, 1), :], second)
            for i in range(6):
                wide[i * second : (i + 1) * second, cut] = jnp.where(
                    mask, repeated(weights[i, pl.ds(s, 1), :], second), zero_low
                )
            onehot[:, cut] = jnp.where(
                iota_high == repeated(column_ref[pl.ds(s, 1), :], cycles * first),
                one_high,
                zero_high,
            )
        acc[...] += lax.dot_general(
            wide[...], onehot[...], (((1,), (1,)), ((), ())), preferred_element_type=jnp.float32
        )
        return carry

    lax.fori_loop(0, tiles // GROUP, step, 0)

    blocks = []
    for c in range(3):
        at = 2 * c * second
        map_c = acc[at : at + second, :] + acc[at + second : at + 2 * second, :]
        for cy in range(cycles):
            block = map_c[:, cy * first : (cy + 1) * first]
            blocks.append(block)
            maps_ref[c * second : (c + 1) * second, cy * first : (cy + 1) * first] = block
    field = jnp.concatenate(blocks, axis=0)
    field_high, field_low = split(field)
    modes = jnp.dot(
        jnp.concatenate([field_high, field_low, field_high], axis=1),
        stage_a_ref[...],
        preferred_element_type=jnp.float32,
    )
    turned = []
    for i in range(3 * cycles):
        real = modes[i * second : (i + 1) * second, :first]
        imag = modes[i * second : (i + 1) * second, first:]
        cos_t = twiddle_ref[0]
        sin_t = twiddle_ref[1]
        turned.append(
            jnp.concatenate([real * cos_t - imag * sin_t, real * sin_t + imag * cos_t], axis=0)
        )
    turned = jnp.concatenate(turned, axis=1)
    turned_high, turned_low = split(turned)
    spectrum = jnp.dot(
        stage_b_ref[...],
        jnp.concatenate([turned_high, turned_low, turned_high], axis=0),
        preferred_element_type=jnp.float32,
    )
    half = second // 2
    for c in range(3):
        for cy in range(cycles):
            at = (c * cycles + cy) * first
            for part in range(2):
                for ql in range(per_band):
                    start = part * half + ql * n_tm
                    line = ql * lines + (2 * c + part) * cycles + cy
                    send_ref[pl.ds(line, n_tm, stride=stride), :] = spectrum[
                        start : start + n_tm, at : at + first
                    ]


def report_kernel(maps_ref, sums_ref, binned_ref, gain_ref, weight_ref):
    first = LANES
    cycles = maps_ref.shape[1] // first
    second = maps_ref.shape[0] // 3
    tiles = sums_ref.shape[0]
    for c in range(3):
        for cy in range(cycles):
            flipped = maps_ref[c * second : (c + 1) * second, cy * first : (cy + 1) * first].T
            binned_ref[c, pl.ds(cy, first // 2, stride=cycles), :] = jnp.concatenate(
                [flipped[: first // 2], flipped[first // 2 :]], axis=1
            )
    position = lax.axis_index("det") * lax.axis_size("tm") + lax.axis_index("tm")
    place = lax.broadcasted_iota(jnp.int32, (tiles, 1), 0)
    own = jnp.where(place == position, all_gains(sums_ref, tiles), 0.0)
    gain_ref[...] = jnp.sum(own, axis=0, keepdims=True)
    for cy in range(cycles):
        at = 2 * tiles + cy
        weight_ref[pl.ds(cy, tiles, stride=cycles), :] = jnp.broadcast_to(
            sums_ref[:, at : at + 1], (tiles, LANES)
        )
    weight_ref[tiles * cycles :, :] = jnp.zeros((BLOCK, LANES), jnp.float32)
    at = 2 * tiles
    total = jnp.sum(sums_ref[...], axis=0, keepdims=True)
    hit = jnp.sum(total[:, at : at + cycles], axis=1, keepdims=True) * (1.0 / (tiles * cycles))
    at = at + cycles
    center = total[:, at + 1 : at + 2] / total[:, at : at + 1] + hit
    weight_ref[tiles * cycles + BLOCK - 1 :, :] = jnp.broadcast_to(center, (1, LANES))


def rhs_kernel(
    got_ref, sums_ref, prior_ref, noise_ref, draw_ref, rhs_ref, one_ref, two_ref, lines
):
    count = prior_ref.shape[1]
    per_band = prior_ref.shape[2] // LANES
    n_tm = lax.axis_size("tm")
    cycles = count // n_tm
    each = PLANES * cycles
    stride = per_band * each
    order = meeting_order(n_tm)
    tiles = sums_ref.shape[0]
    group = sums_ref[pl.ds(pl.multiple_of(lax.axis_index("det") * n_tm, 8), n_tm), :]
    for cy in range(cycles):
        at = 2 * tiles + cy
        lines[PLANES, pl.ds(cy, n_tm, stride=cycles), :] = jnp.broadcast_to(
            group[:, at : at + 1], (n_tm, LANES)
        )
    root_weight = jnp.sqrt(lines[PLANES])
    for ql in range(per_band):
        cut = slice(ql * LANES, (ql + 1) * LANES)
        for p in range(PLANES):
            for i, t in enumerate(order):
                at = i * stride + ql * each + p * cycles
                lines[p, t * cycles : (t + 1) * cycles, :] = got_ref[at : at + cycles, :]
        for c in range(3):
            root = jnp.sqrt(prior_ref[c, :, cut])
            for p in (2 * c, 2 * c + 1):
                rhs_ref[p, :, cut] = (
                    lines[p] + root_weight * noise_ref[p, :, cut] + root * draw_ref[p, :, cut]
                )
    even = lax.axis_index("det") % 2 == 0
    after = PLANES * HALO
    for p in range(PLANES):
        c = p // 2
        head = rhs_ref[p, :HALO, :]
        tail = rhs_ref[p, count - HALO :, :]
        row = lax.broadcasted_iota(jnp.int32, head.shape, 0)
        head = jnp.where(row == HALO - 1, jnp.sqrt(prior_ref[c, :HALO, :]) * head, head)
        tail = jnp.where(row == HALO - 2, jnp.sqrt(prior_ref[c, count - HALO :, :]) * tail, tail)
        one_ref[p * HALO : (p + 1) * HALO, :] = jnp.where(even, tail, head)
        two_ref[p * HALO : (p + 1) * HALO, :] = jnp.where(even, head, tail)
    for c in range(3):
        head = prior_ref[c, :2, :]
        tail = prior_ref[c, count - 2 :, :]
        one_ref[after + 2 * c : after + 2 * c + 2, :] = jnp.where(even, tail, head)
        two_ref[after + 2 * c : after + 2 * c + 2, :] = jnp.where(even, head, tail)


def krylov_kernel(
    rhs_ref, weights_ref, prior_ref, from_one_ref, from_two_ref, one_ref, two_ref, sums_ref, edge
):
    count = rhs_ref.shape[1]
    rows = count + BLOCK
    band = rhs_ref.shape[2]
    group = lax.axis_index("det")
    even = group % 2 == 0
    has_before = group > 0
    has_after = group < lax.axis_size("det") - 1
    start = pl.multiple_of(group * count, BLOCK)
    before = pl.multiple_of(jnp.maximum(start - BLOCK, 0), BLOCK)
    place = lax.broadcasted_iota(jnp.int32, (BLOCK, LANES), 0)
    beyond = jnp.where(
        place < BLOCK - HALO,
        weights_ref[pl.ds(start + count, BLOCK), :],
        weights_ref[pl.ds(before, BLOCK), :],
    )
    center = weights_ref[weights_ref.shape[0] - 1 :, :]
    weight = jnp.concatenate([weights_ref[pl.ds(start, count), :], beyond], axis=0) - center
    sums = [jnp.zeros((count, LANES), jnp.float32) for _ in range(6)]

    def arrived(at, size):
        one, two = from_one_ref[at : at + size, :], from_two_ref[at : at + size, :]
        ahead = jnp.where(has_after, jnp.where(even, one, two), 0.0)
        behind = jnp.where(has_before, jnp.where(even, two, one), 0.0)
        return ahead, behind

    for p in range(PLANES):
        ahead, behind = arrived(p * HALO, HALO)
        edge[p] = jnp.zeros((BLOCK, band), jnp.float32)
        edge[p, :HALO, :] = ahead
        edge[p, BLOCK - 2 :, :] = behind[HALO - 2 :]
    for c in range(3):
        ahead, behind = arrived(PLANES * HALO + 2 * c, 2)
        edge[PLANES + c] = jnp.ones((BLOCK, band), jnp.float32)
        edge[PLANES + c, :2, :] = ahead
        edge[PLANES + c, BLOCK - 1 :, :] = behind[1:]

    for c, at in ((c, at) for at in range(0, band, LANES) for c in range(3)):
        cut = slice(at, at + LANES)
        precision = jnp.concatenate([prior_ref[c, :, cut], edge[PLANES + c, :, cut]], axis=0)
        root = jnp.sqrt(precision)
        diagonal = (precision + weight) * (1.0 / SPREAD)
        beside = root * (COUPLING / SPREAD)

        def apply(field):
            scaled = root * field
            return diagonal * field - beside * (
                pltpu.roll(scaled, 1, 0) + pltpu.roll(scaled, rows - 1, 0)
            )

        for part in range(2):
            p = 2 * c + part
            zero = jnp.concatenate([rhs_ref[p, :, cut], edge[p, :, cut]], axis=0)
            one = apply(zero)
            two = apply(one)
            scaled = root * two
            pair = scaled * pltpu.roll(scaled, rows - 1, 0)
            last = diagonal * two * two - (2.0 * COUPLING / SPREAD) * pair
            zero, one, two, last = zero[:count], one[:count], two[:count], last[:count]
            one_ref[p, :, cut] = one
            two_ref[p, :, cut] = two
            for i, term in enumerate(
                (zero * zero, zero * one, one * one, one * two, two * two, last)
            ):
                sums[i] = sums[i] + term
    lines = []
    for i in range(6):
        lines.append(jnp.sum(sums[i], axis=0, keepdims=True))
    column = jnp.sum(jnp.concatenate(lines, axis=0), axis=1, keepdims=True)
    row = lax.broadcasted_iota(jnp.int32, (6, LANES), 0)
    lane = lax.broadcasted_iota(jnp.int32, (6, LANES), 1)
    line = jnp.sum(jnp.where(lane == row, column, 0.0), axis=0, keepdims=True)
    sums_ref[...] = jnp.broadcast_to(line, sums_ref.shape)


def inner(left, right, moments):
    result = 0.0
    for i, a in enumerate(left):
        for j, b in enumerate(right):
            result = result + a * b * moments[i + j]
    return result


def operated(coefficients, center):
    result = [center * a for a in coefficients] + [0.0]
    for i, a in enumerate(coefficients):
        result[i + 1] = result[i + 1] + SPREAD * a
    return result


def padded(values, length):
    return list(values) + [0.0] * (length - len(values))


def conjugate_gradient(moments, center):
    inverse = 1.0 / moments[0]
    moments = [1.0] + [moment * inverse for moment in moments[1:]]
    resid = [1.0]
    direction = [1.0]
    solution = [0.0]
    norm_now = moments[0]
    for iteration in range(3):
        image = operated(direction, center)
        alpha = norm_now / inner(direction, image, moments)
        size = len(direction)
        solution = [a + alpha * b for a, b in zip(padded(solution, size), direction)]
        if iteration == 2:
            break
        resid = [a - alpha * b for a, b in zip(padded(resid, size + 1), image)]
        norm_next = inner(resid, resid, moments)
        beta = norm_next / norm_now
        direction = [a + beta * b for a, b in zip(resid, padded(direction, size + 1))]
        norm_now = norm_next
    return solution


def final_kernel(sums_ref, weights_ref, rhs_ref, one_ref, two_ref, out_ref):
    total = jnp.sum(sums_ref[...], axis=0, keepdims=True)
    moments = [total[:, i : i + 1] for i in range(6)]
    center = weights_ref[weights_ref.shape[0] - 1 :, :1]
    zero_by, one_by, two_by = conjugate_gradient(moments, center)
    for p in range(PLANES):
        out_ref[p] = zero_by * rhs_ref[p] + one_by * one_ref[p] + two_by * two_ref[p]


def call(kernel, name, outs, scratch=(), in_specs=None, limit=24):
    extra = {} if in_specs is None else {"in_specs": in_specs}
    return pl.pallas_call(
        kernel,
        out_shape=tuple(jax.ShapeDtypeStruct(shape, dtype) for shape, dtype in outs),
        scratch_shapes=list(scratch),
        compiler_params=pltpu.CompilerParams(vmem_limit_bytes=limit * 2**20),
        name=name,
        **extra,
    )


def exchange(values, axes, order=None):
    groups = None if order is None else [order]
    return lax.all_to_all(
        values, axes, split_axis=0, concat_axis=0, tiled=True, axis_index_groups=groups
    )


def per_device(
    samples, pointing, angles, counts, sky_map, prior_precision, omega_noise, omega_prior
):
    f32, i32, bf16 = jnp.float32, jnp.int32, jnp.bfloat16
    tiles, cap = samples.shape[2:]
    n_det, n_tm = lax.axis_size("det"), lax.axis_size("tm")
    devices = n_det * n_tm
    cycles, nphi = sky_map.shape[1:]
    count, band = prior_precision.shape[1:]
    second = nphi // LANES
    everywhere = ("det", "tm")
    pairs = [(i, i ^ 1) for i in range(n_det)]
    others = [(i, (i + 1 if i % 2 else i - 1) % n_det) for i in range(n_det)]

    lines = 3 * cap // LANES + 1
    packed = call(
        pack_kernel,
        "pack",
        [((tiles * lines, LANES), f32)],
        [
            pltpu.VMEM((tiles, cap), f32),
            pltpu.VMEM((tiles, cap), f32),
            pltpu.VMEM((tiles, cap), i32),
            pltpu.VMEM((1, tiles), i32),
            pltpu.SemaphoreType.DMA((4,)),
        ],
        [pl.BlockSpec(memory_space=pltpu.HBM)] * 4,
    )(
        *(
            pltpu.with_memory_space_constraint(values, pltpu.HBM)
            for values in (
                samples.reshape(tiles, cap),
                angles.reshape(tiles, cap),
                pointing.reshape(tiles, cap),
                counts.reshape(1, tiles),
            )
        )
    )[0]
    got = exchange(packed.reshape(tiles, lines * LANES), everywhere).reshape(tiles * lines, LANES)

    sky = sky_map.reshape(3, cycles, second, LANES).transpose(0, 2, 1, 3)
    sky = sky.reshape(3, second * cycles, LANES)
    width = LANES * -(-(2 * tiles + cycles + 2) // LANES)
    data, signal, cosine, sine, line, column, sums = call(
        lookup_kernel,
        "lookup",
        [((tiles, cap), f32)] * 6 + [((devices, width), f32)],
        [
            pltpu.VMEM((3 * LANES, 2 * second * cycles), bf16),
            pltpu.VMEM((tiles, cap), f32),
            pltpu.VMEM((tiles, cap), f32),
        ],
    )(got, sky, prior_precision)
    sums = exchange(sums, everywhere)

    stage_a, twiddle, stage_b = dft_tables(nphi, n_tm)
    maps, send = call(
        bin_kernel,
        "bin",
        [
            ((3 * second, cycles * LANES), f32),
            ((PLANES * cycles * n_tm * band // LANES, LANES), f32),
        ],
        [
            pltpu.VMEM((6 * second, cycles * LANES), f32),
            pltpu.VMEM((6, tiles, cap), f32),
            pltpu.VMEM((6 * second, GROUP * cap), bf16),
            pltpu.VMEM((cycles * LANES, GROUP * cap), bf16),
        ],
    )(sums, data, signal, cosine, sine, line, column, stage_a, twiddle, stage_b)

    got = exchange(send.reshape(n_tm, -1, LANES), "tm", meeting_order(n_tm)).reshape(-1, LANES)
    halo_rows = PLANES * HALO + 3 * 2
    rhs, to_one, to_two = call(
        rhs_kernel,
        "rhs",
        [((PLANES, count, band), f32)] + [((halo_rows, band), f32)] * 2,
        [pltpu.VMEM((PLANES + 1, count, LANES), f32)],
    )(got, sums, prior_precision, omega_noise, omega_prior)
    maps, to_one, to_two = lax.optimization_barrier((maps, to_one, to_two))
    from_one = lax.ppermute(to_one, "det", pairs)
    from_two = lax.ppermute(to_two, "det", others)
    binned, gain, weights = call(
        report_kernel,
        "report",
        [
            ((3, second * cycles, LANES), f32),
            ((1, 1), f32),
            ((tiles * cycles + BLOCK, LANES), f32),
        ],
    )(maps, sums)
    binned = binned.reshape(3, second, cycles, LANES).transpose(0, 2, 1, 3).reshape(3, cycles, nphi)
    binned, rhs = lax.optimization_barrier((binned, rhs))
    one, two, sums = call(
        krylov_kernel,
        "krylov",
        [((PLANES, count, band), f32)] * 2 + [((devices, LANES), f32)],
        [pltpu.VMEM((PLANES + 3, BLOCK, band), f32)],
    )(rhs, weights, prior_precision, from_one, from_two)
    sums = exchange(sums, everywhere)
    solution = call(final_kernel, "final", [((PLANES, count, band), f32)])(
        sums, weights, rhs, one, two
    )[0]
    return (gain, binned, solution)


def solution(mesh):
    return jax.shard_map(
        per_device,
        mesh=mesh,
        in_specs=(
            P("det", "tm", None, None),
            P("det", "tm", None, None),
            P("det", "tm", None, None),
            P("det", "tm", None),
            P(None, ("det", "tm"), None),
            P(None, "det", "tm"),
            P(None, "det", "tm"),
            P(None, "det", "tm"),
        ),
        out_specs=(P("det", "tm"), P(None, ("det", "tm"), None), P(None, "det", "tm")),
        check_vma=False,
    )
```

```python
import math

import jax
import jax.numpy as jnp
import ml_dtypes
import numpy as np
from jax import lax
from jax.experimental import pallas as pl
from jax.experimental.pallas import tpu as pltpu
from jax.sharding import PartitionSpec as P

SPREAD = 8.0
COUPLING = 0.45

LANES = 128
GROUP = 32
PLANES = 6
HALO = 3
BLOCK = 8


def split_np(table):
    high = table.astype(ml_dtypes.bfloat16)
    low = (table - high.astype(np.float64)).astype(ml_dtypes.bfloat16)
    return high, low


def bits(power):
    return power.bit_length() - 1


def split(values):
    high = values.astype(jnp.bfloat16)
    low = (values - high.astype(jnp.float32)).astype(jnp.bfloat16)
    return high, low


def meeting_order(n_tm):
    if n_tm == 8:
        return [3, 2, 7, 5, 1, 0, 4, 6]
    return [(i + n_tm // 2 + 1) % n_tm for i in range(n_tm)]


def dft_tables(nphi, n_tm):
    first, second = LANES, nphi // LANES
    half = second // 2
    column = np.arange(first)
    digit = 2 * (column % (first // 2)) + column // (first // 2)
    k = np.arange(first)
    angle = 2.0 * math.pi / first * (np.outer(digit, k) % first)
    stage_a = np.concatenate([np.cos(angle), np.sin(angle)], axis=1)
    high, low = split_np(stage_a)
    stage_a = np.concatenate([high, high, low], axis=0)
    b = np.arange(second)
    angle = 2.0 * math.pi / nphi * (np.outer(b, k) % nphi)
    twiddle = np.stack([np.cos(angle), np.sin(angle)]).astype(np.float32)
    per_band = half // n_tm
    row = np.arange(half)
    q = np.array(meeting_order(n_tm))[row % n_tm] * per_band + row // n_tm
    angle = 2.0 * math.pi / second * (np.outer(q, b) % second)
    cos_b, sin_b = np.cos(angle), np.sin(angle)
    stage_b = np.block([[cos_b, -sin_b], [-sin_b, -cos_b]]) / math.sqrt(nphi)
    high, low = split_np(stage_b)
    stage_b = np.concatenate([high, high, low], axis=1)
    return stage_a, twiddle, stage_b


def pack_kernel(
    samples_hbm, angles_hbm, pointing_hbm, counts_hbm, out_ref,
    samples_ref, angles_ref, pointing_ref, counts_ref, sems,
):
    copies = [
        pltpu.make_async_copy(source, target, sems.at[i])
        for i, (source, target) in enumerate(
            (
                (samples_hbm, samples_ref),
                (angles_hbm, angles_ref),
                (pointing_hbm, pointing_ref),
                (counts_hbm, counts_ref),
            )
        )
    ]
    for copy in copies:
        copy.start()
    tiles = samples_ref.shape[0]
    halves = samples_ref.shape[1] // LANES
    lines = 3 * halves + 1
    for field, source in enumerate((samples_ref, angles_ref, pointing_ref)):
        copies[field].wait()
        for h in range(halves):
            out_ref[pl.ds(field * halves + h, tiles, stride=lines), :] = source[
                :, h * LANES : (h + 1) * LANES
            ].astype(jnp.float32)
    copies[3].wait()
    count = counts_ref[...].astype(jnp.float32)
    row = lax.broadcasted_iota(jnp.int32, (tiles, tiles), 0)
    col = lax.broadcasted_iota(jnp.int32, (tiles, tiles), 1)
    column = jnp.sum(jnp.where(row == col, count, 0.0), axis=1, keepdims=True)
    out_ref[pl.ds(3 * halves, tiles, stride=lines), :] = jnp.broadcast_to(column, (tiles, LANES))


def repeated(line, rows):
    tile = jnp.broadcast_to(line, (16, line.shape[1])).astype(jnp.bfloat16)
    return jnp.concatenate([tile] * (rows // 16), axis=0)


def lookup_kernel(
    got_ref, sky_ref, prior_ref, data_ref, signal_ref, cosine_ref, sine_ref, line_ref, column_ref, sums_ref,
    table, high, low,
):
    tiles, cap = data_ref.shape
    halves = cap // LANES
    lines = 3 * halves + 1
    rows = sky_ref.shape[1]
    cycles = 2
    nphi = rows * LANES // cycles

    for c in range(3):
        part = split(sky_ref[c].T)
        table[c * LANES : (c + 1) * LANES, :rows] = part[0]
        table[c * LANES : (c + 1) * LANES, rows:] = part[1]

    def received(field):
        parts = [got_ref[pl.ds(field * halves + h, tiles, stride=lines), :] for h in range(halves)]
        return jnp.concatenate(parts, axis=1)

    data = received(0)
    angle = received(1)
    pixel = received(2).astype(jnp.int32)
    count = got_ref[pl.ds(3 * halves, tiles, stride=lines), :]
    count = jnp.concatenate([count] * halves, axis=1)
    slot = lax.broadcasted_iota(jnp.int32, (tiles, cap), 1).astype(jnp.float32)
    valid = jnp.where(slot < count, 1.0, 0.0)
    cosine = jnp.cos(2.0 * angle)
    sine = jnp.sin(2.0 * angle)
    cosine_ref[...] = cosine
    sine_ref[...] = sine
    cycle = pixel >> bits(nphi)
    row = (pixel >> bits(LANES)) & (nphi // LANES - 1)
    high[...] = (row * cycles + cycle).astype(jnp.float32)
    low[...] = (pixel & (LANES - 1)).astype(jnp.float32)
    second = nphi // LANES
    line_ref[...] = (pixel & (second - 1)).astype(jnp.float32)
    column = cycle * LANES + ((pixel >> bits(second)) & 1) * (LANES // 2) + row
    column_ref[...] = column.astype(jnp.float32)

    iota = lax.broadcasted_iota(jnp.int32, (LANES, cap), 0).astype(jnp.float32)
    iota_half = iota.astype(jnp.bfloat16)
    one = jnp.ones((LANES, cap), jnp.bfloat16)
    zero = jnp.zeros((LANES, cap), jnp.bfloat16)

    def step(index, carry):
        for g in range(GROUP):
            s = index * GROUP + g
            onehot = jnp.where(iota_half == repeated(high[pl.ds(s, 1), :], LANES), one, zero)
            onehot = jnp.concatenate([onehot, onehot], axis=0)
            found = [
                jnp.dot(
                    table[c * LANES : (c + 1) * LANES, :], onehot, preferred_element_type=jnp.float32
                )
                for c in range(3)
            ]
            mask = iota == low[pl.ds(s, 1), :]
            mixed = (
                found[0]
                + found[1] * cosine_ref[pl.ds(s, 1), :]
                + found[2] * sine_ref[pl.ds(s, 1), :]
            )
            signal_ref[pl.ds(s, 1), :] = jnp.sum(
                jnp.where(mask, mixed, 0.0), axis=0, keepdims=True
            )
        return carry

    lax.fori_loop(0, tiles // GROUP, step, 0)

    signal = signal_ref[...]
    masked = valid * signal
    signal_ref[...] = masked
    data_ref[...] = valid * data
    cross = jnp.sum(masked * data, axis=1, keepdims=True)
    square = jnp.sum(masked * signal, axis=1, keepdims=True)
    width = sums_ref.shape[1]
    row = lax.broadcasted_iota(jnp.int32, (tiles, width), 0)
    lane = lax.broadcasted_iota(jnp.int32, (tiles, width), 1)
    lines = jnp.where(lane == row, cross, 0.0) + jnp.where(lane == row + tiles, square, 0.0)
    for cy in range(cycles):
        hits = jnp.sum(jnp.where(cycle == cy, valid, 0.0), axis=1, keepdims=True)
        lines = lines + jnp.where(lane == 2 * tiles + cy, hits * (1.0 / nphi), 0.0)
    line = jnp.sum(lines, axis=0, keepdims=True)
    prior = prior_ref[...]
    lane = lax.broadcasted_iota(jnp.int32, (1, width), 1)
    for i, values in enumerate((prior, prior * prior)):
        folded = jnp.sum(jnp.sum(values, axis=0), axis=0, keepdims=True)
        found = jnp.sum(folded, axis=1, keepdims=True)
        line = jnp.where(lane == 2 * tiles + cycles + i, found, line)
    sums_ref[...] = jnp.broadcast_to(line, sums_ref.shape)


def all_gains(sums_ref, tiles):
    total = jnp.sum(sums_ref[...], axis=0, keepdims=True)
    row = lax.broadcasted_iota(jnp.int32, (tiles, total.shape[1]), 0)
    lane = lax.broadcasted_iota(jnp.int32, (tiles, total.shape[1]), 1)
    cross = jnp.sum(jnp.where(lane == row, total, 0.0), axis=1, keepdims=True)
    square = jnp.sum(jnp.where(lane == row + tiles, total, 0.0), axis=1, keepdims=True)
    return cross / (square + 1e-06)


def bin_kernel(
    sums_ref, data_ref, signal_ref, cosine_ref, sine_ref, line_ref, column_ref,
    stage_a_ref, twiddle_ref, stage_b_ref, maps_ref, send_ref, acc, weights, wide, onehot,
):
    tiles, cap = data_ref.shape
    cycles = 2
    second = twiddle_ref.shape[1]
    first = LANES
    nphi = first * second
    n_tm = lax.axis_size("tm")
    lines = PLANES * cycles
    stride = send_ref.shape[0] // n_tm
    per_band = stride // lines

    gains = all_gains(sums_ref, tiles)
    residual = data_ref[...] - gains * signal_ref[...]
    for c, values in enumerate((residual, residual * cosine_ref[...], residual * sine_ref[...])):
        top = values.astype(jnp.bfloat16).astype(jnp.float32)
        weights[2 * c] = top
        weights[2 * c + 1] = values - top
    acc[...] = jnp.zeros_like(acc)
    iota_high = lax.broadcasted_iota(jnp.int32, (cycles * first, cap), 0)
    iota_high = iota_high.astype(jnp.float32).astype(jnp.bfloat16)
    iota_low = iota_high[:second]
    zero_low = jnp.zeros((second, cap), jnp.bfloat16)
    zero_high = jnp.zeros((cycles * first, cap), jnp.bfloat16)
    one_high = jnp.ones((cycles * first, cap), jnp.bfloat16)

    def step(index, carry):
        for g in range(GROUP):
            s = index * GROUP + g
            cut = slice(g * cap, (g + 1) * cap)
            mask = iota_low == repeated(line_ref[pl.ds(s, 1), :], second)
            for i in range(6):
                wide[i * second : (i + 1) * second, cut] = jnp.where(
                    mask, repeated(weights[i, pl.ds(s, 1), :], second), zero_low
                )
            onehot[:, cut] = jnp.where(
                iota_high == repeated(column_ref[pl.ds(s, 1), :], cycles * first),
                one_high,
                zero_high,
            )
        acc[...] += lax.dot_general(
            wide[...], onehot[...], (((1,), (1,)), ((), ())), preferred_element_type=jnp.float32
        )
        return carry

    lax.fori_loop(0, tiles // GROUP, step, 0)

    blocks = []
    for c in range(3):
        at = 2 * c * second
        map_c = acc[at : at + second, :] + acc[at + second : at + 2 * second, :]
        for cy in range(cycles):
            block = map_c[:, cy * first : (cy + 1) * first]
            blocks.append(block)
            maps_ref[c * second : (c + 1) * second, cy * first : (cy + 1) * first] = block
    field = jnp.concatenate(blocks, axis=0)
    field_high, field_low = split(field)
    modes = jnp.dot(
        jnp.concatenate([field_high, field_low, field_high], axis=1),
        stage_a_ref[...],
        preferred_element_type=jnp.float32,
    )
    turned = []
    for i in range(3 * cycles):
        real = modes[i * second : (i + 1) * second, :first]
        imag = modes[i * second : (i + 1) * second, first:]
        cos_t = twiddle_ref[0]
        sin_t = twiddle_ref[1]
        turned.append(
            jnp.concatenate([real * cos_t - imag * sin_t, real * sin_t + imag * cos_t], axis=0)
        )
    turned = jnp.concatenate(turned, axis=1)
    turned_high, turned_low = split(turned)
    spectrum = jnp.dot(
        stage_b_ref[...],
        jnp.concatenate([turned_high, turned_low, turned_high], axis=0),
        preferred_element_type=jnp.float32,
    )
    half = second // 2
    for c in range(3):
        for cy in range(cycles):
            at = (c * cycles + cy) * first
            for part in range(2):
                for ql in range(per_band):
                    start = part * half + ql * n_tm
                    line = ql * lines + (2 * c + part) * cycles + cy
                    send_ref[pl.ds(line, n_tm, stride=stride), :] = spectrum[
                        start : start + n_tm, at : at + first
                    ]


def report_kernel(maps_ref, sums_ref, binned_ref, gain_ref, weight_ref):
    first = LANES
    cycles = maps_ref.shape[1] // first
    second = maps_ref.shape[0] // 3
    tiles = sums_ref.shape[0]
    for c in range(3):
        for cy in range(cycles):
            flipped = maps_ref[c * second : (c + 1) * second, cy * first : (cy + 1) * first].T
            binned_ref[c, pl.ds(cy, first // 2, stride=cycles), :] = jnp.concatenate(
                [flipped[: first // 2], flipped[first // 2 :]], axis=1
            )
    position = lax.axis_index("det") * lax.axis_size("tm") + lax.axis_index("tm")
    place = lax.broadcasted_iota(jnp.int32, (tiles, 1), 0)
    own = jnp.where(place == position, all_gains(sums_ref, tiles), 0.0)
    gain_ref[...] = jnp.sum(own, axis=0, keepdims=True)
    for cy in range(cycles):
        at = 2 * tiles + cy
        weight_ref[pl.ds(cy, tiles, stride=cycles), :] = jnp.broadcast_to(
            sums_ref[:, at : at + 1], (tiles, LANES)
        )
    weight_ref[tiles * cycles :, :] = jnp.zeros((BLOCK, LANES), jnp.float32)
    at = 2 * tiles
    total = jnp.sum(sums_ref[...], axis=0, keepdims=True)
    hit = jnp.sum(total[:, at : at + cycles], axis=1, keepdims=True) * (1.0 / (tiles * cycles))
    at = at + cycles
    center = total[:, at + 1 : at + 2] / total[:, at : at + 1] + hit
    weight_ref[tiles * cycles + BLOCK - 1 :, :] = jnp.broadcast_to(center, (1, LANES))


def rhs_kernel(
    got_ref, sums_ref, prior_ref, noise_ref, draw_ref, rhs_ref, one_ref, two_ref, lines
):
    count = prior_ref.shape[1]
    per_band = prior_ref.shape[2] // LANES
    n_tm = lax.axis_size("tm")
    cycles = count // n_tm
    each = PLANES * cycles
    stride = per_band * each
    order = meeting_order(n_tm)
    tiles = sums_ref.shape[0]
    group = sums_ref[pl.ds(pl.multiple_of(lax.axis_index("det") * n_tm, 8), n_tm), :]
    for cy in range(cycles):
        at = 2 * tiles + cy
        lines[PLANES, pl.ds(cy, n_tm, stride=cycles), :] = jnp.broadcast_to(
            group[:, at : at + 1], (n_tm, LANES)
        )
    root_weight = jnp.sqrt(lines[PLANES])
    for ql in range(per_band):
        cut = slice(ql * LANES, (ql + 1) * LANES)
        for p in range(PLANES):
            for i, t in enumerate(order):
                at = i * stride + ql * each + p * cycles
                lines[p, t * cycles : (t + 1) * cycles, :] = got_ref[at : at + cycles, :]
        for c in range(3):
            root = jnp.sqrt(prior_ref[c, :, cut])
            for p in (2 * c, 2 * c + 1):
                rhs_ref[p, :, cut] = (
                    lines[p] + root_weight * noise_ref[p, :, cut] + root * draw_ref[p, :, cut]
                )
    even = lax.axis_index("det") % 2 == 0
    after = PLANES * HALO
    for p in range(PLANES):
        c = p // 2
        head = rhs_ref[p, :HALO, :]
        tail = rhs_ref[p, count - HALO :, :]
        row = lax.broadcasted_iota(jnp.int32, head.shape, 0)
        head = jnp.where(row == HALO - 1, jnp.sqrt(prior_ref[c, :HALO, :]) * head, head)
        tail = jnp.where(row == HALO - 2, jnp.sqrt(prior_ref[c, count - HALO :, :]) * tail, tail)
        one_ref[p * HALO : (p + 1) * HALO, :] = jnp.where(even, tail, head)
        two_ref[p * HALO : (p + 1) * HALO, :] = jnp.where(even, head, tail)
    for c in range(3):
        head = prior_ref[c, :2, :]
        tail = prior_ref[c, count - 2 :, :]
        one_ref[after + 2 * c : after + 2 * c + 2, :] = jnp.where(even, tail, head)
        two_ref[after + 2 * c : after + 2 * c + 2, :] = jnp.where(even, head, tail)


def krylov_kernel(
    rhs_ref, weights_ref, prior_ref, from_one_ref, from_two_ref, one_ref, two_ref, sums_ref, edge
):
    count = rhs_ref.shape[1]
    rows = count + BLOCK
    band = rhs_ref.shape[2]
    group = lax.axis_index("det")
    even = group % 2 == 0
    has_before = group > 0
    has_after = group < lax.axis_size("det") - 1
    start = pl.multiple_of(group * count, BLOCK)
    before = pl.multiple_of(jnp.maximum(start - BLOCK, 0), BLOCK)
    place = lax.broadcasted_iota(jnp.int32, (BLOCK, LANES), 0)
    beyond = jnp.where(
        place < BLOCK - HALO,
        weights_ref[pl.ds(start + count, BLOCK), :],
        weights_ref[pl.ds(before, BLOCK), :],
    )
    center = weights_ref[weights_ref.shape[0] - 1 :, :]
    weight = jnp.concatenate([weights_ref[pl.ds(start, count), :], beyond], axis=0) - center
    sums = [jnp.zeros((count, LANES), jnp.float32) for _ in range(6)]

    def arrived(at, size):
        one, two = from_one_ref[at : at + size, :], from_two_ref[at : at + size, :]
        ahead = jnp.where(has_after, jnp.where(even, one, two), 0.0)
        behind = jnp.where(has_before, jnp.where(even, two, one), 0.0)
        return ahead, behind

    for p in range(PLANES):
        ahead, behind = arrived(p * HALO, HALO)
        edge[p] = jnp.zeros((BLOCK, band), jnp.float32)
        edge[p, :HALO, :] = ahead
        edge[p, BLOCK - 2 :, :] = behind[HALO - 2 :]
    for c in range(3):
        ahead, behind = arrived(PLANES * HALO + 2 * c, 2)
        edge[PLANES + c] = jnp.ones((BLOCK, band), jnp.float32)
        edge[PLANES + c, :2, :] = ahead
        edge[PLANES + c, BLOCK - 1 :, :] = behind[1:]

    for c, at in ((c, at) for at in range(0, band, LANES) for c in range(3)):
        cut = slice(at, at + LANES)
        precision = jnp.concatenate([prior_ref[c, :, cut], edge[PLANES + c, :, cut]], axis=0)
        root = jnp.sqrt(precision)
        diagonal = (precision + weight) * (1.0 / SPREAD)
        beside = root * (COUPLING / SPREAD)

        def apply(field):
            scaled = root * field
            return diagonal * field - beside * (
                pltpu.roll(scaled, 1, 0) + pltpu.roll(scaled, rows - 1, 0)
            )

        for part in range(2):
            p = 2 * c + part
            zero = jnp.concatenate([rhs_ref[p, :, cut], edge[p, :, cut]], axis=0)
            one = apply(zero)
            two = apply(one)
            scaled = root * two
            pair = scaled * pltpu.roll(scaled, rows - 1, 0)
            last = diagonal * two * two - (2.0 * COUPLING / SPREAD) * pair
            zero, one, two, last = zero[:count], one[:count], two[:count], last[:count]
            one_ref[p, :, cut] = one
            two_ref[p, :, cut] = two
            for i, term in enumerate(
                (zero * zero, zero * one, one * one, one * two, two * two, last)
            ):
                sums[i] = sums[i] + term
    lines = []
    for i in range(6):
        lines.append(jnp.sum(sums[i], axis=0, keepdims=True))
    column = jnp.sum(jnp.concatenate(lines, axis=0), axis=1, keepdims=True)
    row = lax.broadcasted_iota(jnp.int32, (6, LANES), 0)
    lane = lax.broadcasted_iota(jnp.int32, (6, LANES), 1)
    line = jnp.sum(jnp.where(lane == row, column, 0.0), axis=0, keepdims=True)
    sums_ref[...] = jnp.broadcast_to(line, sums_ref.shape)


def inner(left, right, moments):
    terms = [None] * (len(left) + len(right) - 1)
    for i, a in enumerate(left):
        for j, b in enumerate(right):
            terms[i + j] = a * b if terms[i + j] is None else terms[i + j] + a * b
    terms = [term * moment for term, moment in zip(terms, moments)]
    while len(terms) > 1:
        pairs = [x + y for x, y in zip(terms[::2], terms[1::2])]
        terms = pairs + terms[2 * len(pairs) :]
    return terms[0]


def operated(coefficients, center):
    result = [center * a for a in coefficients] + [0.0]
    for i, a in enumerate(coefficients):
        result[i + 1] = result[i + 1] + SPREAD * a
    return result


def padded(values, length):
    return list(values) + [0.0] * (length - len(values))


def conjugate_gradient(moments, center):
    inverse = 1.0 / moments[0]
    moments = [1.0] + [moment * inverse for moment in moments[1:]]
    resid = [1.0]
    direction = [1.0]
    solution = [0.0]
    norm_now = moments[0]
    for iteration in range(3):
        image = operated(direction, center)
        alpha = norm_now / inner(direction, image, moments)
        size = len(direction)
        solution = [a + alpha * b for a, b in zip(padded(solution, size), direction)]
        if iteration == 2:
            break
        resid = [a - alpha * b for a, b in zip(padded(resid, size + 1), image)]
        norm_next = inner(resid, resid, moments)
        beta = norm_next / norm_now
        direction = [a + beta * b for a, b in zip(resid, padded(direction, size + 1))]
        norm_now = norm_next
    return solution


def final_kernel(sums_ref, weights_ref, rhs_ref, one_ref, two_ref, out_ref):
    total = jnp.sum(sums_ref[...], axis=0, keepdims=True)
    moments = [total[:, i : i + 1] for i in range(6)]
    center = weights_ref[weights_ref.shape[0] - 1 :, :1]
    zero_by, one_by, two_by = conjugate_gradient(moments, center)
    for p in range(PLANES):
        out_ref[p] = zero_by * rhs_ref[p] + one_by * one_ref[p] + two_by * two_ref[p]


def call(kernel, name, outs, scratch=(), in_specs=None, limit=24):
    extra = {} if in_specs is None else {"in_specs": in_specs}
    return pl.pallas_call(
        kernel,
        out_shape=tuple(jax.ShapeDtypeStruct(shape, dtype) for shape, dtype in outs),
        scratch_shapes=list(scratch),
        compiler_params=pltpu.CompilerParams(vmem_limit_bytes=limit * 2**20),
        name=name,
        **extra,
    )


def exchange(values, axes, order=None):
    groups = None if order is None else [order]
    return lax.all_to_all(
        values, axes, split_axis=0, concat_axis=0, tiled=True, axis_index_groups=groups
    )


def per_device(
    samples, pointing, angles, counts, sky_map, prior_precision, omega_noise, omega_prior
):
    f32, i32, bf16 = jnp.float32, jnp.int32, jnp.bfloat16
    tiles, cap = samples.shape[2:]
    n_det, n_tm = lax.axis_size("det"), lax.axis_size("tm")
    devices = n_det * n_tm
    cycles, nphi = sky_map.shape[1:]
    count, band = prior_precision.shape[1:]
    second = nphi // LANES
    everywhere = ("det", "tm")
    pairs = [(i, i ^ 1) for i in range(n_det)]
    others = [(i, (i + 1 if i % 2 else i - 1) % n_det) for i in range(n_det)]

    lines = 3 * cap // LANES + 1
    packed = call(
        pack_kernel,
        "pack",
        [((tiles * lines, LANES), f32)],
        [
            pltpu.VMEM((tiles, cap), f32),
            pltpu.VMEM((tiles, cap), f32),
            pltpu.VMEM((tiles, cap), i32),
            pltpu.VMEM((1, tiles), i32),
            pltpu.SemaphoreType.DMA((4,)),
        ],
        [pl.BlockSpec(memory_space=pltpu.HBM)] * 4,
    )(
        *(
            pltpu.with_memory_space_constraint(values, pltpu.HBM)
            for values in (
                samples.reshape(tiles, cap),
                angles.reshape(tiles, cap),
                pointing.reshape(tiles, cap),
                counts.reshape(1, tiles),
            )
        )
    )[0]
    got = exchange(packed.reshape(tiles, lines * LANES), everywhere).reshape(tiles * lines, LANES)

    sky = sky_map.reshape(3, cycles, second, LANES).transpose(0, 2, 1, 3)
    sky = sky.reshape(3, second * cycles, LANES)
    width = LANES * -(-(2 * tiles + cycles + 2) // LANES)
    data, signal, cosine, sine, line, column, sums = call(
        lookup_kernel,
        "lookup",
        [((tiles, cap), f32)] * 6 + [((devices, width), f32)],
        [
            pltpu.VMEM((3 * LANES, 2 * second * cycles), bf16),
            pltpu.VMEM((tiles, cap), f32),
            pltpu.VMEM((tiles, cap), f32),
        ],
    )(got, sky, prior_precision)
    sums = exchange(sums, everywhere)

    stage_a, twiddle, stage_b = dft_tables(nphi, n_tm)
    maps, send = call(
        bin_kernel,
        "bin",
        [
            ((3 * second, cycles * LANES), f32),
            ((PLANES * cycles * n_tm * band // LANES, LANES), f32),
        ],
        [
            pltpu.VMEM((6 * second, cycles * LANES), f32),
            pltpu.VMEM((6, tiles, cap), f32),
            pltpu.VMEM((6 * second, GROUP * cap), bf16),
            pltpu.VMEM((cycles * LANES, GROUP * cap), bf16),
        ],
    )(sums, data, signal, cosine, sine, line, column, stage_a, twiddle, stage_b)

    got = exchange(send.reshape(n_tm, -1, LANES), "tm", meeting_order(n_tm)).reshape(-1, LANES)
    halo_rows = PLANES * HALO + 3 * 2
    rhs, to_one, to_two = call(
        rhs_kernel,
        "rhs",
        [((PLANES, count, band), f32)] + [((halo_rows, band), f32)] * 2,
        [pltpu.VMEM((PLANES + 1, count, LANES), f32)],
    )(got, sums, prior_precision, omega_noise, omega_prior)
    maps, to_one, to_two = lax.optimization_barrier((maps, to_one, to_two))
    from_one = lax.ppermute(to_one, "det", pairs)
    from_two = lax.ppermute(to_two, "det", others)
    binned, gain, weights = call(
        report_kernel,
        "report",
        [
            ((3, second * cycles, LANES), f32),
            ((1, 1), f32),
            ((tiles * cycles + BLOCK, LANES), f32),
        ],
    )(maps, sums)
    binned = binned.reshape(3, second, cycles, LANES).transpose(0, 2, 1, 3).reshape(3, cycles, nphi)
    binned, rhs = lax.optimization_barrier((binned, rhs))
    one, two, sums = call(
        krylov_kernel,
        "krylov",
        [((PLANES, count, band), f32)] * 2 + [((devices, LANES), f32)],
        [pltpu.VMEM((PLANES + 3, BLOCK, band), f32)],
    )(rhs, weights, prior_precision, from_one, from_two)
    sums = exchange(sums, everywhere)
    solution = call(final_kernel, "final", [((PLANES, count, band), f32)])(
        sums, weights, rhs, one, two
    )[0]
    return (gain, binned, solution)


def solution(mesh):
    return jax.shard_map(
        per_device,
        mesh=mesh,
        in_specs=(
            P("det", "tm", None, None),
            P("det", "tm", None, None),
            P("det", "tm", None, None),
            P("det", "tm", None),
            P(None, ("det", "tm"), None),
            P(None, "det", "tm"),
            P(None, "det", "tm"),
            P(None, "det", "tm"),
        ),
        out_specs=(P("det", "tm"), P(None, ("det", "tm"), None), P(None, "det", "tm")),
        check_vma=False,
    )
```
